32 devices in a mesh: dp: 8 (over z, x), tensor: 4 (over y, core).
Axes of the slice: x: 2, y: 2, z: 4, core: 2. Of those that a mesh axis runs over, the one named last changes fastest.
Arguments:
- tokens: bfloat16 [16384, 1024], P(('dp', 'tensor')), may hold values from -6 to 6
- ln1_gain: float32 [1024], replicated, may hold values from 0.1 to 1.9
- ln1_bias: float32 [1024], replicated, may hold values from -2 to 2
- ln2_gain: float32 [1024], replicated, may hold values from 0.1 to 1.9
- ln2_bias: float32 [1024], replicated, may hold values from -2 to 2
- w_qkv: bfloat16 [3, 1024, 1024], P(None, None, 'tensor'), may hold values from -0.1875 to 0.1875
- w_out: bfloat16 [1024, 1024], P('tensor'), may hold values from -1.5 to 1.5
- w_up: bfloat16 [1024, 4096], P(None, 'tensor'), may hold values from -0.1875 to 0.1875
- w_down: bfloat16 [4096, 1024], P('tensor'), may hold values from -0.09375 to 0.09375
- feature_scale: float32 [16, 64], P('tensor'), may hold values from 0.1 to 0.5
- feature_weight: float32 [16, 64], P('tensor'), may hold values from 0.5 to 2
- lengths: int32 [8, 3], P('dp'), may hold values from 1 to 20, 32 in all within a row
- cotangent: bfloat16 [16384, 1024], P(('dp', 'tensor')), may hold values from -6 to 6
Outputs:
- mixed_out: bfloat16 [16384, 1024], P(('dp', 'tensor'))
- input_grad: bfloat16 [16384, 1024], P(('dp', 'tensor'))
- grad_ln1_gain: float32 [1024], replicated
- grad_ln1_bias: float32 [1024], replicated
- grad_ln2_gain: float32 [1024], replicated
- grad_ln2_bias: float32 [1024], replicated
- grad_qkv: float32 [3, 1024, 1024], P(None, None, 'tensor')
- grad_out: float32 [1024, 1024], P('tensor')
- grad_up: float32 [1024, 4096], P(None, 'tensor')
- grad_down: float32 [4096, 1024], P('tensor')
- grad_scale: float32 [16, 64], P('tensor')
- grad_weight: float32 [16, 64], P('tensor')
The draws below stay inside these ranges and needn't reach their ends.
Inputs may be any that keep to these rules, and one draw needn't show every extreme that they name: `lengths`: each row sums to 32, and its largest entry is exactly 20.
All inputs are finite; a program needn't handle non-finite values.
Results may differ from the reference program's by a relative error of at most 0.0035.
The reference program's roundings to bfloat16 on the way (of `mixed` and `hidden`) count: a program that leaves them out, or rounds other values in their place, can miss the bound.
Values may be sent and summed in bfloat16 or wider, within the bound.
A program may use at most 192 MiB of HBM per device.

```python
import math
import jax
import jax.numpy as jnp
import numpy as np
from jax import lax

D = 1024
HEADS = 16
HEAD_DIM = 64
ROT = 16
FF = 4096
BLOCK = 64
GROUP = 2048
TOKENS = 16384
N_DP = 8


def block_levels(key, dims, shards, low, largest):
    def one(axis_at, shards_of):
        draws = jax.random.uniform(jax.random.fold_in(jax.random.fold_in(key, 6), axis_at), (shards_of,), jnp.float32, low / len(shards), largest / len(shards))
        return jnp.repeat(jnp.exp(draws), dims[axis_at] // shards_of).reshape((-1,) + (1,) * (len(dims) - axis_at - 1))

    level = one(*shards[0])
    for cut in shards[1:]:
        level = level * one(*cut)
    return level


def split_up(amount, total, most, slope):
    loads = [(1 << 20) // math.isqrt(standing ** slope) + 1 for standing in range(2, amount + 1)]
    surplus, given = total - most - (amount - 1), [1] * (amount - 1)
    while surplus > 0:
        movable = [i for i in range(amount - 1) if given[i] < most]
        mass, left = sum([loads[i] for i in movable]), surplus
        for i in movable:
            extra = min(most - given[i], max(1, left * loads[i] // mass), surplus)
            given[i] = given[i] + extra
            surplus = surplus - extra
    return np.array([most] + given)


def ragged_sizes(own_key, number_of, total, limit, skew):
    if number_of == 2:
        one = jax.random.randint(own_key, (), max(1, total - limit), min(limit, total - 1) + 1)
        return jnp.stack([one, total - one])
    sizes = jnp.asarray(split_up(number_of, total, limit, skew), jnp.int32)
    twos = (number_of - 1) // 2
    donor, receiver = sizes[1:1 + 2 * twos:2], sizes[2:2 + 2 * twos:2]
    slack = jnp.minimum(donor - 1, limit - receiver)
    passed = jax.random.randint(jax.random.fold_in(own_key, 1), (twos,), 0, 1 << 20) % (slack + 1)
    sizes = sizes.at[1:1 + 2 * twos:2].set(donor - passed).at[2:2 + 2 * twos:2].set(receiver + passed)
    return sizes[jax.random.permutation(jax.random.fold_in(own_key, 2), number_of)]


def bell_draw(key, shape, width, limit, split=(), kind=jnp.bfloat16):
    entries = jax.random.normal(key, shape, jnp.float32) * width
    if len(split) > 0:
        entries = block_levels(key, shape, split, -0.22, 0.18) * entries
    return jnp.clip(entries, min=-limit, max=limit).astype(kind)


def setup_inputs(seed: int = 0) -> dict:
    keys = jax.random.split(jax.random.key(seed), 14)
    tokens = bell_draw(keys[0], (TOKENS, D), 1.0, 6.0, ((0, 32),))
    ln1_gain = jnp.clip(1.0 + 0.18 * jax.random.normal(keys[1], (D,), jnp.float32), 0.1, 1.9)
    ln1_bias = bell_draw(keys[2], (D,), 0.3, 2.0, (), jnp.float32)
    ln2_gain = jnp.clip(1.0 + 0.18 * jax.random.normal(keys[3], (D,), jnp.float32), 0.1, 1.9)
    ln2_bias = bell_draw(keys[4], (D,), 0.3, 2.0, (), jnp.float32)
    w_qkv = bell_draw(keys[5], (3, D, D), D ** -0.5, 0.1875, ((2, 4),))
    w_out = bell_draw(keys[6], (D, D), (D // 64) ** -0.5, 1.5, ((0, 4),))
    w_up = bell_draw(keys[7], (D, FF), D ** -0.5, 0.1875, ((1, 4),))
    w_down = bell_draw(keys[8], (FF, D), FF ** -0.5, 0.09375, ((0, 4),))
    feature_scale = jnp.clip(jnp.exp(math.log(0.5) - 1.609438 * jax.random.uniform(keys[9], (HEADS, HEAD_DIM), jnp.float32) ** block_levels(keys[9], (HEADS, HEAD_DIM), ((0, 4),), -0.2, 0.2)), 0.1, 0.5)
    feature_weight = jnp.clip(jnp.exp(math.log(2.0) - 1.3862944 * jax.random.uniform(keys[10], (HEADS, HEAD_DIM), jnp.float32) ** block_levels(keys[10], (HEADS, HEAD_DIM), ((0, 4),), -0.2, 0.2)), 0.5, 2.0)
    lengths = jax.vmap(lambda own: ragged_sizes(own, 3, GROUP // BLOCK, GROUP // BLOCK * 5 // 8, 1))(jax.random.split(keys[11], N_DP)).reshape((N_DP, 3)).astype(jnp.int32)
    cotangent = bell_draw(keys[12], (TOKENS, D), 1.0, 6.0, ((0, 32),))
    return dict(tokens=tokens, ln1_gain=ln1_gain, ln1_bias=ln1_bias, ln2_gain=ln2_gain, ln2_bias=ln2_bias, w_qkv=w_qkv, w_out=w_out, w_up=w_up, w_down=w_down, feature_scale=feature_scale, feature_weight=feature_weight, lengths=lengths, cotangent=cotangent)


@jax.custom_vjp
def low(v):
    return lax.optimization_barrier(v.astype(jnp.bfloat16)).astype(jnp.float32)

@jax.custom_vjp
def low_back(v):
    return v

def low_keep(v):
    return (low(v), None)

def low_pass(kept, grad):
    return (grad,)

def back_keep(v):
    return (v, None)

def back_low(kept, grad):
    return (low(grad),)
low.defvjp(low_keep, low_pass)
low_back.defvjp(back_keep, back_low)
HIGH = lax.Precision.HIGHEST

def dct_table(order):
    freq_rows = jnp.arange(order, dtype=jnp.float32)[:, None]
    dim_cols = jnp.arange(order, dtype=jnp.float32)[None, :]
    cosines = jnp.cos(math.pi * (dim_cols + 0.5) * freq_rows / order) * math.sqrt(2.0 / order)
    return cosines * jnp.where(freq_rows == 0, math.sqrt(0.5), 1.0)

def rotate(field_rows, positions):
    half_rot = ROT // 2
    frequency = 10000.0 ** (-jnp.arange(half_rot, dtype=jnp.float32) * 2.0 / ROT)
    angles = positions.astype(jnp.float32)[:, None] * frequency[None, :]
    cosine = jnp.cos(angles)[:, None, :]
    sinusoid = jnp.sin(angles)[:, None, :]
    first_half = field_rows[..., :half_rot]
    second_half = field_rows[..., half_rot:ROT]
    passive = field_rows[..., ROT:]
    return jnp.concatenate([first_half * cosine - second_half * sinusoid, second_half * cosine + first_half * sinusoid, passive], -1)

def features(field_rows, table, scale_part, weight_part):
    spectrum = jnp.einsum('ghd,fd->ghf', field_rows, table, precision=HIGH)
    return weight_part[None] * jnp.exp(scale_part[None] * spectrum)

def linear_mixer(projected, scale_part, weight_part, lengths_row):
    group_rows = projected.shape[0]
    head_count = projected.shape[2]
    head_width = projected.shape[3]
    blocks = group_rows // BLOCK
    lengths_row = lengths_row.astype(jnp.int32)
    starts = (jnp.cumsum(lengths_row) - lengths_row).astype(jnp.int32)
    block_ids = jnp.arange(blocks, dtype=jnp.int32)
    started = starts[None, :] <= block_ids[:, None]
    segment = lax.optimization_barrier(jnp.sum(started.astype(jnp.int32), 1)).astype(jnp.int32)
    seg_start = lax.optimization_barrier(jnp.max(jnp.where(started, starts[None, :], 0), 1)).astype(jnp.int32)
    positions = jnp.arange(group_rows, dtype=jnp.int32) - jnp.repeat(seg_start, BLOCK, total_repeat_length=group_rows) * BLOCK
    table = dct_table(head_width)
    queries = rotate(projected[:, 0], positions)
    keys_rot = rotate(projected[:, 1], positions)
    values = low(projected[:, 2]).reshape(blocks, BLOCK, head_count, head_width)
    feat_q = low(features(queries, table, scale_part, weight_part)).reshape(blocks, BLOCK, head_count, head_width)
    feat_k = low(features(keys_rot, table, scale_part, weight_part)).reshape(blocks, BLOCK, head_count, head_width)
    causal = jnp.arange(BLOCK)[:, None] >= jnp.arange(BLOCK)[None, :]
    scores = jnp.einsum('bthf,bshf->bhts', feat_q, feat_k, precision=HIGH)
    scores = jnp.where(causal[None, None], scores, 0.0)
    states = jnp.einsum('bshf,bshd->bhfd', feat_k, values, precision=HIGH)
    totals = lax.optimization_barrier(jnp.sum(feat_k, 1))
    earlier = jnp.where((block_ids[None, :] < block_ids[:, None]) & (segment[None, :] == segment[:, None]), 1.0, 0.0).astype(jnp.float32)
    carried = jnp.einsum('ac,chfd->ahfd', earlier, states, precision=HIGH)
    carried_sum = jnp.einsum('ac,chf->ahf', earlier, totals, precision=HIGH)
    numerator = jnp.einsum('bthf,bhfd->bthd', feat_q, low(carried), precision=HIGH)
    numerator = numerator + jnp.einsum('bhts,bshd->bthd', low(scores), values, precision=HIGH)
    denominator = jnp.einsum('bthf,bhf->bth', feat_q, carried_sum, precision=HIGH)
    denominator = denominator + jnp.swapaxes(lax.optimization_barrier(jnp.sum(scores, -1)), 1, 2)
    return (numerator / denominator[..., None]).reshape(group_rows, head_count * head_width)

def layer_norm(row_block, gain, bias):
    average = lax.optimization_barrier(jnp.mean(row_block, -1, keepdims=True))
    centered = row_block - average
    variance = lax.optimization_barrier(jnp.mean(centered * centered, -1, keepdims=True))
    return centered * lax.rsqrt(variance + 1e-05) * gain + bias

def group_forward(row_block, lengths_row, params):
    gain_one, bias_one, gain_two, bias_two, w_qkv, w_out, w_up, w_down, scale_part, weight_part = params
    normed_one = low(layer_norm(row_block, gain_one, bias_one))
    normed_two = low(layer_norm(row_block, gain_two, bias_two))
    projected = low_back(jnp.einsum('gd,sde->gse', normed_one, w_qkv, precision=HIGH))
    projected = projected.reshape(GROUP, 3, HEADS, HEAD_DIM)
    mixed = low(linear_mixer(projected, scale_part, weight_part, lengths_row))
    attn_out = jnp.dot(mixed, w_out, precision=HIGH)
    up_proj = low_back(jnp.dot(normed_two, w_up, precision=HIGH))
    hidden = low(jax.nn.gelu(up_proj, approximate=False))
    feed_out = jnp.dot(hidden, w_down, precision=HIGH)
    return row_block + attn_out + feed_out

def reference(tokens, ln1_gain, ln1_bias, ln2_gain, ln2_bias, w_qkv, w_out, w_up, w_down, feature_scale, feature_weight, lengths, cotangent):
    params = (ln1_gain.astype(jnp.float32), ln1_bias.astype(jnp.float32), ln2_gain.astype(jnp.float32), ln2_bias.astype(jnp.float32), w_qkv.astype(jnp.float32), w_out.astype(jnp.float32), w_up.astype(jnp.float32), w_down.astype(jnp.float32), feature_scale.astype(jnp.float32), feature_weight.astype(jnp.float32))
    token_rows = tokens.astype(jnp.float32)

    def forward(rows_in, weights_in):
        shaped = rows_in.reshape(N_DP, GROUP, D)

        def one_group(packed):
            return group_forward(packed[0], packed[1], weights_in)
        outputs = lax.map(jax.checkpoint(one_group), (shaped, lengths))
        return outputs.reshape(TOKENS, D)
    outputs, pullback = jax.vjp(forward, token_rows, params)
    input_grad, weight_grads = pullback(cotangent.astype(jnp.float32))
    return (outputs.astype(jnp.bfloat16), input_grad.astype(jnp.bfloat16), weight_grads[0], weight_grads[1], weight_grads[2], weight_grads[3], weight_grads[4], weight_grads[5], weight_grads[6], weight_grads[7], weight_grads[8], weight_grads[9])
```

```python
import functools
import math

import jax
import jax.numpy as jnp
import ml_dtypes
import numpy as np
from jax import lax
from jax.experimental import pallas as pl
from jax.experimental.pallas import tpu as pltpu
from jax.sharding import PartitionSpec as P

HEAD_DIM = 64
ROT = 16
BLOCK = 64
CHUNK = 128
TILE = 256
SUB = 32
MESH = pl.DeviceIdType.MESH
F32 = jnp.float32
BF = jnp.bfloat16
NN = (((1,), (0,)), ((), ()))
NT = (((1,), (1,)), ((), ()))
TN = (((0,), (0,)), ((), ()))


def dot(left, right, dims=NN):
    return lax.dot_general(left, right, dims, preferred_element_type=F32)


def split(value):
    high = value.astype(BF)
    return high, (value - high.astype(F32)).astype(BF)


def wide(parts, axis=1):
    return jnp.concatenate(parts, axis)


def tables(blocks, heads):
    width = heads * HEAD_DIM
    freq, dims = np.arange(HEAD_DIM)[:, None], np.arange(HEAD_DIM)[None, :]
    dct = np.cos(np.pi * (dims + 0.5) * freq / HEAD_DIM) * math.sqrt(2.0 / HEAD_DIM)
    dct[0] *= math.sqrt(0.5)
    dct = np.kron(np.eye(heads), dct).astype(np.float32)
    high = dct.astype(ml_dtypes.bfloat16)
    low = (dct - high.astype(np.float32)).astype(ml_dtypes.bfloat16)
    forward = np.concatenate([high.T, high.T, low.T], 0)
    backward = np.concatenate([high, high, low], 0)
    half = ROT // 2
    lane = np.arange(2 * HEAD_DIM) % HEAD_DIM
    rate = np.where(lane < ROT, 10000.0 ** (-(lane % half) * 2.0 / ROT), 0.0)
    in_block = np.arange(BLOCK)[:, None] * rate[None]
    of_block = np.arange(blocks)[:, None] * BLOCK * rate[None]
    signs = np.stack([np.where(lane < half, -1.0, 0.0), np.where((lane >= half) & (lane < ROT), 1.0, 0.0)] + [0.0 * lane] * 6)
    angles = np.concatenate([np.cos(in_block), np.sin(in_block), np.cos(of_block), np.sin(of_block), signs], 0)
    diagonal = np.kron(np.eye(heads), np.ones((HEAD_DIM, HEAD_DIM)))
    masks = np.kron(np.eye(heads), np.ones((CHUNK, HEAD_DIM)))
    return (
        forward,
        backward,
        angles.astype(np.float32),
        diagonal.astype(np.float32),
        np.concatenate([diagonal, diagonal], 0).astype(ml_dtypes.bfloat16),
        masks.astype(ml_dtypes.bfloat16),
    )


def kernel(
    lengths,
    tok_in,
    cot_in,
    norms,
    w_qkv,
    w_out,
    w_up,
    w_down,
    feature,
    dct_fwd,
    dct_bwd,
    angles,
    diag,
    diag_two,
    masks,
    out_part,
    back_part,
    g_down,
    g_out,
    g_up,
    g_qkv,
    small,
    tok,
    cot,
    n_one,
    n_two,
    hid,
    slope,
    fqkv,
    spec,
    mixed,
    att,
    rden,
    states,
    ksums,
    state,
    krow,
    stage,
    wide_one,
    wide_two,
    sums,
    feat_sums,
    local_sem,
    send_sem,
    recv_sem,
    stage_sem,
):
    rows_own = tok_in.shape[0]
    rows = tok.shape[0]
    width = w_out.shape[0]
    heads = width // HEAD_DIM
    chunks = rows // CHUNK
    half_rows = rows_own // 2
    me = lax.axis_index("tensor")
    core = lax.rem(me, 2)
    mate = me + 1 - 2 * core
    peer = lax.rem(me + 2, 4)
    cross = 3 - me

    barrier = pltpu.get_barrier_semaphore()
    for other in (mate, peer):
        pl.semaphore_signal(barrier, inc=1, device_id={"tensor": other}, device_id_type=MESH)
    pl.semaphore_wait(barrier, 2)

    def slot(buf, owner, piece=None):
        if piece is None:
            return buf.at[pl.ds(pl.multiple_of(owner * rows_own, rows_own), rows_own)]
        return buf.at[pl.ds(pl.multiple_of(owner * rows_own + piece * half_rows, half_rows), half_rows)]

    class Gather:
        def __init__(self, source, buf, base):
            self.source, self.buf, self.base = source, buf, base

        def copy(self, number, src, dst, target):
            return pltpu.make_async_remote_copy(
                src_ref=src,
                dst_ref=dst,
                send_sem=send_sem.at[self.base + number],
                recv_sem=recv_sem.at[self.base + number],
                device_id={"tensor": target},
                device_id_type=MESH,
            )

        def local(self):
            return pltpu.make_async_copy(self.source, slot(self.buf, me), local_sem.at[self.base])

        def to_mate(self, owner):
            return self.copy(0, self.source, slot(self.buf, owner), mate)

        def to_peer(self, owner, piece):
            part = self.source.at[pl.ds(piece * half_rows, half_rows)]
            return self.copy(1 + piece, part, slot(self.buf, owner, piece), peer)

        def forward(self, owner, piece):
            return self.copy(3 + piece, slot(self.buf, owner, piece), slot(self.buf, owner, piece), mate)

    g_tok, g_cot = Gather(tok_in, tok, 0), Gather(cot_in, cot, 5)
    g_tok.to_mate(me).start()
    for piece in range(2):
        g_tok.to_peer(me, piece).start()
    g_tok.local().start()
    g_cot.to_mate(me).start()
    g_cot.local().start()

    start_one = lengths[0, 0]
    start_two = start_one + lengths[0, 1]

    def segment(block):
        return (block >= start_one).astype(jnp.int32) + (block >= start_two).astype(jnp.int32)

    def in_sequence(block):
        return block - jnp.where(block >= start_two, start_two, jnp.where(block >= start_one, start_one, 0))

    gain_one, bias_one, gain_two, bias_two = (norms[i : i + 1, :] for i in range(4))
    scale_row, weight_row = feature[0:1, :], feature[1:2, :]
    blocks = rows // BLOCK

    def rotation(row0, count):
        cos_in, sin_in = angles[0:BLOCK, :], angles[BLOCK : 2 * BLOCK, :]
        sign_a = angles[2 * BLOCK + 2 * blocks : 2 * BLOCK + 2 * blocks + 1, :]
        sign_b = angles[2 * BLOCK + 2 * blocks + 1 : 2 * BLOCK + 2 * blocks + 2, :]
        cosines, sines = [], []
        for k in range(count):
            place = in_sequence(lax.div(row0, BLOCK) + k)
            cos_at = angles[pl.ds(2 * BLOCK + place, 1), :]
            sin_at = angles[pl.ds(2 * BLOCK + blocks + place, 1), :]
            cosines.append(cos_in * cos_at - sin_in * sin_at)
            sines.append(sin_in * cos_at + cos_in * sin_at)
        cosine, sine = wide(cosines, 0), wide(sines, 0)
        return cosine, sine * sign_a, sine * sign_b

    def rotate(field, turn, back=False):
        cosine, sine_a, sine_b = turn
        parts = []
        for at in range(0, width, 2 * HEAD_DIM):
            part = field[:, at : at + 2 * HEAD_DIM]
            ahead = pltpu.roll(part, 2 * HEAD_DIM - ROT // 2, 1) * sine_a
            behind = pltpu.roll(part, ROT // 2, 1) * sine_b
            parts.append(part * cosine - (ahead + behind) if back else part * cosine + (ahead + behind))
        return wide(parts)

    def centered(at, size):
        value = tok[pl.ds(at, size), :].astype(F32)
        value = value - jnp.mean(value, -1, keepdims=True)
        deviation = lax.rsqrt(jnp.mean(value * value, -1, keepdims=True) + 1e-05)
        return value * deviation, deviation

    def project(j, carry):
        @pl.when(j == 0)
        def _():
            g_tok.local().wait()

        @pl.when(j == 2)
        def _():
            g_tok.to_mate(mate).wait_recv()

        for piece in range(2):

            @pl.when(j == 4 + 2 * piece)
            def _():
                g_tok.to_peer(peer, piece).wait_recv()
                g_tok.forward(peer, piece).start()
                g_cot.to_peer(me, piece).start()

            @pl.when(j == 5 + 2 * piece)
            def _():
                g_tok.forward(cross, piece).wait_recv()

        late = lax.div(j, 4)
        owner_early = jnp.where(j < 2, me, mate)
        owner_late = jnp.where(lax.rem(j, 2) == 0, peer, cross)
        owner = jnp.where(late == 0, owner_early, owner_late)
        piece = jnp.where(late == 0, lax.rem(j, 2), lax.div(j - 4, 2))
        row0 = pl.multiple_of(owner * rows_own + piece * TILE, TILE)

        def norm(i, inner):
            at = pl.multiple_of(row0 + i * SUB, SUB)
            unit, _ = centered(at, SUB)
            n_one[pl.ds(at, SUB), :] = (unit * gain_one + bias_one).astype(BF)
            n_two[pl.ds(at, SUB), :] = (unit * gain_two + bias_two).astype(BF)
            return inner

        lax.fori_loop(0, TILE // SUB, norm, 0)
        here = pl.ds(row0, TILE)
        first = n_one[here, :]
        turn = rotation(row0, TILE // BLOCK)
        for s in range(2):
            high, low = split(rotate(dot(first, w_qkv[s]), turn))
            spectrum = dot(wide([high, low, high]), dct_fwd[...])
            spec[s, here, :] = spectrum
            fqkv[here, s * width : (s + 1) * width] = (weight_row * jnp.exp(scale_row * spectrum)).astype(BF)
        fqkv[here, 2 * width : 3 * width] = dot(first, w_qkv[2]).astype(BF)
        second = n_two[here, :]
        for at in range(0, w_up.shape[1], TILE):
            up = dot(second, w_up[:, at : at + TILE])
            below = 0.5 * (1.0 + lax.erf(up * math.sqrt(0.5)))
            hid[here, at : at + TILE] = (up * below).astype(BF)
            slope[here, at : at + TILE] = below + up * (jnp.exp(-0.5 * up * up) * (1.0 / math.sqrt(2.0 * math.pi)))
        return carry

    lax.fori_loop(0, rows // TILE, project, 0)

    grid_t = lax.broadcasted_iota(jnp.int32, (CHUNK, CHUNK), 0)
    grid_s = lax.broadcasted_iota(jnp.int32, (CHUNK, CHUNK), 1)
    causal = jnp.where((grid_t >= grid_s) & ((grid_t < BLOCK) | (grid_s >= BLOCK)), 1.0, 0.0).astype(F32)

    def joined(block):
        return jnp.where(segment(block) == segment(block - 1), jnp.float32(1.0), jnp.float32(0.0))

    def per_head(value):
        return [value * masks[h * CHUNK : (h + 1) * CHUNK, :] for h in range(heads)]

    def halves(value):
        return [value[k * BLOCK : (k + 1) * BLOCK] for k in range(CHUNK // BLOCK)]

    state[...] = jnp.zeros_like(state)
    krow[...] = jnp.zeros_like(krow)

    def mix(i, carry):
        here = pl.ds(pl.multiple_of(i * CHUNK, CHUNK), CHUNK)
        query, key, value = (fqkv[here, s * width : (s + 1) * width] for s in range(3))
        stacked = dot(wide(per_head(query), 0), key, NT)
        highs, lows = zip(*(split(stacked[h * CHUNK : (h + 1) * CHUNK] * causal) for h in range(heads)))
        scores = wide(highs)
        over = dot(scores, wide(per_head(value), 0))
        under = dot(scores, masks[...]) + dot(wide(lows), masks[...])
        now, row = state[...], krow[0:1, :]
        overs, rows_under = [], []
        for k, (query_k, key_k, value_k) in enumerate(zip(*map(halves, (query, key, value)))):
            carried = now.astype(BF)
            states[2 * i + k] = carried
            ksums[2 * i + k] = jnp.broadcast_to(row, (8, width))
            overs.append(dot(query_k, carried))
            rows_under.append(query_k.astype(F32) * row)
            keep = joined(2 * i + k + 1)
            now = (now + dot(key_k, value_k, TN) * diag[...]) * keep
            row = (row + jnp.sum(key_k.astype(F32), 0, keepdims=True)) * keep
        state[...] = now
        krow[0:1, :] = row
        high, low = split(wide(rows_under, 0))
        over = over + wide(overs, 0)
        under = under + dot(wide([high, low]), diag_two[...])
        inverse = 1.0 / under
        attended = over * inverse
        att[here, :] = attended
        rden[here, :] = inverse
        mixed[here, :] = attended.astype(BF)
        return carry

    lax.fori_loop(0, chunks, mix, 0)

    for piece in range(2):
        g_cot.to_peer(peer, piece).wait_recv()
        g_cot.forward(peer, piece).start()

    def staged(number, target):
        return pltpu.make_async_copy(stage.at[number], target, stage_sem.at[number])

    def put(j, tile, target, first):
        number = lax.rem(j, 2)
        if first is None:
            staged(number, target).wait()
        else:

            @pl.when(j >= first + 2)
            def _():
                staged(number, target).wait()

        stage[number] = tile.astype(BF)
        staged(number, target).start()

    def drain(target):
        for number in range(2):
            staged(number, target).wait()

    def produce(j, carry):
        here = pl.ds(pl.multiple_of(j * TILE, TILE), TILE)
        tile = dot(mixed[here, :], w_out[...]) + dot(hid[here, :], w_down[...])
        put(j, tile, out_part.at[here], 0)
        return carry

    lax.fori_loop(0, rows // TILE, produce, 0)
    drain(out_part.at[pl.ds(0, TILE)])

    for piece in range(2):
        g_cot.forward(cross, piece).wait_recv()
    g_cot.to_mate(mate).wait_recv()
    g_cot.local().wait()

    def down(j, carry):
        at = pl.ds(pl.multiple_of(j * TILE, TILE), TILE)
        put(j, dot(hid[:, at], cot[...], TN), g_down.at[at], 0)
        return carry

    lax.fori_loop(0, hid.shape[1] // TILE, down, 0)
    put(0, dot(mixed[...], cot[...], TN), g_out, None)
    drain(g_out)

    def descend(j, carry):
        here = pl.ds(pl.multiple_of(j * TILE, TILE), TILE)
        for at in range(0, hid.shape[1], TILE):
            d_hidden = dot(cot[here, :], w_down[at : at + TILE, :], NT)
            hid[here, at : at + TILE] = (d_hidden * slope[here, at : at + TILE]).astype(BF)
        return carry

    lax.fori_loop(0, rows // TILE, descend, 0)

    def upward(j, carry):
        at = pl.ds(pl.multiple_of(j * TILE, TILE), TILE)
        put(j, dot(n_two[:, at], hid[...], TN), g_up.at[at], 0)
        return carry

    lax.fori_loop(0, n_two.shape[1] // TILE, upward, 0)
    drain(g_out)

    state[...] = jnp.zeros_like(state)
    krow[...] = jnp.zeros_like(krow)
    feat_sums[...] = jnp.zeros_like(feat_sums)

    def unmix(step, carry):
        i = chunks - 1 - step
        row0 = pl.multiple_of(i * CHUNK, CHUNK)
        here = pl.ds(row0, CHUNK)
        query, key, value = (fqkv[here, s * width : (s + 1) * width] for s in range(3))
        inverse, attended = rden[here, :], att[here, :]
        d_over = dot(cot[here, :], w_out[...], NT) * inverse
        high, low = split(d_over * attended)
        d_under = -dot(wide([high, low]), diag_two[...])
        over_high, over_low = split(d_over)
        both = wide([wide(per_head(over_high), 0), wide(per_head(over_low), 0)])
        stacked = dot(both, wide([value, value]), NT)
        heads_high, heads_low = [], []
        for h in range(heads):
            d_scores = stacked[h * CHUNK : (h + 1) * CHUNK] + d_under[:, h * HEAD_DIM : h * HEAD_DIM + 1]
            high, low = split(d_scores * causal)
            heads_high.append(high)
            heads_low.append(low)
        query_heads = wide(per_head(query), 0)
        key_heads = wide(per_head(key), 0)
        over_both = wide([over_high, over_low])
        d_query = dot(wide(heads_high + heads_low), wide([key_heads, key_heads], 0))
        d_key = dot(wide(heads_high + heads_low, 0), wide([query_heads, query_heads], 0), TN)
        stacked = dot(query_heads, key, NT)
        scores = [(stacked[h * CHUNK : (h + 1) * CHUNK] * causal).astype(BF) for h in range(heads)]
        d_value = dot(wide(scores, 0), both, TN)
        d_value = d_value[:, :width] + d_value[:, width:]
        later, later_row = state[...], krow[0:1, :]
        more_query, more_key, more_value = [], [], []
        parts = list(zip(*map(halves, (query, key, value, over_both, over_high, over_low, d_under))))
        for k in reversed(range(len(parts))):
            query_k, key_k, value_k, both_k, high_k, low_k, under_k = parts[k]
            carried, row = states[2 * i + k], ksums[2 * i + k][0:1, :]
            more_query.insert(0, dot(both_k, wide([carried, carried]), NT) + under_k * row)
            keep = joined(2 * i + k + 1)
            later_high, later_low = split(later * keep)
            more_key.insert(0, dot(wide([value_k, value_k]), wide([later_high, later_low]), NT) + later_row * keep)
            more_value.insert(0, dot(wide([key_k, key_k]), wide([later_high, later_low], 0)))
            add = dot(wide([query_k, query_k], 0), wide([high_k, low_k], 0), TN)
            later = later * keep + add * diag[...]
            later_row = later_row * keep + jnp.sum(query_k.astype(F32) * under_k, 0, keepdims=True)
        state[...] = later
        krow[0:1, :] = later_row
        d_query = d_query + wide(more_query, 0)
        d_key = d_key + wide(more_key, 0)
        d_value = d_value + wide(more_value, 0)
        turn = rotation(row0, CHUNK // BLOCK)
        for s, grad in enumerate((d_query, d_key)):
            spectrum = spec[s, here, :]
            grad = grad * (weight_row * jnp.exp(scale_row * spectrum))
            feat_sums[0:1, :] += jnp.sum(grad * spectrum, 0, keepdims=True)
            feat_sums[1:2, :] += jnp.sum(grad, 0, keepdims=True)
            high, low = split(grad * scale_row)
            fqkv[here, s * width : (s + 1) * width] = rotate(
                dot(wide([high, low, high]), dct_bwd[...]), turn, True
            ).astype(BF)
        fqkv[here, 2 * width : 3 * width] = d_value.astype(BF)
        return carry

    lax.fori_loop(0, chunks, unmix, 0)

    def projected(j, carry):
        at = pl.ds(pl.multiple_of(j * TILE, TILE), TILE)
        number = lax.rem(j, 2)
        tile = dot(n_one[:, at], fqkv[...], TN)

        def piece(s):
            return pltpu.make_async_copy(
                stage.at[number, :, s * width : (s + 1) * width], g_qkv.at[s, at], stage_sem.at[number]
            )

        @pl.when(j >= 2)
        def _():
            for s in range(3):
                piece(s).wait()

        stage[number, :, 0 : 3 * width] = tile.astype(BF)
        for s in range(3):
            piece(s).start()
        return carry

    lax.fori_loop(0, n_one.shape[1] // TILE, projected, 0)
    for number in range(2):
        for s in range(3):
            pltpu.make_async_copy(
                stage.at[number, :, s * width : (s + 1) * width], g_qkv.at[s, pl.ds(0, TILE)], stage_sem.at[number]
            ).wait()

    sums[...] = jnp.zeros_like(sums)

    def inputs(j, carry):
        row0 = pl.multiple_of(j * TILE, TILE)
        here = pl.ds(row0, TILE)
        total = dot(fqkv[here, 0:width], w_qkv[0], NT)
        for s in (1, 2):
            total = total + dot(fqkv[here, s * width : (s + 1) * width], w_qkv[s], NT)
        wide_one[...] = total
        wide_two[...] = dot(hid[here, :], w_up[...], NT)

        def fold(i, inner):
            at = pl.ds(pl.multiple_of(i * SUB, SUB), SUB)
            unit, _ = centered(pl.multiple_of(row0 + i * SUB, SUB), SUB)
            one, two = wide_one[at, :], wide_two[at, :]
            for number, term in enumerate((one * unit, one, two * unit, two)):
                sums[number] += jnp.sum(term.reshape(SUB // 8, 8, term.shape[1]), 0)
            wide_one[at, :] = one * gain_one + two * gain_two
            return inner

        lax.fori_loop(0, TILE // SUB, fold, 0)
        put(j, wide_one[...], back_part.at[here], 0)
        return carry

    lax.fori_loop(0, rows // TILE, inputs, 0)
    drain(back_part.at[pl.ds(0, TILE)])
    small[...] = jnp.zeros_like(small)
    for number in range(4):
        small[number : number + 1, :] = jnp.sum(sums[number], 0, keepdims=True)
    small[4:5, 0:width] = feat_sums[0:1, :]
    small[5:6, 0:width] = feat_sums[1:2, :] / weight_row

    for gather in (g_tok, g_cot):
        gather.to_mate(me).wait_send()
        for piece in range(2):
            gather.to_peer(me, piece).wait_send()
            gather.forward(peer, piece).wait_send()


def shards(
    tokens,
    ln1_gain,
    ln1_bias,
    ln2_gain,
    ln2_bias,
    w_qkv,
    w_out,
    w_up,
    w_down,
    feature_scale,
    feature_weight,
    lengths,
    cotangent,
):
    rows_own, model = tokens.shape
    rows = 4 * rows_own
    heads = feature_scale.shape[0]
    width = heads * HEAD_DIM
    hidden = w_up.shape[1]
    consts = tables(rows // BLOCK, heads)
    norms = jnp.stack([ln1_gain, ln1_bias, ln2_gain, ln2_bias])
    feature = jnp.stack([feature_scale.reshape(-1), feature_weight.reshape(-1)])
    anywhere = pl.BlockSpec(memory_space=pl.ANY)
    vmem = pl.BlockSpec(memory_space=pltpu.VMEM)
    smem = pl.BlockSpec(memory_space=pltpu.SMEM)
    shape = jax.ShapeDtypeStruct
    out_part, back_part, g_down, g_out, g_up, g_qkv, small = pl.pallas_call(
        kernel,
        out_shape=(
            shape((rows, model), BF),
            shape((rows, model), BF),
            shape((hidden, model), BF),
            shape((width, model), BF),
            shape((model, hidden), BF),
            shape((3, model, width), BF),
            shape((8, model), F32),
        ),
        in_specs=[smem, anywhere, anywhere] + [vmem] * 12,
        out_specs=(anywhere,) * 6 + (vmem,),
        scratch_shapes=[
            pltpu.VMEM((rows, model), BF),
            pltpu.VMEM((rows, model), BF),
            pltpu.VMEM((rows, model), BF),
            pltpu.VMEM((rows, model), BF),
            pltpu.VMEM((rows, hidden), BF),
            pltpu.VMEM((rows, hidden), F32),
            pltpu.VMEM((rows, 3 * width), BF),
            pltpu.VMEM((2, rows, width), F32),
            pltpu.VMEM((rows, width), BF),
            pltpu.VMEM((rows, width), F32),
            pltpu.VMEM((rows, width), F32),
            pltpu.VMEM((rows // BLOCK, width, width), BF),
            pltpu.VMEM((rows // BLOCK, 8, width), F32),
            pltpu.VMEM((width, width), F32),
            pltpu.VMEM((8, width), F32),
            pltpu.VMEM((2, TILE, model), BF),
            pltpu.VMEM((TILE, model), F32),
            pltpu.VMEM((TILE, model), F32),
            pltpu.VMEM((4, 8, model), F32),
            pltpu.VMEM((8, width), F32),
            pltpu.SemaphoreType.DMA((10,)),
            pltpu.SemaphoreType.DMA((10,)),
            pltpu.SemaphoreType.DMA((10,)),
            pltpu.SemaphoreType.DMA((2,)),
        ],
        compiler_params=pltpu.CompilerParams(
            collective_id=0, has_side_effects=True, vmem_limit_bytes=63 * 2**20
        ),
    )(lengths, tokens, cotangent, norms, w_qkv, w_out, w_up, w_down, feature, *consts)
    branches = lax.psum_scatter(out_part.astype(F32), "tensor", scatter_dimension=0, tiled=True).astype(F32)
    mixed_out = (tokens.astype(F32) + branches).astype(BF)
    d_rows = lax.psum_scatter(back_part.astype(F32), "tensor", scatter_dimension=0, tiled=True).astype(F32)
    rows_in = tokens.astype(F32)
    unit = rows_in - jnp.mean(rows_in, -1, keepdims=True)
    deviation = lax.rsqrt(jnp.mean(unit * unit, -1, keepdims=True) + 1e-05)
    unit = unit * deviation
    inner = d_rows - jnp.mean(d_rows, -1, keepdims=True) - unit * jnp.mean(d_rows * unit, -1, keepdims=True)
    input_grad = (cotangent.astype(F32) + deviation * inner).astype(BF)
    g_down, g_out, g_up, g_qkv = (
        lax.psum(tuple(g.astype(F32) for g in (g_down, g_out, g_up, g_qkv)), "dp")
    )
    norm_sums = lax.psum(small[0:4], ("dp", "tensor"))
    feat_sums = lax.psum(small[4:6, 0:width], "dp").reshape(2, heads, HEAD_DIM)
    return (
        mixed_out,
        input_grad,
        norm_sums[0],
        norm_sums[1],
        norm_sums[2],
        norm_sums[3],
        g_qkv,
        g_out,
        g_up,
        g_down,
        feat_sums[0],
        feat_sums[1],
    )


def solution(mesh):
    placed = (
        P(("dp", "tensor"), None),
        P(),
        P(),
        P(),
        P(),
        P(None, None, "tensor"),
        P("tensor", None),
        P(None, "tensor"),
        P("tensor", None),
        P("tensor", None),
        P("tensor", None),
        P("dp", None),
        P(("dp", "tensor"), None),
    )
    return jax.shard_map(
        shards,
        mesh=mesh,
        in_specs=placed,
        out_specs=(
            P(("dp", "tensor"), None),
            P(("dp", "tensor"), None),
            P(),
            P(),
            P(),
            P(),
            P(None, None, "tensor"),
            P("tensor", None),
            P(None, "tensor"),
            P("tensor", None),
            P("tensor", None),
            P("tensor", None),
        ),
        check_vma=False,
    )
```

```python
import functools
import math

import jax
import jax.numpy as jnp
import ml_dtypes
import numpy as np
from jax import lax
from jax.experimental import pallas as pl
from jax.experimental.pallas import tpu as pltpu
from jax.sharding import PartitionSpec as P

HEAD_DIM = 64
ROT = 16
BLOCK = 64
CHUNK = 128
TILE = 256
UNIT = 128
SUB = 32
SLOTS = 12
MESH = pl.DeviceIdType.MESH
F32 = jnp.float32
BF = jnp.bfloat16
NN = (((1,), (0,)), ((), ()))
NT = (((1,), (1,)), ((), ()))
TN = (((0,), (0,)), ((), ()))


def dot(left, right, dims=NN):
    return lax.dot_general(left, right, dims, preferred_element_type=F32)


def split(value):
    high = value.astype(BF)
    return high, (value - high.astype(F32)).astype(BF)


def wide(parts, axis=1):
    return jnp.concatenate(parts, axis)


def tables(blocks, heads):
    width = heads * HEAD_DIM
    freq, dims = np.arange(HEAD_DIM)[:, None], np.arange(HEAD_DIM)[None, :]
    dct = np.cos(np.pi * (dims + 0.5) * freq / HEAD_DIM) * math.sqrt(2.0 / HEAD_DIM)
    dct[0] *= math.sqrt(0.5)
    dct = np.kron(np.eye(heads), dct).astype(np.float32)
    high = dct.astype(ml_dtypes.bfloat16)
    low = (dct - high.astype(np.float32)).astype(ml_dtypes.bfloat16)
    halves = np.concatenate([high, high, low], 1)
    half = ROT // 2
    lane = np.arange(2 * HEAD_DIM) % HEAD_DIM
    rate = np.where(lane < ROT, 10000.0 ** (-(lane % half) * 2.0 / ROT), 0.0)
    in_block = np.arange(BLOCK)[:, None] * rate[None]
    of_block = np.arange(blocks)[:, None] * BLOCK * rate[None]
    signs = np.stack([np.where(lane < half, -1.0, 0.0), np.where((lane >= half) & (lane < ROT), 1.0, 0.0)] + [0.0 * lane] * 6)
    angles = np.concatenate([np.cos(in_block), np.sin(in_block), np.cos(of_block), np.sin(of_block), signs], 0)
    diagonal = np.kron(np.eye(heads), np.ones((HEAD_DIM, HEAD_DIM)))
    masks = np.kron(np.eye(heads), np.ones((CHUNK, HEAD_DIM)))
    return (
        halves,
        angles.astype(np.float32),
        np.concatenate([diagonal, diagonal], 0).astype(ml_dtypes.bfloat16),
        masks.astype(ml_dtypes.bfloat16),
    )


def kernel(
    reduce_dp,
    lengths,
    tok_in,
    cot_in,
    gain_one_in,
    bias_one_in,
    gain_two_in,
    bias_two_in,
    w_qkv,
    w_out,
    w_up,
    w_down,
    feature_scale,
    feature_weight,
    dct,
    angles,
    diag_two,
    masks,
    mixed_out,
    input_grad,
    grads_out,
    qkv_out,
    slopes,
    own_part,
    small,
    feat_out,
    tok,
    cot,
    n_one,
    n_two,
    hid,
    fqkv,
    spec,
    mixed,
    att,
    rden,
    states,
    ksums,
    state,
    krow,
    grads,
    recv_a,
    recv_b,
    rs_out,
    rs_in,
    y_in,
    temp,
    sums,
    feat_sums,
    small_in,
    local_sem,
    send_sem,
    recv_sem,
    ar_send,
    ar_recv,
    rs_send,
    rs_recv,
    small_send,
    small_recv,
    grad_sem,
    temp_sem,
    result_sem,
    free_mate,
    free_peer,
):
    rows_own = tok_in.shape[0]
    rows = tok.shape[0]
    width = w_out.shape[0]
    heads = width // HEAD_DIM
    chunks = rows // CHUNK
    half_rows = rows_own // 2
    me = lax.axis_index("tensor")
    core = lax.rem(me, 2)
    mate = me + 1 - 2 * core
    peer = lax.rem(me + 2, 4)
    cross = 3 - me
    group = lax.axis_index("dp")
    along_x = lax.rem(group, 2)
    across = group + 1 - 2 * along_x
    along_z = lax.div(group, 2)
    middle = along_z * (3 - along_z)

    def at_end(step):
        pl.when(middle == 0)(step)

    def at_mid(step):
        pl.when(middle > 0)(step)

    side = jnp.where(along_z < 2, 0, 1)
    inward = group + 2 - 4 * side
    outward = group - 2 + 4 * side
    units = grads.shape[0]

    barrier = pltpu.get_barrier_semaphore()
    for other in (mate, peer):
        pl.semaphore_signal(barrier, inc=1, device_id={"tensor": other}, device_id_type=MESH)
    if reduce_dp:
        for other in (across, inward):
            pl.semaphore_signal(barrier, inc=1, device_id={"dp": other}, device_id_type=MESH)

        @at_mid
        def _():
            pl.semaphore_signal(barrier, inc=1, device_id={"dp": outward}, device_id_type=MESH)
            pl.semaphore_wait(barrier, 5)

        @at_end
        def _():
            pl.semaphore_wait(barrier, 4)
    else:
        pl.semaphore_wait(barrier, 2)

    def slot(buf, owner, piece=None):
        if piece is None:
            return buf.at[pl.ds(pl.multiple_of(owner * rows_own, rows_own), rows_own)]
        return buf.at[pl.ds(pl.multiple_of(owner * rows_own + piece * half_rows, half_rows), half_rows)]

    class Gather:
        def __init__(self, source, buf, base):
            self.source, self.buf, self.base = source, buf, base

        def copy(self, number, src, dst, target):
            return pltpu.make_async_remote_copy(
                src_ref=src,
                dst_ref=dst,
                send_sem=send_sem.at[self.base + number],
                recv_sem=recv_sem.at[self.base + number],
                device_id={"tensor": target},
                device_id_type=MESH,
            )

        def local(self):
            return pltpu.make_async_copy(self.source, slot(self.buf, me), local_sem.at[self.base])

        def to_mate(self, owner):
            return self.copy(0, self.source, slot(self.buf, owner), mate)

        def to_peer(self, owner, piece):
            part = self.source.at[pl.ds(piece * half_rows, half_rows)]
            return self.copy(1 + piece, part, slot(self.buf, owner, piece), peer)

        def forward(self, owner, piece):
            return self.copy(3 + piece, slot(self.buf, owner, piece), slot(self.buf, owner, piece), mate)

    g_tok, g_cot = Gather(tok_in, tok, 0), Gather(cot_in, cot, 5)
    g_tok.to_mate(me).start()
    for piece in range(2):
        g_tok.to_peer(me, piece).start()
    g_tok.local().start()
    g_cot.to_mate(me).start()
    g_cot.local().start()

    start_one = lengths[0, 0]
    start_two = start_one + lengths[0, 1]

    def segment(block):
        return (block >= start_one).astype(jnp.int32) + (block >= start_two).astype(jnp.int32)

    def in_sequence(block):
        return block - jnp.where(block >= start_two, start_two, jnp.where(block >= start_one, start_one, 0))

    gain_one, bias_one, gain_two, bias_two = gain_one_in[...], bias_one_in[...], gain_two_in[...], bias_two_in[...]
    scale_row, weight_row = (
        wide([field[h : h + 1, :] for h in range(heads)]) for field in (feature_scale, feature_weight)
    )
    blocks = rows // BLOCK

    def rotation(row0, count):
        cos_in, sin_in = angles[0:BLOCK, :], angles[BLOCK : 2 * BLOCK, :]
        sign_a = angles[2 * BLOCK + 2 * blocks : 2 * BLOCK + 2 * blocks + 1, :]
        sign_b = angles[2 * BLOCK + 2 * blocks + 1 : 2 * BLOCK + 2 * blocks + 2, :]
        cosines, sines = [], []
        for k in range(count):
            place = in_sequence(lax.div(row0, BLOCK) + k)
            cos_at = angles[pl.ds(2 * BLOCK + place, 1), :]
            sin_at = angles[pl.ds(2 * BLOCK + blocks + place, 1), :]
            cosines.append(cos_in * cos_at - sin_in * sin_at)
            sines.append(sin_in * cos_at + cos_in * sin_at)
        cosine, sine = wide(cosines, 0), wide(sines, 0)
        return cosine, sine * sign_a, sine * sign_b

    def rotate(field, turn, back=False):
        cosine, sine_a, sine_b = turn
        parts = []
        for at in range(0, width, 2 * HEAD_DIM):
            part = field[:, at : at + 2 * HEAD_DIM]
            ahead = pltpu.roll(part, 2 * HEAD_DIM - ROT // 2, 1) * sine_a
            behind = pltpu.roll(part, ROT // 2, 1) * sine_b
            parts.append(part * cosine - (ahead + behind) if back else part * cosine + (ahead + behind))
        return wide(parts)

    def centered(at, size):
        value = tok[pl.ds(at, size), :].astype(F32)
        value = value - jnp.mean(value, -1, keepdims=True)
        deviation = lax.rsqrt(jnp.mean(value * value, -1, keepdims=True) + 1e-05)
        return value * deviation, deviation

    def project(j, carry):
        @pl.when(j == 0)
        def _():
            g_tok.local().wait()

        @pl.when(j == 2)
        def _():
            g_tok.to_mate(mate).wait_recv()

        for piece in range(2):

            @pl.when(j == 4 + 2 * piece)
            def _():
                g_tok.to_peer(peer, piece).wait_recv()
                g_tok.forward(peer, piece).start()
                g_cot.to_peer(me, piece).start()

            @pl.when(j == 5 + 2 * piece)
            def _():
                g_tok.forward(cross, piece).wait_recv()

        late = lax.div(j, 4)
        owner_early = jnp.where(j < 2, me, mate)
        owner_late = jnp.where(lax.rem(j, 2) == 0, peer, cross)
        owner = jnp.where(late == 0, owner_early, owner_late)
        piece = jnp.where(late == 0, lax.rem(j, 2), lax.div(j - 4, 2))
        row0 = pl.multiple_of(owner * rows_own + piece * TILE, TILE)

        def norm(i, inner):
            at = pl.multiple_of(row0 + i * SUB, SUB)
            unit, _ = centered(at, SUB)
            n_one[pl.ds(at, SUB), :] = (unit * gain_one + bias_one).astype(BF)
            n_two[pl.ds(at, SUB), :] = (unit * gain_two + bias_two).astype(BF)
            return inner

        lax.fori_loop(0, TILE // SUB, norm, 0)
        here = pl.ds(row0, TILE)
        first = n_one[here, :]
        turn = rotation(row0, TILE // BLOCK)
        for s in range(2):
            high, low = split(rotate(dot(first, w_qkv[s]), turn))
            spectrum = dot(wide([high, low]), dct[:, 0 : 2 * width], NT) + dot(high, dct[:, 2 * width :], NT)
            spec[s, here, :] = spectrum
            fqkv[here, s * width : (s + 1) * width] = (weight_row * jnp.exp(scale_row * spectrum)).astype(BF)
        fqkv[here, 2 * width : 3 * width] = dot(first, w_qkv[2]).astype(BF)
        second = n_two[here, :]
        parity = lax.rem(j, 2)

        @pl.when(j >= 2)
        def _():
            pltpu.make_async_copy(temp.at[parity], slopes.at[here], temp_sem.at[parity]).wait()

        for at in range(0, w_up.shape[1], TILE):
            up = dot(second, w_up[:, at : at + TILE])
            below = 0.5 * (1.0 + lax.erf(up * math.sqrt(0.5)))
            hid[here, at : at + TILE] = (up * below).astype(BF)
            temp[parity, :, at : at + TILE] = below + up * (jnp.exp(-0.5 * up * up) * (1.0 / math.sqrt(2.0 * math.pi)))
        pltpu.make_async_copy(temp.at[parity], slopes.at[here], temp_sem.at[parity]).start()
        return carry

    with jax.named_scope("project"):
        lax.fori_loop(0, rows // TILE, project, 0)
    for parity in range(2):
        pltpu.make_async_copy(temp.at[parity], slopes.at[pl.ds(0, TILE)], temp_sem.at[parity]).wait()

    grid_t = lax.broadcasted_iota(jnp.int32, (CHUNK, CHUNK), 0)
    grid_s = lax.broadcasted_iota(jnp.int32, (CHUNK, CHUNK), 1)
    causal = jnp.where((grid_t >= grid_s) & ((grid_t < BLOCK) | (grid_s >= BLOCK)), 1.0, 0.0).astype(F32)

    def joined(block):
        return jnp.where(segment(block) == segment(block - 1), jnp.float32(1.0), jnp.float32(0.0))

    def per_head(value):
        return [value * masks[h * CHUNK : (h + 1) * CHUNK, :] for h in range(heads)]

    def halves(value):
        return [value[k * BLOCK : (k + 1) * BLOCK] for k in range(CHUNK // BLOCK)]

    state[...] = jnp.zeros_like(state)
    krow[...] = jnp.zeros_like(krow)

    def mix(i, carry):
        diag = diag_two[0:width, :].astype(F32)
        here = pl.ds(pl.multiple_of(i * CHUNK, CHUNK), CHUNK)
        query, key, value = (fqkv[here, s * width : (s + 1) * width] for s in range(3))
        stacked = dot(wide(per_head(query), 0), key, NT)
        highs, lows = zip(*(split(stacked[h * CHUNK : (h + 1) * CHUNK] * causal) for h in range(heads)))
        scores = wide(highs)
        over = dot(scores, wide(per_head(value), 0))
        under = dot(scores, masks[...]) + dot(wide(lows), masks[...])
        now, row = state[...], krow[0:1, :]
        overs, rows_under = [], []
        for k, (query_k, key_k, value_k) in enumerate(zip(*map(halves, (query, key, value)))):
            carried = now.astype(BF)
            states[2 * i + k] = sum(now[h * HEAD_DIM : (h + 1) * HEAD_DIM] for h in range(heads)).astype(BF)
            ksums[2 * i + k] = jnp.broadcast_to(row, (8, width))
            overs.append(dot(query_k, carried))
            rows_under.append(query_k.astype(F32) * row)
            keep = joined(2 * i + k + 1)
            now = (now + dot(key_k, value_k, TN) * diag) * keep
            row = (row + jnp.sum(key_k.astype(F32), 0, keepdims=True)) * keep
        state[...] = now
        krow[0:1, :] = row
        high, low = split(wide(rows_under, 0))
        over = over + wide(overs, 0)
        under = under + dot(wide([high, low]), diag_two[...])
        inverse = 1.0 / under
        attended = over * inverse
        att[here, :] = attended
        rden[here, :] = wide([inverse[:, h * HEAD_DIM : h * HEAD_DIM + HEAD_DIM // 2] for h in range(heads)])
        mixed[here, :] = attended.astype(BF)
        return carry

    with jax.named_scope("mixer"):
        lax.fori_loop(0, chunks, mix, 0)

    for piece in range(2):
        g_cot.to_peer(peer, piece).wait_recv()
        g_cot.forward(peer, piece).start()

    def add_parts(base, first, count, sources):
        for at in range(0, count, SUB):
            total = base[pl.ds(first + at, SUB), :].astype(F32)
            for source, place in sources:
                total = total + source[pl.ds(place + at, SUB), :].astype(F32)
            base[pl.ds(first + at, SUB), :] = total.astype(BF)

    def bring(base, first, box, place, count):
        base[pl.ds(first, count), :] = box[pl.ds(place, count), :]

    half, quarter = UNIT // 2, UNIT // 4

    def rows_of(index, size):
        return pl.multiple_of(index * size, size)

    def hop(n, kind, source, target, device):
        return pltpu.make_async_remote_copy(
            src_ref=source,
            dst_ref=target,
            send_sem=ar_send.at[n, kind],
            recv_sem=ar_recv.at[n, kind],
            device_id={"dp": device},
            device_id_type=MESH,
        )

    plain = units - 3 * width // UNIT

    class Copies:
        def __init__(self, n):
            self.n = n

        def whole(self):
            first = pl.multiple_of(self.n * UNIT, UNIT)
            return pltpu.make_async_copy(grads.at[self.n], grads_out.at[pl.ds(first, UNIT)], grad_sem.at[self.n])

        def piece(self, q):
            u = self.n - plain
            at = 4 * lax.div(u, 2) + q
            row = pl.multiple_of(lax.div(at, 3) * TILE + lax.rem(u, 2) * UNIT, UNIT)
            return pltpu.make_async_copy(
                grads.at[self.n, :, q * width : (q + 1) * width],
                qkv_out.at[lax.rem(at, 3), pl.ds(row, UNIT)],
                grad_sem.at[self.n],
            )

        def start(self):
            pl.when(self.n < plain)(lambda: self.whole().start())

            @pl.when(self.n >= plain)
            def _():
                for q in range(4):
                    self.piece(q).start()

        def wait(self):
            pl.when(self.n < plain)(lambda: self.whole().wait())

            @pl.when(self.n >= plain)
            def _():
                for q in range(4):
                    self.piece(q).wait()

    def begin(n):
        place = lax.rem(lax.div(n, 2), SLOTS // 2)
        code = 4 * lax.rem(n, 2) + middle

        @pl.when(code < 4)
        def _():
            theirs = grads.at[n, pl.ds(rows_of(1 - along_x, half), half)]
            hop(n, 0, theirs, recv_a.at[place, pl.ds(0, half)], across).start()

        @pl.when(code == 4)
        def _():
            hop(n, 0, grads.at[n], recv_b.at[place, pl.ds(0, UNIT)], inward).start()

    def advance(n, stage):
        kind = jnp.where(n < 0, 2, jnp.where(n >= units, 2, lax.rem(n, 2)))
        code = 4 * kind + middle
        place = lax.rem(lax.div(n, 2), SLOTS // 2)

        def case(number):
            return pl.when(code == number)

        base, box = grads.at[n], recv_a.at[place]
        mine_at, theirs_at = rows_of(along_x, half), rows_of(1 - along_x, half)
        own_at = pl.multiple_of(along_x * half + side * quarter, quarter)
        other_at = pl.multiple_of(along_x * half + (1 - side) * quarter, quarter)
        own_in, other_in = rows_of(side, quarter), rows_of(1 - side, quarter)

        def rows(first, size):
            return base.at[pl.ds(first, size)]

        def x_one():
            return hop(n, 0, rows(theirs_at, half), box.at[pl.ds(0, half)], across)

        def z_one():
            return hop(n, 1, rows(mine_at, half), box.at[pl.ds(half, half)], inward)

        def z_two():
            return hop(n, 2, rows(other_at, quarter), box.at[pl.ds(2 * half, quarter)], inward)

        def z_swap():
            return hop(n, 3, rows(own_at, quarter), box.at[pl.ds(swap_at, quarter)], inward)

        def out(kind, first, place_in):
            return hop(n, kind, rows(first, quarter), box.at[pl.ds(half + place_in, quarter)], outward)

        def x_two():
            return hop(n, 6, rows(mine_at, half), box.at[pl.ds(last_at, half)], across)

        swap_at, last_at = 2 * half + quarter, 3 * half

        if stage == 1:

            @case(0)
            def _():
                x_one().wait_recv()
                add_parts(base, mine_at, half, [(box, 0)])
                z_one().start()

        if stage == 2:

            @case(2)
            def _():
                x_one().wait_recv()
                z_one().wait_recv()
                add_parts(base, other_at, quarter, [(box, other_in), (box, half + other_in)])
                z_two().start()

        if stage == 3:

            @case(2)
            def _():
                z_two().wait_recv()
                add_parts(base, own_at, quarter, [(box, own_in), (box, half + own_in), (box, 2 * half)])
                z_swap().start()
                out(4, own_at, own_in).start()

        if stage == 4:

            @case(2)
            def _():
                z_swap().wait_recv()
                z_two().wait_send()
                bring(base, other_at, box, swap_at, quarter)
                out(5, other_at, other_in).start()
                x_two().start()

        if stage == 5:

            @case(0)
            def _():
                z_one().wait_send()
                out(4, own_at, own_in).wait_recv()
                out(5, other_at, other_in).wait_recv()
                bring(base, mine_at, box, half, half)
                x_two().start()

        if stage == 6:

            @case(2)
            def _():
                z_swap().wait_send()
                out(4, own_at, own_in).wait_send()
                out(5, other_at, other_in).wait_send()

            @pl.when(kind == 0)
            def _():
                x_one().wait_send()
                x_two().wait()
                bring(base, theirs_at, box, last_at, half)

        box_b = recv_b.at[place]
        mine_z, theirs_z = rows_of(side, half), rows_of(1 - side, half)
        own_x = pl.multiple_of(side * half + along_x * quarter, quarter)
        other_x = pl.multiple_of(side * half + (1 - along_x) * quarter, quarter)
        own_part_at, other_part_at = rows_of(along_x, quarter), rows_of(1 - along_x, quarter)

        def z_in():
            return hop(n, 0, base, box_b.at[pl.ds(0, UNIT)], inward)

        def z_mid():
            return hop(n, 1, rows(theirs_z, half), box_b.at[pl.ds(UNIT, half)], inward)

        def x_mid():
            return hop(n, 2, rows(other_x, quarter), box_b.at[pl.ds(UNIT + half, quarter)], across)

        def x_swap():
            return hop(n, 3, rows(own_x, quarter), box_b.at[pl.ds(swap_at, quarter)], across)

        def z_share():
            return hop(n, 4, rows(mine_z, half), box_b.at[pl.ds(last_at, half)], inward)

        def z_out(kind, first):
            return hop(n, kind, rows(first, half), box_b.at[pl.ds(first, half)], outward)

        swap_at, last_at = UNIT + half + quarter, 2 * UNIT

        if stage == 1:

            @case(6)
            def _():
                z_in().wait_recv()
                add_parts(base, theirs_z, half, [(box_b, theirs_z)])
                z_mid().start()

        if stage == 2:

            @case(6)
            def _():
                z_mid().wait_recv()
                add_parts(base, other_x, quarter, [(box_b, other_x), (box_b, UNIT + other_part_at)])
                x_mid().start()

        if stage == 3:

            @case(6)
            def _():
                x_mid().wait_recv()
                add_parts(
                    base, own_x, quarter, [(box_b, own_x), (box_b, UNIT + own_part_at), (box_b, UNIT + half)]
                )
                x_swap().start()

        if stage == 4:

            @case(6)
            def _():
                x_swap().wait_recv()
                x_mid().wait_send()
                bring(base, other_x, box_b, swap_at, quarter)
                z_share().start()
                z_out(5, mine_z).start()

        if stage == 5:

            @case(6)
            def _():
                z_share().wait_recv()
                z_mid().wait_send()
                bring(base, theirs_z, box_b, last_at, half)
                z_out(6, theirs_z).start()

        if stage == 6:

            @case(6)
            def _():
                x_swap().wait_send()
                z_share().wait_send()
                z_out(5, mine_z).wait_send()
                z_out(6, theirs_z).wait_send()

            @case(4)
            def _():
                z_in().wait_send()
                z_out(5, mine_z).wait_recv()
                z_out(6, theirs_z).wait_recv()
                bring(base, 0, box_b, 0, UNIT)

            pl.when(kind < 2)(lambda: Copies(n).start())

    def ready(first, count):
        for n in (first + k for k in range(count)):
            if reduce_dp:
                pl.when(n < SLOTS)(functools.partial(begin, n))
            else:
                Copies(n).start()

    def tick(t):
        if not reduce_dp:
            return
        for stage in (6, 5, 4, 3, 2, 1):
            advance(t - 2 * (stage - 1), stage)
        later = t + 2

        @pl.when(jnp.where(later < SLOTS, 0, jnp.where(later >= units, 0, 1)) == 1)
        def _():
            begin(later)

    def tick_at(j, every, first):
        @pl.when(lax.rem(j, every) == every - 1)
        def _():
            tick(first + lax.div(j, every))

    ticks = units + 10

    def to_mate(which, number):
        return pltpu.make_async_remote_copy(
            src_ref=rs_out.at[lax.rem(number, 2)],
            dst_ref=rs_in.at[number],
            send_sem=rs_send.at[which, number],
            recv_sem=rs_recv.at[which, number],
            device_id={"tensor": mate},
            device_id_type=MESH,
        )

    def to_peer(which, number):
        return pltpu.make_async_remote_copy(
            src_ref=rs_in.at[number],
            dst_ref=y_in.at[number],
            send_sem=rs_send.at[which, 4 + number],
            recv_sem=rs_recv.at[which, 4 + number],
            device_id={"tensor": peer},
            device_id_type=MESH,
        )

    def scatter(j, which, compute):
        owner = jnp.where(j < 2, cross, jnp.where(j < 4, peer, mate))
        number = lax.rem(j, 2)
        compute(pl.multiple_of(owner * rows_own + number * TILE, TILE))

        @pl.when(lax.div(j, 2) != 1)
        def _():
            at = jnp.where(j < 2, j, j - 2)
            pl.when(j >= 4)(lambda: to_mate(which, number).wait_send())
            rs_out[number] = temp[0].astype(BF)
            to_mate(which, at).start()

        @pl.when(lax.div(j, 2) == 1)
        def _():
            to_mate(which, number).wait_recv()
            add_into_wide(rs_in.at[number])
            to_peer(which, number).start()

    def add_into_wide(target):
        def step(i, carry):
            at = pl.ds(pl.multiple_of(i * SUB, SUB), SUB)
            target[at, :] = (target[at, :].astype(F32) + temp[0, at, :]).astype(BF)
            return carry

        lax.fori_loop(0, TILE // SUB, step, 0)

    def gathered(which, number):
        to_mate(which, 2 + number).wait_recv()
        to_peer(which, number).wait_recv()

    def settle(which):
        for number in range(2):
            to_mate(which, 2 + number).wait_send()
            to_peer(which, number).wait_send()

    def stored(number, target):
        return pltpu.make_async_copy(rs_out.at[number], target, result_sem.at[number])

    for piece in range(2):
        g_cot.forward(cross, piece).wait_recv()
    g_cot.to_mate(mate).wait_recv()
    g_cot.local().wait()

    def keep_unit(n, value):
        for k in range(value.shape[0] // UNIT):
            grads[n + k] = value[k * UNIT : (k + 1) * UNIT]
        ready(n, value.shape[0] // UNIT)

    per_tile = TILE // UNIT
    first_out = hid.shape[1] // UNIT
    first_up = first_out + width // UNIT

    def down(j, carry):
        at = pl.ds(pl.multiple_of(j * TILE, TILE), TILE)
        keep_unit(per_tile * j, dot(hid[:, at], cot[...], TN).astype(BF))
        return carry

    with jax.named_scope("grad_down"):
        lax.fori_loop(0, hid.shape[1] // TILE, down, 0)
    keep_unit(first_out, dot(mixed[...], cot[...], TN).astype(BF))

    def branch(row0):
        here = pl.ds(row0, TILE)
        temp[0] = dot(mixed[here, :], w_out[...]) + dot(hid[here, :], w_down[...])

    def own_copy(number, back=False):
        held = own_part.at[pl.ds(pl.multiple_of(number * TILE, TILE), TILE)]
        return pltpu.make_async_copy(*((held, temp.at[0]) if back else (temp.at[0], held)), temp_sem.at[0])

    def produce(j, carry):
        @pl.when(j < 6)
        def _():
            scatter(j, 0, branch)

        @pl.when(j >= 6)
        def _():
            branch(pl.multiple_of(me * rows_own + (j - 6) * TILE, TILE))
            own_copy(j - 6).start()
            own_copy(j - 6).wait()

        tick_at(j, 4, 0)
        return carry

    with jax.named_scope("outputs"):
        lax.fori_loop(0, 8, produce, 0)

    def finish(number, carry):
        row0 = pl.multiple_of(me * rows_own + number * TILE, TILE)
        own_copy(number, True).start()
        own_copy(number, True).wait()
        gathered(0, number)

        def step(i, inner):
            at = pl.ds(pl.multiple_of(i * SUB, SUB), SUB)
            total = temp[0, at, :] + rs_in[2 + number, at, :].astype(F32) + y_in[number, at, :].astype(F32)
            total = total + tok[pl.ds(pl.multiple_of(row0 + i * SUB, SUB), SUB), :].astype(F32)
            rs_out[number, at, :] = total.astype(BF)
            return inner

        lax.fori_loop(0, TILE // SUB, step, 0)
        stored(number, mixed_out.at[pl.ds(pl.multiple_of(number * TILE, TILE), TILE)]).start()
        return carry

    def slope(j):
        here = pl.ds(pl.multiple_of(j * TILE, TILE), TILE)
        return pltpu.make_async_copy(slopes.at[here], temp.at[lax.rem(j, 2)], temp_sem.at[lax.rem(j, 2)])

    def descend(j, carry):
        here = pl.ds(pl.multiple_of(j * TILE, TILE), TILE)
        slope(j).wait()
        pl.when(j + 1 < rows // TILE)(lambda: slope(j + 1).start())
        for at in range(0, hid.shape[1], TILE):
            d_hidden = dot(cot[here, :], w_down[at : at + TILE, :], NT)
            hid[here, at : at + TILE] = (d_hidden * temp[lax.rem(j, 2), :, at : at + TILE]).astype(BF)
        tick_at(j, 4, 2)
        return carry

    with jax.named_scope("grad_gelu"):
        slope(0).start()
        lax.fori_loop(0, rows // TILE, descend, 0)

    def upward(j, carry):
        at = pl.ds(pl.multiple_of(j * TILE, TILE), TILE)
        keep_unit(first_up + per_tile * j, dot(n_two[:, at], hid[...], TN).astype(BF))
        tick_at(j, 2, 4)
        return carry

    with jax.named_scope("grad_up"):
        lax.fori_loop(0, n_two.shape[1] // TILE, upward, 0)

    state[...] = jnp.zeros_like(state)
    krow[...] = jnp.zeros_like(krow)
    feat_sums[...] = jnp.zeros_like(feat_sums)

    def unmix(step, carry):
        i = chunks - 1 - step
        diag = diag_two[0:width, :].astype(F32)
        row0 = pl.multiple_of(i * CHUNK, CHUNK)
        here = pl.ds(row0, CHUNK)
        query, key, value = (fqkv[here, s * width : (s + 1) * width] for s in range(3))
        attended, packed = att[here, :], rden[here, :]
        inverse = wide([packed[:, h // 2 * HEAD_DIM // 2 : (h // 2 + 1) * HEAD_DIM // 2] for h in range(2 * heads)])
        d_over = dot(cot[here, :], w_out[...], NT) * inverse
        high, low = split(d_over * attended)
        d_under = -dot(wide([high, low]), diag_two[...])
        over_high, over_low = split(d_over)
        both = wide([wide(per_head(over_high), 0), wide(per_head(over_low), 0)])
        stacked = dot(both, wide([value, value]), NT)
        heads_high, heads_low = [], []
        for h in range(heads):
            d_scores = stacked[h * CHUNK : (h + 1) * CHUNK] + d_under[:, h * HEAD_DIM : h * HEAD_DIM + 1]
            high, low = split(d_scores * causal)
            heads_high.append(high)
            heads_low.append(low)
        query_heads = wide(per_head(query), 0)
        key_heads = wide(per_head(key), 0)
        over_both = wide([over_high, over_low])
        d_query = dot(wide(heads_high + heads_low), wide([key_heads, key_heads], 0))
        d_key = dot(wide(heads_high + heads_low, 0), wide([query_heads, query_heads], 0), TN)
        stacked = dot(query_heads, key, NT)
        scores = [(stacked[h * CHUNK : (h + 1) * CHUNK] * causal).astype(BF) for h in range(heads)]
        d_value = dot(wide(scores, 0), both, TN)
        d_value = d_value[:, :width] + d_value[:, width:]
        later, later_row = state[...], krow[0:1, :]
        more_query, more_key, more_value = [], [], []
        parts = list(zip(*map(halves, (query, key, value, over_both, over_high, over_low, d_under))))
        for k in reversed(range(len(parts))):
            query_k, key_k, value_k, both_k, high_k, low_k, under_k = parts[k]
            carried = wide([states[2 * i + k]] * heads, 0) * diag_two[0:width, :]
            row = ksums[2 * i + k][0:1, :]
            more_query.insert(0, dot(both_k, wide([carried, carried]), NT) + under_k * row)
            keep = joined(2 * i + k + 1)
            later_high, later_low = split(later * keep)
            more_key.insert(0, dot(wide([value_k, value_k]), wide([later_high, later_low]), NT) + later_row * keep)
            more_value.insert(0, dot(wide([key_k, key_k]), wide([later_high, later_low], 0)))
            add = dot(wide([query_k, query_k], 0), wide([high_k, low_k], 0), TN)
            later = later * keep + add * diag
            later_row = later_row * keep + jnp.sum(query_k.astype(F32) * under_k, 0, keepdims=True)
        state[...] = later
        krow[0:1, :] = later_row
        d_query = d_query + wide(more_query, 0)
        d_key = d_key + wide(more_key, 0)
        d_value = d_value + wide(more_value, 0)
        turn = rotation(row0, CHUNK // BLOCK)
        for s, grad in enumerate((d_query, d_key)):
            spectrum = spec[s, here, :]
            grad = grad * (weight_row * jnp.exp(scale_row * spectrum))
            feat_sums[0:1, :] += jnp.sum(grad * spectrum, 0, keepdims=True)
            feat_sums[1:2, :] += jnp.sum(grad, 0, keepdims=True)
            high, low = split(grad * scale_row)
            turned = dot(high, dct[:, 0:width]) + dot(low, dct[:, 0:width]) + dot(high, dct[:, 2 * width :])
            fqkv[here, s * width : (s + 1) * width] = rotate(turned, turn, True).astype(BF)
        fqkv[here, 2 * width : 3 * width] = d_value.astype(BF)

        tick_at(step, 2, 6)
        return carry

    with jax.named_scope("mixer_back"):
        lax.fori_loop(0, chunks, unmix, 0)

    for j in range(n_one.shape[1] // TILE):
        tile = dot(n_one[:, j * TILE : (j + 1) * TILE], fqkv[...], TN).astype(BF)
        for s in range(3):
            at = 3 * j + s
            for k in range(per_tile):
                grads[plain + at // 4 * per_tile + k, :, at % 4 * width : (at % 4 + 1) * width] = tile[
                    k * UNIT : (k + 1) * UNIT, s * width : (s + 1) * width
                ]
        if j:
            ready(plain + (j - 1) * per_tile, per_tile)

    def pause(t, carry):
        tick(t)
        return carry

    lax.fori_loop(14, 16, pause, 0)

    sums[...] = jnp.zeros_like(sums)

    def row_grads(row0):
        here = pl.ds(row0, TILE)
        total = dot(fqkv[here, 0:width], w_qkv[0], NT)
        for s in (1, 2):
            total = total + dot(fqkv[here, s * width : (s + 1) * width], w_qkv[s], NT)
        temp[0] = total
        temp[1] = dot(hid[here, :], w_up[...], NT)

        def fold(i, inner):
            at = pl.ds(pl.multiple_of(i * SUB, SUB), SUB)
            unit, _ = centered(pl.multiple_of(row0 + i * SUB, SUB), SUB)
            one, two = temp[0, at, :], temp[1, at, :]
            for number, term in enumerate((one * unit, one, two * unit, two)):
                sums[number] += jnp.sum(term.reshape(SUB // 8, 8, term.shape[1]), 0)
            temp[0, at, :] = one * gain_one + two * gain_two
            return inner

        lax.fori_loop(0, TILE // SUB, fold, 0)

    with jax.named_scope("finish"):
        settle(0)
        lax.fori_loop(0, 2, finish, 0)
    for number in range(2):
        stored(number, mixed_out.at[pl.ds(0, TILE)]).wait()
    pl.semaphore_signal(free_mate, inc=1, device_id={"tensor": mate}, device_id_type=MESH)
    pl.semaphore_signal(free_peer, inc=1, device_id={"tensor": peer}, device_id_type=MESH)
    pl.semaphore_wait(free_mate, 1)
    pl.semaphore_wait(free_peer, 1)

    def inputs(j, carry):
        scatter(j, 1, row_grads)
        tick(16 + j)
        return carry

    with jax.named_scope("row_grads"):
        lax.fori_loop(0, 6, inputs, 0)
    settle(1)

    def conclude(number, carry):
        row0 = pl.multiple_of(me * rows_own + number * TILE, TILE)
        row_grads(row0)
        gathered(1, number)

        def step(i, inner):
            at = pl.ds(pl.multiple_of(i * SUB, SUB), SUB)
            group_at = pl.multiple_of(row0 + i * SUB, SUB)
            unit, deviation = centered(group_at, SUB)
            total = temp[0, at, :] + rs_in[2 + number, at, :].astype(F32) + y_in[number, at, :].astype(F32)
            along = jnp.mean(total * unit, -1, keepdims=True)
            total = total - jnp.mean(total, -1, keepdims=True) - unit * along
            total = cot[pl.ds(group_at, SUB), :].astype(F32) + deviation * total
            rs_out[number, at, :] = total.astype(BF)
            return inner

        lax.fori_loop(0, TILE // SUB, step, 0)
        stored(number, input_grad.at[pl.ds(pl.multiple_of(number * TILE, TILE), TILE)]).start()
        tick(22 + number)
        return carry

    with jax.named_scope("conclude"):
        lax.fori_loop(0, 2, conclude, 0)

    small[...] = jnp.zeros_like(small)
    for number in range(4):
        small[number : number + 1, :] = jnp.sum(sums[number], 0, keepdims=True)
    small[4:5, 0:width] = feat_sums[0:1, :]
    small[5:6, 0:width] = feat_sums[1:2, :] / weight_row

    def small_hop(number, device, count=8):
        return pltpu.make_async_remote_copy(
            src_ref=small,
            dst_ref=small_in.at[number],
            send_sem=small_send.at[number],
            recv_sem=small_recv.at[number],
            device_id=device,
            device_id_type=MESH,
        )

    row_number = lax.broadcasted_iota(jnp.int32, small.shape, 0)
    over_tensor = jnp.where(row_number < 4, 1.0, 0.0).astype(F32)
    to_both = [small_hop(0, {"tensor": mate}), small_hop(1, {"tensor": peer}), small_hop(2, {"dp": across})]
    inner, centre, outer = small_hop(3, {"dp": inward}), small_hop(4, {"dp": inward}), small_hop(5, {"dp": outward})

    def add_small(number):
        to_both[number].wait()
        small[...] += small_in[number] * over_tensor if number < 2 else small_in[number]

    def small_step(k):
        if k < 3:
            if k:
                add_small(k - 1)
            if k < 2 or reduce_dp:
                to_both[k].start()
        if not reduce_dp:
            return
        if k == 3:
            add_small(2)
            at_end(inner.start)
        if k == 4:

            @at_mid
            def _():
                inner.wait_recv()
                small[...] += small_in[3]
                centre.start()

        if k == 5:

            @at_mid
            def _():
                centre.wait()
                small[...] += small_in[4]
                outer.start()

        if k == 6:
            at_mid(outer.wait_send)

            @at_end
            def _():
                inner.wait_send()
                outer.wait_recv()
                small[...] = small_in[5]

    if reduce_dp:

        def rest(t, carry):
            for k in range(7):
                pl.when(t == 24 + k)(functools.partial(small_step, k))
            tick(t)
            return carry

        lax.fori_loop(24, ticks, rest, 0)
    else:
        for k in range(3):
            small_step(k)
    for h in range(heads):
        at = slice(h * HEAD_DIM, (h + 1) * HEAD_DIM)
        feat_out[0, h : h + 1, :] = small[4:5, at]
        feat_out[1, h : h + 1, :] = small[5:6, at]

    def copied(n, carry):
        Copies(n).wait()
        return carry

    lax.fori_loop(0, units, copied, 0)
    for number in range(2):
        stored(number, input_grad.at[pl.ds(0, TILE)]).wait()

    for gather in (g_tok, g_cot):
        gather.to_mate(me).wait_send()
        for piece in range(2):
            gather.to_peer(me, piece).wait_send()
            gather.forward(peer, piece).wait_send()


def shards(
    reduce_dp,
    tokens,
    ln1_gain,
    ln1_bias,
    ln2_gain,
    ln2_bias,
    w_qkv,
    w_out,
    w_up,
    w_down,
    feature_scale,
    feature_weight,
    lengths,
    cotangent,
):
    rows_own, model = tokens.shape
    rows = 4 * rows_own
    heads = feature_scale.shape[0]
    width = heads * HEAD_DIM
    hidden = w_up.shape[1]
    consts = tables(rows // BLOCK, heads)
    norms = [value.reshape(1, model) for value in (ln1_gain, ln1_bias, ln2_gain, ln2_bias)]
    anywhere = pl.BlockSpec(memory_space=pl.ANY)
    vmem = pl.BlockSpec(memory_space=pltpu.VMEM)
    smem = pl.BlockSpec(memory_space=pltpu.SMEM)
    shape = jax.ShapeDtypeStruct
    plain = 2 * hidden + width
    units = (plain + 3 * width) // UNIT
    mixed_out, input_grad, grads, g_qkv, _, _, small, feats = pl.pallas_call(
        functools.partial(kernel, reduce_dp),
        out_shape=(
            shape((rows_own, model), BF),
            shape((rows_own, model), BF),
            shape((plain, model), BF),
            shape((3, model, width), BF),
            shape((rows, hidden), F32),
            shape((rows_own, model), F32),
            shape((8, model), F32),
            shape((2, heads, HEAD_DIM), F32),
        ),
        in_specs=[smem, anywhere, anywhere] + [vmem] * 14,
        out_specs=(anywhere,) * 6 + (vmem, vmem),
        scratch_shapes=[
            pltpu.VMEM((rows, model), BF),
            pltpu.VMEM((rows, model), BF),
            pltpu.VMEM((rows, model), BF),
            pltpu.VMEM((rows, model), BF),
            pltpu.VMEM((rows, hidden), BF),
            pltpu.VMEM((rows, 3 * width), BF),
            pltpu.VMEM((2, rows, width), F32),
            pltpu.VMEM((rows, width), BF),
            pltpu.VMEM((rows, width), F32),
            pltpu.VMEM((rows, width // 2), F32),
            pltpu.VMEM((rows // BLOCK, HEAD_DIM, width), BF),
            pltpu.VMEM((rows // BLOCK, 8, width), F32),
            pltpu.VMEM((width, width), F32),
            pltpu.VMEM((8, width), F32),
            pltpu.VMEM((units, UNIT, model), BF),
            pltpu.VMEM((SLOTS // 2, 2 * UNIT, model), BF),
            pltpu.VMEM((SLOTS // 2, 5 * UNIT // 2, model), BF),
            pltpu.VMEM((2, TILE, model), BF),
            pltpu.VMEM((4, TILE, model), BF),
            pltpu.VMEM((2, TILE, model), BF),
            pltpu.VMEM((2, TILE, model), F32),
            pltpu.VMEM((4, 8, model), F32),
            pltpu.VMEM((8, width), F32),
            pltpu.VMEM((6, 8, model), F32),
            pltpu.SemaphoreType.DMA((10,)),
            pltpu.SemaphoreType.DMA((10,)),
            pltpu.SemaphoreType.DMA((10,)),
            pltpu.SemaphoreType.DMA((units, 7)),
            pltpu.SemaphoreType.DMA((units, 7)),
            pltpu.SemaphoreType.DMA((2, 6)),
            pltpu.SemaphoreType.DMA((2, 6)),
            pltpu.SemaphoreType.DMA((6,)),
            pltpu.SemaphoreType.DMA((6,)),
            pltpu.SemaphoreType.DMA((units,)),
            pltpu.SemaphoreType.DMA((2,)),
            pltpu.SemaphoreType.DMA((2,)),
            pltpu.SemaphoreType.REGULAR,
            pltpu.SemaphoreType.REGULAR,
        ],
        compiler_params=pltpu.CompilerParams(
            collective_id=0, has_side_effects=True, vmem_limit_bytes=62 * 2**20
        ),
    )(lengths, tokens, cotangent, *norms, w_qkv, w_out, w_up, w_down, feature_scale, feature_weight, *consts)
    norm_sums = small[0:4]
    if not reduce_dp:
        grads, g_qkv, norm_sums, feats = lax.psum(
            (*lax.optimization_barrier((grads.astype(F32), g_qkv.astype(F32))), norm_sums, feats), "dp"
        )
    g_down, g_out, g_up = (
        grads[first:last].astype(F32)
        for first, last in ((0, hidden), (hidden, hidden + width), (hidden + width, plain))
    )
    g_qkv = g_qkv.astype(F32)
    return (
        mixed_out,
        input_grad,
        norm_sums[0],
        norm_sums[1],
        norm_sums[2],
        norm_sums[3],
        g_qkv,
        g_out,
        g_up,
        g_down,
        feats[0],
        feats[1],
    )


def solution(mesh):
    placed = (
        P(("dp", "tensor"), None),
        P(),
        P(),
        P(),
        P(),
        P(None, None, "tensor"),
        P("tensor", None),
        P(None, "tensor"),
        P("tensor", None),
        P("tensor", None),
        P("tensor", None),
        P("dp", None),
        P(("dp", "tensor"), None),
    )
    return jax.shard_map(
        functools.partial(shards, mesh.shape["dp"] == 8),
        mesh=mesh,
        in_specs=placed,
        out_specs=(
            P(("dp", "tensor"), None),
            P(("dp", "tensor"), None),
            P(),
            P(),
            P(),
            P(),
            P(None, None, "tensor"),
            P("tensor", None),
            P(None, "tensor"),
            P("tensor", None),
            P("tensor", None),
            P("tensor", None),
        ),
        check_vma=False,
    )
```

```python
import functools
import math

import jax
import jax.numpy as jnp
import ml_dtypes
import numpy as np
from jax import lax
from jax.experimental import pallas as pl
from jax.experimental.pallas import tpu as pltpu
from jax.sharding import PartitionSpec as P

HEAD_DIM = 64
ROT = 16
BLOCK = 64
CHUNK = 128
TILE = 256
UNIT = 128
SUB = 32
SLOTS = 12
MESH = pl.DeviceIdType.MESH
F32 = jnp.float32
BF = jnp.bfloat16
NN = (((1,), (0,)), ((), ()))
NT = (((1,), (1,)), ((), ()))
TN = (((0,), (0,)), ((), ()))


def dot(left, right, dims=NN):
    return lax.dot_general(left, right, dims, preferred_element_type=F32)


def split(value):
    high = value.astype(BF)
    return high, (value - high.astype(F32)).astype(BF)


def wide(parts, axis=1):
    return jnp.concatenate(parts, axis)


def tables(blocks, heads):
    width = heads * HEAD_DIM
    freq, dims = np.arange(HEAD_DIM)[:, None], np.arange(HEAD_DIM)[None, :]
    dct = np.cos(np.pi * (dims + 0.5) * freq / HEAD_DIM) * math.sqrt(2.0 / HEAD_DIM)
    dct[0] *= math.sqrt(0.5)
    dct = np.kron(np.eye(heads), dct).astype(np.float32)
    high = dct.astype(ml_dtypes.bfloat16)
    low = (dct - high.astype(np.float32)).astype(ml_dtypes.bfloat16)
    halves = np.concatenate([high, high, low], 1)
    half = ROT // 2
    lane = np.arange(2 * HEAD_DIM) % HEAD_DIM
    rate = np.where(lane < ROT, 10000.0 ** (-(lane % half) * 2.0 / ROT), 0.0)
    in_block = np.arange(BLOCK)[:, None] * rate[None]
    of_block = np.arange(blocks)[:, None] * BLOCK * rate[None]
    signs = np.stack([np.where(lane < half, -1.0, 0.0), np.where((lane >= half) & (lane < ROT), 1.0, 0.0)] + [0.0 * lane] * 6)
    angles = np.concatenate([np.cos(in_block), np.sin(in_block), np.cos(of_block), np.sin(of_block), signs], 0)
    diagonal = np.kron(np.eye(heads), np.ones((HEAD_DIM, HEAD_DIM)))
    masks = np.kron(np.eye(heads), np.ones((CHUNK, HEAD_DIM)))
    return (
        halves,
        angles.astype(np.float32),
        np.concatenate([diagonal, diagonal], 0).astype(ml_dtypes.bfloat16),
        masks.astype(ml_dtypes.bfloat16),
    )


def kernel(
    reduce_dp,
    lengths,
    tok_in,
    cot_in,
    gain_one_in,
    bias_one_in,
    gain_two_in,
    bias_two_in,
    w_qkv_in,
    w_out_in,
    w_up_in,
    w_down_in,
    feature_scale,
    feature_weight,
    dct,
    angles,
    diag_two,
    masks,
    mixed_out,
    input_grad,
    grads_out,
    qkv_out,
    slopes,
    own_part,
    tok_kept,
    small,
    feat_out,
    tok_tile,
    cot,
    n_one,
    n_two,
    hid,
    fqkv,
    spec,
    mixed,
    att,
    rden,
    states,
    ksums,
    state,
    krow,
    grads,
    recv_a,
    recv_b,
    rs_out,
    rs_in,
    y_in,
    temp,
    sums,
    feat_sums,
    small_in,
    small_wide,
    w_qkv,
    w_out,
    w_up,
    w_down,
    local_sem,
    send_sem,
    recv_sem,
    weight_sem,
    ar_send,
    ar_recv,
    rs_send,
    rs_recv,
    small_send,
    small_recv,
    grad_sem,
    temp_sem,
    tok_sem,
    result_sem,
    free_mate,
    free_peer,
):
    rows_own = tok_in.shape[0]
    rows = cot.shape[0]
    tok = grads
    width = w_out_in.shape[0]
    heads = width // HEAD_DIM
    chunks = rows // CHUNK
    me = lax.axis_index("tensor")
    core = lax.rem(me, 2)
    mate = me + 1 - 2 * core
    peer = lax.rem(me + 2, 4)
    cross = 3 - me
    group = lax.axis_index("dp")
    along_x = lax.rem(group, 2)
    across = group + 1 - 2 * along_x
    along_z = lax.div(group, 2)
    middle = along_z * (3 - along_z)

    def at_end(step):
        pl.when(middle == 0)(step)

    def at_mid(step):
        pl.when(middle > 0)(step)

    side = jnp.where(along_z < 2, 0, 1)
    inward = group + 2 - 4 * side
    outward = group - 2 + 4 * side
    units = grads.shape[0] // UNIT

    weight_copies = [
        pltpu.make_async_copy(source, target, weight_sem.at[k])
        for k, (source, target) in enumerate(
            ((w_qkv_in, w_qkv), (w_up_in, w_up), (w_out_in, w_out), (w_down_in, w_down))
        )
    ]
    for copy in weight_copies:
        copy.start()

    barrier = pltpu.get_barrier_semaphore()
    members = 8 if reduce_dp else 1
    for step in range(1, 4):
        other = lax.rem(me + step, 4)
        pl.semaphore_signal(barrier, inc=1, device_id={"tensor": other}, device_id_type=MESH)
    for step in range(1, members):
        other = lax.rem(group + step, members)
        pl.semaphore_signal(barrier, inc=1, device_id={"dp": other}, device_id_type=MESH)
    pl.semaphore_wait(barrier, 2 + members)

    def slot(buf, owner, piece=None, columns=False):
        if piece is None:
            return buf.at[pl.ds(pl.multiple_of(owner * rows_own, rows_own), rows_own)]
        if columns:
            here = pl.ds(pl.multiple_of(owner * rows_own, rows_own), rows_own)
            return buf.at[here, piece * TILE : (piece + 1) * TILE]
        return buf.at[pl.ds(pl.multiple_of(owner * rows_own + piece * UNIT, UNIT), UNIT)]

    class Gather:
        def __init__(self, source, buf, base, columns):
            self.source, self.buf, self.base, self.columns = source, buf, base, columns
            self.pieces = source.shape[1] // TILE if columns else source.shape[0] // UNIT

        def copy(self, number, src, dst, target):
            return pltpu.make_async_remote_copy(
                src_ref=src,
                dst_ref=dst,
                send_sem=send_sem.at[self.base + number],
                recv_sem=recv_sem.at[self.base + number],
                device_id={"tensor": target},
                device_id_type=MESH,
            )

        def local(self):
            return pltpu.make_async_copy(self.source, slot(self.buf, me), local_sem.at[self.base])

        def to_mate(self, owner):
            return self.copy(0, self.source, slot(self.buf, owner), mate)

        def to_peer(self, owner, piece):
            if self.columns:
                part = self.source.at[:, piece * TILE : (piece + 1) * TILE]
            else:
                part = self.source.at[pl.ds(piece * UNIT, UNIT)]
            return self.copy(1 + piece, part, slot(self.buf, owner, piece, self.columns), peer)

        def forward(self, owner, piece):
            part = slot(self.buf, owner, piece, self.columns)
            return self.copy(1 + self.pieces + piece, part, part, mate)

    g_tok, g_cot = Gather(tok_in, tok, 0, False), Gather(cot_in, cot, 1 + 2 * (rows_own // UNIT), True)
    g_tok.to_mate(me).start()
    for piece in range(g_tok.pieces):
        g_tok.to_peer(me, piece).start()
    g_tok.local().start()
    g_cot.to_mate(me).start()
    g_cot.local().start()

    start_one = lengths[0, 0]
    start_two = start_one + lengths[0, 1]

    def segment(block):
        return (block >= start_one).astype(jnp.int32) + (block >= start_two).astype(jnp.int32)

    def in_sequence(block):
        return block - jnp.where(block >= start_two, start_two, jnp.where(block >= start_one, start_one, 0))

    gain_one, bias_one, gain_two, bias_two = gain_one_in[...], bias_one_in[...], gain_two_in[...], bias_two_in[...]
    scale_row, weight_row = (
        wide([field[h : h + 1, :] for h in range(heads)]) for field in (feature_scale, feature_weight)
    )
    blocks = rows // BLOCK

    def rotation(row0, count):
        cos_in, sin_in = angles[0:BLOCK, :], angles[BLOCK : 2 * BLOCK, :]
        sign_a = angles[2 * BLOCK + 2 * blocks : 2 * BLOCK + 2 * blocks + 1, :]
        sign_b = angles[2 * BLOCK + 2 * blocks + 1 : 2 * BLOCK + 2 * blocks + 2, :]
        cosines, sines = [], []
        for k in range(count):
            place = in_sequence(lax.div(row0, BLOCK) + k)
            cos_at = angles[pl.ds(2 * BLOCK + place, 1), :]
            sin_at = angles[pl.ds(2 * BLOCK + blocks + place, 1), :]
            cosines.append(cos_in * cos_at - sin_in * sin_at)
            sines.append(sin_in * cos_at + cos_in * sin_at)
        cosine, sine = wide(cosines, 0), wide(sines, 0)
        return cosine, sine * sign_a, sine * sign_b

    def rotate(field, turn, back=False):
        cosine, sine_a, sine_b = turn
        parts = []
        for at in range(0, width, 2 * HEAD_DIM):
            part = field[:, at : at + 2 * HEAD_DIM]
            ahead = pltpu.roll(part, 2 * HEAD_DIM - ROT // 2, 1) * sine_a
            behind = pltpu.roll(part, ROT // 2, 1) * sine_b
            parts.append(part * cosine - (ahead + behind) if back else part * cosine + (ahead + behind))
        return wide(parts)

    def centered(source, at, size):
        value = source[pl.ds(at, size), :].astype(F32)
        value = value - jnp.mean(value, -1, keepdims=True)
        deviation = lax.rsqrt(jnp.mean(value * value, -1, keepdims=True) + 1e-05)
        return value * deviation, deviation

    chip_row = pl.multiple_of(lax.div(me, 2) * 2 * rows_own, rows_own)

    def slope_copy(p, back=False):
        held = slopes.at[pl.ds(pl.multiple_of(p * TILE, TILE), TILE)]
        slot_of = temp.at[lax.rem(p, 2)]
        return pltpu.make_async_copy(*((held, slot_of) if back else (slot_of, held)), temp_sem.at[lax.rem(p, 2)])

    def project(j, carry):
        @pl.when(j == 0)
        def _():
            g_tok.local().wait()

            g_cot.local().wait()

        @pl.when(j == 2)
        def _():
            g_tok.to_mate(mate).wait_recv()
            g_cot.to_mate(mate).wait_recv()

        for piece in range(g_tok.pieces):

            @pl.when(j == 4 + piece)
            def _():
                g_tok.to_peer(peer, piece).wait_recv()
                g_tok.forward(peer, piece).start()
                g_cot.to_peer(me, piece).start()
                g_tok.forward(cross, piece).wait_recv()

        late = lax.div(j, 4)
        early_at = jnp.where(j < 2, me, mate) * rows_own + lax.rem(j, 2) * TILE
        row_a = pl.multiple_of(jnp.where(late == 0, early_at, peer * rows_own + (j - 4) * UNIT), UNIT)
        row_b = pl.multiple_of(jnp.where(late == 0, early_at + UNIT, cross * rows_own + (j - 4) * UNIT), UNIT)
        here = [pl.ds(row_a, UNIT), pl.ds(row_b, UNIT)]

        def norm(i, inner):
            for row0 in (row_a, row_b):
                at = pl.multiple_of(row0 + i * SUB, SUB)
                unit, _ = centered(tok, at, SUB)
                n_one[pl.ds(at, SUB), :] = (unit * gain_one + bias_one).astype(BF)
                n_two[pl.ds(at, SUB), :] = (unit * gain_two + bias_two).astype(BF)
            return inner

        lax.fori_loop(0, UNIT // SUB, norm, 0)
        first = wide([n_one[at, :] for at in here], 0)
        turn = [wide(pair, 0) for pair in zip(*(rotation(at, UNIT // BLOCK) for at in (row_a, row_b)))]

        def keep(write, value):
            for k, at in enumerate(here):
                write(at, value[k * UNIT : (k + 1) * UNIT])

        def keep_field(s, value):
            def write(at, part):
                fqkv[at, s * width : (s + 1) * width] = part

            keep(write, value.astype(BF))

        for s in range(2):
            high, low = split(rotate(dot(first, w_qkv[s]), turn))
            spectrum = dot(wide([high, low]), dct[:, 0 : 2 * width], NT) + dot(high, dct[:, 2 * width :], NT)

            def keep_spectrum(at, part):
                spec[s, at, :] = part

            keep(keep_spectrum, spectrum)
            keep_field(s, weight_row * jnp.exp(scale_row * spectrum))
        keep_field(2, dot(first, w_qkv[2]))
        second = wide([n_two[at, :] for at in here], 0)
        parity = lax.rem(j, 2)
        pl.when(j >= 6)(lambda: slope_copy(j - 6).wait())
        for at in range(0, w_up.shape[1], TILE):
            up = dot(second, w_up[:, at : at + TILE])
            below = 0.5 * (1.0 + lax.erf(up * math.sqrt(0.5)))

            def keep_hidden(rows_at, part):
                hid[rows_at, at : at + TILE] = part

            keep(keep_hidden, (up * below).astype(BF))
            temp[parity, :, at : at + TILE] = below + up * (
                jnp.exp(-0.5 * up * up) * (1.0 / math.sqrt(2.0 * math.pi))
            )

        @pl.when(late == 0)
        def _():
            turned = wide([cot[at, :] for at in here], 0)
            first_at = pl.multiple_of(rows + row_a - chip_row, TILE)
            for at in range(0, hid.shape[1], TILE):
                d_hidden = dot(turned, w_down[at : at + TILE, :], NT)
                grads[pl.ds(first_at, TILE), at : at + TILE] = (d_hidden * temp[parity, :, at : at + TILE]).astype(BF)

        pl.when(late == 1)(lambda: slope_copy(j - 4).start())
        return carry

    for copy in weight_copies:
        copy.wait()
    with jax.named_scope("project"):
        lax.fori_loop(0, rows // TILE, project, 0)
    for p in (2, 3):
        slope_copy(p).wait()
    keep_tok = pltpu.make_async_copy(tok.at[pl.ds(0, rows)], tok_kept, tok_sem.at[0])
    keep_tok.start()

    grid_t = lax.broadcasted_iota(jnp.int32, (CHUNK, CHUNK), 0)
    grid_s = lax.broadcasted_iota(jnp.int32, (CHUNK, CHUNK), 1)
    together = (grid_t < BLOCK) == (grid_s < BLOCK)
    causal = wide([jnp.where((grid_t >= grid_s) & together, 1.0, 0.0).astype(F32)] * heads)
    causal_back = wide([jnp.where((grid_t <= grid_s) & together, 1.0, 0.0).astype(F32)] * heads)
    head_rows = jnp.where(
        lax.broadcasted_iota(jnp.int32, (8, width), 0) == lax.div(lax.broadcasted_iota(jnp.int32, (8, width), 1), HEAD_DIM),
        1.0,
        0.0,
    ).astype(BF)
    both_chunks = range(2)
    both_blocks = range(CHUNK // BLOCK)

    def joined(block):
        return jnp.where(segment(block) == segment(block - 1), jnp.float32(1.0), jnp.float32(0.0))

    def per_head(value):
        return wide([value * masks[h * CHUNK : (h + 1) * CHUNK, :] for h in range(heads)], 0)

    def halves(value):
        return [value[k * BLOCK : (k + 1) * BLOCK] for k in both_blocks]

    def chunk_rows(pair):
        return [pl.ds(pl.multiple_of((2 * pair + c) * CHUNK, CHUNK), CHUNK) for c in both_chunks]

    state[...] = jnp.zeros_like(state)
    krow[...] = jnp.zeros_like(krow)

    def mix(pair, carry):
        diag = diag_two[0:width, :].astype(F32)
        here = chunk_rows(pair)
        query, key, value = ([fqkv[at, s * width : (s + 1) * width] for at in here] for s in range(3))
        scores = [split(dot(query[c], per_head(key[c]), NT) * causal) for c in both_chunks]
        turned = [key[c].T for c in both_chunks]
        over = [dot(scores[c][0], per_head(value[c])) for c in both_chunks]
        under = [dot(scores[c][0], masks[...]) + dot(scores[c][1], masks[...]) for c in both_chunks]
        made = [
            dot(turned[c][:, k * BLOCK : (k + 1) * BLOCK], halves(value[c])[k]) * diag
            for c in both_chunks
            for k in both_blocks
        ]
        row_made = [jnp.sum(halves(key[c])[k].astype(F32), 0, keepdims=True) for c in both_chunks for k in both_blocks]
        now, row = state[...], krow[0:1, :]
        carried, rows_in = [], []
        for k in range(4):
            carried.append(now.astype(BF))
            rows_in.append(row)
            states[4 * pair + k] = sum(now[h * HEAD_DIM : (h + 1) * HEAD_DIM] for h in range(heads)).astype(BF)
            ksums[4 * pair + k] = jnp.broadcast_to(row, (8, width))
            keep = joined(4 * pair + k + 1)
            now = (now + made[k]) * keep
            row = (row + row_made[k]) * keep
        state[...] = now
        krow[0:1, :] = row
        for c in both_chunks:
            parts = halves(query[c])
            more = wide([dot(parts[k], carried[2 * c + k]) for k in both_blocks], 0)
            high, low = split(wide([parts[k].astype(F32) * rows_in[2 * c + k] for k in both_blocks], 0))
            inverse = 1.0 / (under[c] + dot(wide([high, low]), diag_two[...]))
            attended = (over[c] + more) * inverse
            att[here[c], :] = attended
            rden[here[c], :] = wide([inverse[:, h * HEAD_DIM : h * HEAD_DIM + HEAD_DIM // 2] for h in range(heads)])
            mixed[here[c], :] = attended.astype(BF)

        return carry

    def add_parts(base, first, count, sources):
        for at in range(0, count, SUB):
            total = base[pl.ds(first + at, SUB), :].astype(F32)
            for source, place in sources:
                total = total + source[pl.ds(place + at, SUB), :].astype(F32)
            base[pl.ds(first + at, SUB), :] = total.astype(BF)

    def bring(base, first, box, place, count):
        base[pl.ds(first, count), :] = box[pl.ds(place, count), :]

    half, quarter = UNIT // 2, UNIT // 4

    def rows_of(index, size):
        return pl.multiple_of(index * size, size)

    def unit_of(n):
        return grads.at[pl.ds(pl.multiple_of(n * UNIT, UNIT), UNIT)]

    def hop(n, kind, source, target, device):
        return pltpu.make_async_remote_copy(
            src_ref=source,
            dst_ref=target,
            send_sem=ar_send.at[n, kind],
            recv_sem=ar_recv.at[n, kind],
            device_id={"dp": device},
            device_id_type=MESH,
        )

    plain = units - 3 * width // UNIT

    class Copies:
        def __init__(self, n):
            self.n = n

        def whole(self):
            first = pl.multiple_of(self.n * UNIT, UNIT)
            return pltpu.make_async_copy(unit_of(self.n), grads_out.at[pl.ds(first, UNIT)], grad_sem.at[self.n])

        def piece(self, q):
            u = self.n - plain
            at = 4 * lax.div(u, 2) + q
            row = pl.multiple_of(lax.div(at, 3) * TILE + lax.rem(u, 2) * UNIT, UNIT)
            return pltpu.make_async_copy(
                unit_of(self.n).at[:, q * width : (q + 1) * width],
                qkv_out.at[lax.rem(at, 3), pl.ds(row, UNIT)],
                grad_sem.at[self.n],
            )

        def start(self):
            pl.when(self.n < plain)(lambda: self.whole().start())

            @pl.when(self.n >= plain)
            def _():
                for q in range(4):
                    self.piece(q).start()

        def wait(self):
            pl.when(self.n < plain)(lambda: self.whole().wait())

            @pl.when(self.n >= plain)
            def _():
                for q in range(4):
                    self.piece(q).wait()

    def begin(n):
        place = lax.rem(lax.div(n, 2), SLOTS // 2)
        code = 4 * lax.rem(n, 2) + middle

        @pl.when(code < 4)
        def _():
            theirs = unit_of(n).at[pl.ds(rows_of(1 - along_x, half), half)]
            hop(n, 0, theirs, recv_a.at[place, pl.ds(0, half)], across).start()

        @pl.when(code == 4)
        def _():
            hop(n, 0, unit_of(n), recv_b.at[place, pl.ds(0, UNIT)], inward).start()

    def advance(n, stage):
        kind = jnp.where(n < 0, 2, jnp.where(n >= units, 2, lax.rem(n, 2)))
        code = 4 * kind + middle
        place = lax.rem(lax.div(n, 2), SLOTS // 2)

        def case(number):
            return pl.when(code == number)

        base, box = unit_of(n), recv_a.at[place]
        mine_at, theirs_at = rows_of(along_x, half), rows_of(1 - along_x, half)
        own_at = pl.multiple_of(along_x * half + side * quarter, quarter)
        other_at = pl.multiple_of(along_x * half + (1 - side) * quarter, quarter)
        own_in, other_in = rows_of(side, quarter), rows_of(1 - side, quarter)

        def rows(first, size):
            return base.at[pl.ds(first, size)]

        def x_one():
            return hop(n, 0, rows(theirs_at, half), box.at[pl.ds(0, half)], across)

        def z_one():
            return hop(n, 1, rows(mine_at, half), box.at[pl.ds(half, half)], inward)

        def z_two():
            return hop(n, 2, rows(other_at, quarter), box.at[pl.ds(2 * half, quarter)], inward)

        def z_swap():
            return hop(n, 3, rows(own_at, quarter), box.at[pl.ds(swap_at, quarter)], inward)

        def out(kind, first, place_in):
            return hop(n, kind, rows(first, quarter), box.at[pl.ds(half + place_in, quarter)], outward)

        def x_two():
            return hop(n, 6, rows(mine_at, half), box.at[pl.ds(last_at, half)], across)

        swap_at, last_at = 2 * half + quarter, 3 * half

        if stage == 1:

            @case(0)
            def _():
                x_one().wait_recv()
                add_parts(base, mine_at, half, [(box, 0)])
                z_one().start()

        if stage == 2:

            @case(2)
            def _():
                x_one().wait_recv()
                z_one().wait_recv()
                add_parts(base, other_at, quarter, [(box, other_in), (box, half + other_in)])
                z_two().start()

        if stage == 3:

            @case(2)
            def _():
                z_two().wait_recv()
                add_parts(base, own_at, quarter, [(box, own_in), (box, half + own_in), (box, 2 * half)])
                z_swap().start()
                out(4, own_at, own_in).start()

        if stage == 4:

            @case(2)
            def _():
                z_swap().wait_recv()
                z_two().wait_send()
                bring(base, other_at, box, swap_at, quarter)
                out(5, other_at, other_in).start()
                x_two().start()

        if stage == 5:

            @case(0)
            def _():
                z_one().wait_send()
                out(4, own_at, own_in).wait_recv()
                out(5, other_at, other_in).wait_recv()
                bring(base, mine_at, box, half, half)
                x_two().start()

        if stage == 6:

            @case(2)
            def _():
                z_swap().wait_send()
                out(4, own_at, own_in).wait_send()
                out(5, other_at, other_in).wait_send()

            @pl.when(kind == 0)
            def _():
                x_one().wait_send()
                x_two().wait()
                bring(base, theirs_at, box, last_at, half)

        box_b = recv_b.at[place]
        mine_z, theirs_z = rows_of(side, half), rows_of(1 - side, half)
        own_x = pl.multiple_of(side * half + along_x * quarter, quarter)
        other_x = pl.multiple_of(side * half + (1 - along_x) * quarter, quarter)
        own_part_at, other_part_at = rows_of(along_x, quarter), rows_of(1 - along_x, quarter)

        def z_in():
            return hop(n, 0, base, box_b.at[pl.ds(0, UNIT)], inward)

        def z_mid():
            return hop(n, 1, rows(theirs_z, half), box_b.at[pl.ds(UNIT, half)], inward)

        def x_mid():
            return hop(n, 2, rows(other_x, quarter), box_b.at[pl.ds(UNIT + half, quarter)], across)

        def x_swap():
            return hop(n, 3, rows(own_x, quarter), box_b.at[pl.ds(swap_at, quarter)], across)

        def z_share():
            return hop(n, 4, rows(mine_z, half), box_b.at[pl.ds(last_at, half)], inward)

        def z_out(kind, first):
            return hop(n, kind, rows(first, half), box_b.at[pl.ds(first, half)], outward)

        swap_at, last_at = UNIT + half + quarter, 2 * UNIT

        if stage == 1:

            @case(6)
            def _():
                z_in().wait_recv()
                add_parts(base, theirs_z, half, [(box_b, theirs_z)])
                z_mid().start()

        if stage == 2:

            @case(6)
            def _():
                z_mid().wait_recv()
                add_parts(base, other_x, quarter, [(box_b, other_x), (box_b, UNIT + other_part_at)])
                x_mid().start()

        if stage == 3:

            @case(6)
            def _():
                x_mid().wait_recv()
                add_parts(
                    base, own_x, quarter, [(box_b, own_x), (box_b, UNIT + own_part_at), (box_b, UNIT + half)]
                )
                x_swap().start()

        if stage == 4:

            @case(6)
            def _():
                x_swap().wait_recv()
                x_mid().wait_send()
                bring(base, other_x, box_b, swap_at, quarter)
                z_share().start()
                z_out(5, mine_z).start()

        if stage == 5:

            @case(6)
            def _():
                z_share().wait_recv()
                z_mid().wait_send()
                bring(base, theirs_z, box_b, last_at, half)
                z_out(6, theirs_z).start()

        if stage == 6:

            @case(6)
            def _():
                x_swap().wait_send()
                z_share().wait_send()
                z_out(5, mine_z).wait_send()
                z_out(6, theirs_z).wait_send()

            @case(4)
            def _():
                z_in().wait_send()
                z_out(5, mine_z).wait_recv()
                z_out(6, theirs_z).wait_recv()
                bring(base, 0, box_b, 0, UNIT)

            pl.when(kind < 2)(lambda: Copies(n).start())

    def at_ready(n):
        return jnp.where(n < 2, 1, jnp.where(n < plain, 0, jnp.where(n < plain + 2, 1, 0)))

    def ready(first, count):
        for n in (first + k for k in range(count)):
            if reduce_dp:
                pl.when(at_ready(n) == 1)(functools.partial(begin, n))
            else:
                Copies(n).start()

    def tick(t):
        if reduce_dp:
            with jax.named_scope("dp_tick"):
                move(t)

    def move(t):
        for stage in (6, 5, 4, 3, 2, 1):
            advance(t - 2 * (stage - 1), stage)
        later = t + 2

        @pl.when(jnp.where(later >= units, 1, at_ready(later)) == 0)
        def _():
            begin(later)

    def tick_at(j, every, first):
        @pl.when(lax.rem(j, every) == every - 1)
        def _():
            tick(first + lax.div(j, every))

    ticks = units + 10

    def to_mate(which, number):
        return pltpu.make_async_remote_copy(
            src_ref=rs_out.at[lax.rem(number, 2)],
            dst_ref=rs_in.at[number],
            send_sem=rs_send.at[which, number],
            recv_sem=rs_recv.at[which, number],
            device_id={"tensor": mate},
            device_id_type=MESH,
        )

    def to_peer(which, number):
        return pltpu.make_async_remote_copy(
            src_ref=rs_in.at[number],
            dst_ref=y_in.at[number],
            send_sem=rs_send.at[which, 4 + number],
            recv_sem=rs_recv.at[which, 4 + number],
            device_id={"tensor": peer},
            device_id_type=MESH,
        )

    def scatter(j, which, compute):
        owner = jnp.where(j < 2, cross, jnp.where(j < 4, peer, mate))
        number = lax.rem(j, 2)
        row0 = pl.multiple_of(owner * rows_own + number * TILE, TILE)

        @pl.when(lax.div(j, 2) != 1)
        def _():
            at = jnp.where(j < 2, j, j - 2)
            pl.when(j >= 4)(lambda: to_mate(which, number).wait_send())

            def put(rows_at, part):
                rs_out[number, rows_at, :] = part.astype(BF)

            compute(row0, put)
            to_mate(which, at).start()

        @pl.when(lax.div(j, 2) == 1)
        def _():
            to_mate(which, number).wait_recv()

            def put(rows_at, part):
                rs_in[number, rows_at, :] = (rs_in[number, rows_at, :].astype(F32) + part).astype(BF)

            compute(row0, put)
            to_peer(which, number).start()

    def gathered(which, number):
        to_mate(which, 2 + number).wait_recv()
        to_peer(which, number).wait_recv()

    def settle(which):
        for number in range(2):
            to_mate(which, 2 + number).wait_send()
            to_peer(which, number).wait_send()

    def stored(number, target):
        return pltpu.make_async_copy(rs_out.at[number], target, result_sem.at[number])

    keep_tok.wait()
    for piece in range(g_tok.pieces):
        g_tok.forward(peer, piece).wait_send()

    def keep_unit(n, value):
        grads[pl.ds(pl.multiple_of(n * UNIT, UNIT), value.shape[0]), :] = value
        ready(n, value.shape[0] // UNIT)

    per_tile = TILE // UNIT
    first_out = hid.shape[1] // UNIT
    first_up = first_out + width // UNIT

    def arrive(piece):
        g_cot.to_peer(peer, piece).wait_recv()
        g_cot.forward(peer, piece).start()

    def down(piece):
        g_cot.forward(cross, piece).wait_recv()
        tile = dot(cot[:, piece * TILE : (piece + 1) * TILE], hid[...], TN)
        keep_unit(per_tile * piece, tile.astype(BF))

    def mix_some(first, last):
        with jax.named_scope("mixer"):
            lax.fori_loop(first, last, mix, 0)

    pairs = chunks // 2
    with jax.named_scope("grad_down"):
        arrive(0)
        arrive(1)
        down(0)
        down(1)
    tick(jnp.int32(0))
    mix_some(0, pairs // 4)
    arrive(2)
    mix_some(pairs // 4, pairs // 2)
    with jax.named_scope("grad_down"):
        down(2)

    def pause(t, carry):
        tick(t)
        return carry

    lax.fori_loop(1, 3, pause, 0)
    mix_some(pairs // 2, 3 * pairs // 4)
    arrive(3)
    mix_some(3 * pairs // 4, pairs)
    with jax.named_scope("grad_down"):
        down(3)
    tick(jnp.int32(3))
    keep_unit(first_out, dot(mixed[...], cot[...], TN).astype(BF))
    tick(jnp.int32(4))

    def branch(row0, put):
        here = pl.ds(row0, TILE)
        put(pl.ds(0, TILE), dot(mixed[here, :], w_out[...]) + dot(hid[here, :], w_down[...]))

    def keep_temp(rows_at, part):
        temp[0, rows_at, :] = part

    def own_copy(number, back=False):
        held = own_part.at[pl.ds(pl.multiple_of(number * TILE, TILE), TILE)]
        return pltpu.make_async_copy(*((held, temp.at[0]) if back else (temp.at[0], held)), temp_sem.at[0])

    def produce(j, carry):
        @pl.when(j >= 2)
        def _():
            scatter(j - 2, 0, branch)

        @pl.when(j < 2)
        def _():
            branch(pl.multiple_of(me * rows_own + j * TILE, TILE), keep_temp)
            own_copy(j).start()
            own_copy(j).wait()

        pl.when(j == 1)(lambda: slope_copy(0, True).start())
        pl.when(j == 2)(lambda: slope_copy(1, True).start())
        tick_at(j, 4, 5)
        return carry

    with jax.named_scope("outputs"):
        lax.fori_loop(0, 8, produce, 0)
    bring_up = pltpu.make_async_copy(
        grads.at[pl.ds(rows, 2 * rows_own)], hid.at[pl.ds(chip_row, 2 * rows_own)], tok_sem.at[0]
    )
    bring_up.start()

    def descend(p, carry):
        here = [pl.ds(pl.multiple_of(owner * rows_own + p * UNIT, UNIT), UNIT) for owner in (peer, cross)]
        parity = lax.rem(p, 2)
        slope_copy(p, True).wait()
        turned = wide([cot[at, :] for at in here], 0)
        for at in range(0, hid.shape[1], TILE):
            d_hidden = dot(turned, w_down[at : at + TILE, :], NT)
            d_up = (d_hidden * temp[parity, :, at : at + TILE]).astype(BF)
            for k, rows_at in enumerate(here):
                hid[rows_at, at : at + TILE] = d_up[k * UNIT : (k + 1) * UNIT]
        pl.when(p < 2)(lambda: slope_copy(p + 2, True).start())
        tick_at(p, 4, 7)
        return carry

    with jax.named_scope("grad_gelu"):
        lax.fori_loop(0, 4, descend, 0)
    bring_up.wait()

    def upward(j, carry):
        at = pl.ds(pl.multiple_of(j * TILE, TILE), TILE)
        keep_unit(first_up + per_tile * j, dot(n_two[:, at], hid[...], TN).astype(BF))
        tick_at(j, 2, 8)
        return carry

    with jax.named_scope("grad_up"):
        lax.fori_loop(0, n_two.shape[1] // TILE, upward, 0)

    state[...] = jnp.zeros_like(state)
    krow[...] = jnp.zeros_like(krow)
    feat_sums[...] = jnp.zeros_like(feat_sums)

    def unmix(step, carry):
        pair = chunks // 2 - 1 - step
        diag = diag_two[0:width, :].astype(F32)
        row_pair = pl.multiple_of(pair * 2 * CHUNK, 2 * CHUNK)
        d_mixed = dot(cot[pl.ds(row_pair, 2 * CHUNK), :], w_out[...], NT)
        here = chunk_rows(pair)
        query, key, value = ([fqkv[at, s * width : (s + 1) * width] for at in here] for s in range(3))
        d_over, under_parts = [], []
        for c in both_chunks:
            packed = rden[here[c], :]
            inverse = wide(
                [packed[:, h // 2 * HEAD_DIM // 2 : (h // 2 + 1) * HEAD_DIM // 2] for h in range(2 * heads)]
            )
            d_over.append(d_mixed[c * CHUNK : (c + 1) * CHUNK] * inverse)
            under_parts.append(wide(split(d_over[c] * att[here[c], :])))
        d_under = [-dot(under_parts[c], diag_two[...]) for c in both_chunks]
        under_row = [-dot(wide([head_rows, head_rows]), under_parts[c], NT) for c in both_chunks]
        over_split = [split(d_over[c]) for c in both_chunks]
        over_both = [wide(over_split[c]) for c in both_chunks]
        over_heads = [wide([per_head(part) for part in over_split[c]]) for c in both_chunks]
        query_heads, key_heads, value_heads = ([per_head(field[c]) for c in both_chunks] for field in (query, key, value))
        scores_back = [(dot(key[c], query_heads[c], NT) * causal_back).astype(BF) for c in both_chunks]
        d_scores = [dot(over_both[c], wide([value_heads[c]] * 2), NT) for c in both_chunks]
        d_back = [dot(wide([value[c]] * 2), over_heads[c], NT) for c in both_chunks]
        turned = [query[c].T for c in both_chunks]
        made = []
        for c in both_chunks:
            for k in both_blocks:
                left = turned[c][:, k * BLOCK : (k + 1) * BLOCK]
                made.append(dot(wide([left, left]), wide([halves(part)[k] for part in over_split[c]], 0)) * diag)
        d_scores = [
            wide(
                split(
                    (
                        d_scores[c]
                        + wide(
                            [
                                jnp.broadcast_to(d_under[c][:, h * HEAD_DIM : h * HEAD_DIM + 1], (CHUNK, CHUNK))
                                for h in range(heads)
                            ]
                        )
                    )
                    * causal
                )
            )
            for c in both_chunks
        ]
        d_back = [
            wide(split((d_back[c] + wide([under_row[c][h : h + 1, :] for h in range(heads)])) * causal_back))
            for c in both_chunks
        ]
        d_query = [dot(d_scores[c], wide([key_heads[c]] * 2, 0)) for c in both_chunks]
        d_key = [dot(d_back[c], wide([query_heads[c]] * 2, 0)) for c in both_chunks]
        d_value = [dot(scores_back[c], over_heads[c]) for c in both_chunks]
        later, later_row = state[...], krow[0:1, :]
        more = {}
        for at in reversed(range(4)):
            c, k = divmod(at, 2)
            block = 4 * pair + at
            query_k, key_k, value_k, both_k, under_k = (
                halves(field[c])[k] for field in (query, key, value, over_both, d_under)
            )
            carried = wide([states[block]] * heads, 0) * diag_two[0:width, :]
            keep = joined(block + 1)
            later, later_row = later * keep, later_row * keep
            high, low = split(later)
            more[at] = (
                dot(both_k, wide([carried, carried]), NT) + under_k * ksums[block][0:1, :],
                dot(wide([value_k, value_k]), wide([high, low]), NT) + later_row,
                dot(wide([key_k, key_k]), wide([high, low], 0)),
            )
            later = later + made[at]
            later_row = later_row + jnp.sum(query_k.astype(F32) * under_k, 0, keepdims=True)
        state[...] = later
        krow[0:1, :] = later_row
        turn = rotation(row_pair, 2 * CHUNK // BLOCK)
        here = pl.ds(row_pair, 2 * CHUNK)
        for s, found in enumerate((d_query, d_key)):
            grad = wide(found, 0) + wide([more[at][s] for at in range(4)], 0)
            spectrum = spec[s, here, :]
            grad = grad * (weight_row * jnp.exp(scale_row * spectrum))
            feat_sums[0:1, :] += jnp.sum(grad * spectrum, 0, keepdims=True)
            feat_sums[1:2, :] += jnp.sum(grad, 0, keepdims=True)
            high, low = split(grad * scale_row)
            back = dot(high, dct[:, 0:width]) + dot(low, dct[:, 0:width]) + dot(high, dct[:, 2 * width :])
            fqkv[here, s * width : (s + 1) * width] = rotate(back, turn, True).astype(BF)
        d_value = wide([d_value[c][:, :width] + d_value[c][:, width:] for c in both_chunks], 0)
        fqkv[here, 2 * width : 3 * width] = (d_value + wide([more[at][2] for at in range(4)], 0)).astype(BF)
        tick(10 + step)

        return carry

    with jax.named_scope("mixer_back"):
        lax.fori_loop(0, chunks // 2, unmix, 0)

    for j in range(n_one.shape[1] // TILE):
        tile = dot(n_one[:, j * TILE : (j + 1) * TILE], fqkv[...], TN).astype(BF)
        for s in range(3):
            at = 3 * j + s
            first = plain * UNIT + at // 4 * TILE
            grads[first : first + TILE, at % 4 * width : (at % 4 + 1) * width] = tile[:, s * width : (s + 1) * width]
        if j:
            ready(plain + (j - 1) * per_tile, per_tile)


    tick(jnp.int32(18))

    sums[...] = jnp.zeros_like(sums)

    def tok_copy(row0):
        return pltpu.make_async_copy(tok_kept.at[pl.ds(row0, TILE)], tok_tile, tok_sem.at[0])

    def row_grads(row0, put):
        here = pl.ds(row0, TILE)
        tok_copy(row0).start()
        total = dot(fqkv[here, 0:width], w_qkv[0], NT)
        for s in (1, 2):
            total = total + dot(fqkv[here, s * width : (s + 1) * width], w_qkv[s], NT)
        temp[0] = total
        temp[1] = dot(hid[here, :], w_up[...], NT)
        tok_copy(row0).wait()

        def fold(i, inner):
            at = pl.ds(pl.multiple_of(i * SUB, SUB), SUB)
            unit, _ = centered(tok_tile, pl.multiple_of(i * SUB, SUB), SUB)
            one, two = temp[0, at, :], temp[1, at, :]
            for number, term in enumerate((one * unit, one, two * unit, two)):
                sums[number] += jnp.sum(term.reshape(SUB // 8, 8, term.shape[1]), 0)
            put(at, one * gain_one + two * gain_two)
            return inner

        lax.fori_loop(0, TILE // SUB, fold, 0)

    def finish(number, carry):
        row0 = pl.multiple_of(me * rows_own + number * TILE, TILE)
        own_copy(number, True).start()
        tok_copy(row0).start()
        own_copy(number, True).wait()
        tok_copy(row0).wait()
        gathered(0, number)

        def step(i, inner):
            at = pl.ds(pl.multiple_of(i * SUB, SUB), SUB)
            total = temp[0, at, :] + rs_in[2 + number, at, :].astype(F32) + y_in[number, at, :].astype(F32)
            total = total + tok_tile[at, :].astype(F32)
            rs_out[number, at, :] = total.astype(BF)
            return inner

        lax.fori_loop(0, TILE // SUB, step, 0)
        stored(number, mixed_out.at[pl.ds(pl.multiple_of(number * TILE, TILE), TILE)]).start()
        return carry

    with jax.named_scope("finish"):
        settle(0)
        lax.fori_loop(0, 2, finish, 0)
    pl.semaphore_signal(free_mate, inc=1, device_id={"tensor": mate}, device_id_type=MESH)
    pl.semaphore_signal(free_peer, inc=1, device_id={"tensor": peer}, device_id_type=MESH)
    for number in range(2):
        stored(number, mixed_out.at[pl.ds(0, TILE)]).wait()
    pl.semaphore_wait(free_mate, 1)
    pl.semaphore_wait(free_peer, 1)

    def inputs(j, carry):
        @pl.when(j < 6)
        def _():
            scatter(j, 1, row_grads)

        @pl.when(j >= 6)
        def _():
            row_grads(pl.multiple_of(me * rows_own + (j - 6) * TILE, TILE), keep_temp)
            own_copy(j - 6).start()
            own_copy(j - 6).wait()

        tick(19 + j)
        return carry

    with jax.named_scope("row_grads"):
        lax.fori_loop(0, 8, inputs, 0)

    def conclude(number):
        row0 = pl.multiple_of(me * rows_own + number * TILE, TILE)
        own_copy(number, True).start()
        tok_copy(row0).start()
        gathered(1, number)
        own_copy(number, True).wait()
        tok_copy(row0).wait()

        def step(i, inner):
            at = pl.ds(pl.multiple_of(i * SUB, SUB), SUB)
            group_at = pl.multiple_of(row0 + i * SUB, SUB)
            unit, deviation = centered(tok_tile, pl.multiple_of(i * SUB, SUB), SUB)
            total = temp[0, at, :] + rs_in[2 + number, at, :].astype(F32) + y_in[number, at, :].astype(F32)
            along = jnp.mean(total * unit, -1, keepdims=True)
            total = total - jnp.mean(total, -1, keepdims=True) - unit * along
            total = cot[pl.ds(group_at, SUB), :].astype(F32) + deviation * total
            rs_out[number, at, :] = total.astype(BF)
            return inner

        lax.fori_loop(0, TILE // SUB, step, 0)
        stored(number, input_grad.at[pl.ds(number * TILE, TILE)]).start()

    small[...] = jnp.zeros_like(small)
    for number in range(4):
        small[number : number + 1, :] = jnp.sum(sums[number], 0, keepdims=True)
    small[4:5, 0:width] = feat_sums[0:1, :]
    small[5:6, 0:width] = feat_sums[1:2, :] / weight_row

    def small_hops(axis, own, count, boxes, first):
        hops = []
        for step in range(1, count):
            hops.append(
                pltpu.make_async_remote_copy(
                    src_ref=small,
                    dst_ref=boxes.at[own],
                    send_sem=small_send.at[first + step - 1],
                    recv_sem=small_recv.at[first + step - 1],
                    device_id={axis: lax.rem(own + step, count)},
                    device_id_type=MESH,
                )
            )
        return hops

    over_tensor = small_hops("tensor", me, 4, small_in, 0)
    over_dp = small_hops("dp", group, members, small_wide, 3)

    def small_step(k):
        if k == 0:
            for copy in over_tensor:
                copy.start()
            small_in[me] = small[...]
        if k == 1:
            for copy in over_tensor:
                copy.wait()
            total = small_in[0]
            for member in range(1, 4):
                total = total + small_in[member]
            small[0:4, :] = total[0:4, :]
        if k == 1 and reduce_dp:
            for copy in over_dp:
                copy.start()
            small_wide[group] = small[...]
        if k == 2 and reduce_dp:
            for copy in over_dp:
                copy.wait()
            total = small_wide[0]
            for member in range(1, members):
                total = total + small_wide[member]
            small[...] = total

    settle_at, late = 28, {27: 0, 29: 1, 32: 2}
    if reduce_dp:

        def rest(t, carry):
            for at, k in late.items():
                pl.when(t == at)(functools.partial(small_step, k))
            for number in range(2):

                @pl.when(t == settle_at + 2 * number)
                def _():
                    if number == 0:
                        settle(1)
                    conclude(number)

            tick(t)
            return carry

        lax.fori_loop(27, ticks, rest, 0)
    else:
        for k in range(2):
            small_step(k)
        settle(1)
        for number in range(2):
            conclude(number)
    for h in range(heads):
        at = slice(h * HEAD_DIM, (h + 1) * HEAD_DIM)
        feat_out[0, h : h + 1, :] = small[4:5, at]
        feat_out[1, h : h + 1, :] = small[5:6, at]

    def copied(n, carry):
        Copies(n).wait()
        return carry

    lax.fori_loop(0, units, copied, 0)
    for number in range(2):
        stored(number, input_grad.at[pl.ds(0, TILE)]).wait()

    for gather in (g_tok, g_cot):
        gather.to_mate(me).wait_send()
        for piece in range(gather.pieces):
            gather.to_peer(me, piece).wait_send()
    for piece in range(g_cot.pieces):
        g_cot.forward(peer, piece).wait_send()


def widen(down_in, out_in, up_in, qkv_in, *outs):
    down, out, up, qkv = outs
    down[...] = down_in[...].astype(F32).T
    out[...] = out_in[...].astype(F32)
    up[...] = up_in[...].astype(F32)
    qkv[...] = qkv_in[...].astype(F32)


def shards(
    reduce_dp,
    tokens,
    ln1_gain,
    ln1_bias,
    ln2_gain,
    ln2_bias,
    w_qkv,
    w_out,
    w_up,
    w_down,
    feature_scale,
    feature_weight,
    lengths,
    cotangent,
):
    rows_own, model = tokens.shape
    rows = 4 * rows_own
    heads = feature_scale.shape[0]
    width = heads * HEAD_DIM
    hidden = w_up.shape[1]
    consts = tables(rows // BLOCK, heads)
    norms = [value.reshape(1, model) for value in (ln1_gain, ln1_bias, ln2_gain, ln2_bias)]
    anywhere = pl.BlockSpec(memory_space=pl.ANY)
    vmem = pl.BlockSpec(memory_space=pltpu.VMEM)
    smem = pl.BlockSpec(memory_space=pltpu.SMEM)
    shape = jax.ShapeDtypeStruct
    plain = 2 * hidden + width
    units = (plain + 3 * width) // UNIT
    mixed_out, input_grad, grads, g_qkv, _, _, _, small, feats = pl.pallas_call(
        functools.partial(kernel, reduce_dp),
        out_shape=(
            shape((rows_own, model), BF),
            shape((rows_own, model), BF),
            shape((plain, model), BF),
            shape((3, model, width), BF),
            shape((rows // 2, hidden), F32),
            shape((rows_own, model), F32),
            shape((rows, model), BF),
            shape((8, model), F32),
            shape((2, heads, HEAD_DIM), F32),
        ),
        in_specs=[smem, anywhere, anywhere] + [vmem] * 4 + [anywhere] * 4 + [vmem] * 6,
        out_specs=(anywhere,) * 7 + (vmem, vmem),
        scratch_shapes=[
            pltpu.VMEM((TILE, model), BF),
            pltpu.VMEM((rows, model), BF),
            pltpu.VMEM((rows, model), BF),
            pltpu.VMEM((rows, model), BF),
            pltpu.VMEM((rows, hidden), BF),
            pltpu.VMEM((rows, 3 * width), BF),
            pltpu.VMEM((2, rows, width), F32),
            pltpu.VMEM((rows, width), BF),
            pltpu.VMEM((rows, width), F32),
            pltpu.VMEM((rows, width // 2), F32),
            pltpu.VMEM((rows // BLOCK, HEAD_DIM, width), BF),
            pltpu.VMEM((rows // BLOCK, 8, width), F32),
            pltpu.VMEM((width, width), F32),
            pltpu.VMEM((8, width), F32),
            pltpu.VMEM((units * UNIT, model), BF),
            pltpu.VMEM((SLOTS // 2, 2 * UNIT, model), BF),
            pltpu.VMEM((SLOTS // 2, 5 * UNIT // 2, model), BF),
            pltpu.VMEM((2, TILE, model), BF),
            pltpu.VMEM((4, TILE, model), BF),
            pltpu.VMEM((2, TILE, model), BF),
            pltpu.VMEM((2, TILE, model), F32),
            pltpu.VMEM((4, 8, model), F32),
            pltpu.VMEM((8, width), F32),
            pltpu.VMEM((4, 8, model), F32),
            pltpu.VMEM((8, 8, model), F32),
            pltpu.VMEM(w_qkv.shape, BF),
            pltpu.VMEM(w_out.shape, BF),
            pltpu.VMEM(w_up.shape, BF),
            pltpu.VMEM(w_down.shape, BF),
            pltpu.SemaphoreType.DMA((2 + 2 * rows_own // UNIT,)),
            pltpu.SemaphoreType.DMA((2 + 2 * rows_own // UNIT + 2 * model // TILE,)),
            pltpu.SemaphoreType.DMA((2 + 2 * rows_own // UNIT + 2 * model // TILE,)),
            pltpu.SemaphoreType.DMA((4,)),
            pltpu.SemaphoreType.DMA((units, 7)),
            pltpu.SemaphoreType.DMA((units, 7)),
            pltpu.SemaphoreType.DMA((2, 6)),
            pltpu.SemaphoreType.DMA((2, 6)),
            pltpu.SemaphoreType.DMA((10,)),
            pltpu.SemaphoreType.DMA((10,)),
            pltpu.SemaphoreType.DMA((units,)),
            pltpu.SemaphoreType.DMA((2,)),
            pltpu.SemaphoreType.DMA((1,)),
            pltpu.SemaphoreType.DMA((2,)),
            pltpu.SemaphoreType.REGULAR,
            pltpu.SemaphoreType.REGULAR,
        ],
        compiler_params=pltpu.CompilerParams(
            collective_id=0, has_side_effects=True, vmem_limit_bytes=62 * 2**20
        ),
    )(lengths, tokens, cotangent, *norms, w_qkv, w_out, w_up, w_down, feature_scale, feature_weight, *consts)
    norm_sums = small[0:4]
    if not reduce_dp:
        grads, g_qkv, norm_sums, feats = lax.psum(
            (*lax.optimization_barrier((grads.astype(F32), g_qkv.astype(F32))), norm_sums, feats), "dp"
        )
    steps = 8
    down_cut, out_cut, up_cut, row_cut = hidden // steps, width // steps, model // steps, model // steps
    g_down, g_out, g_up, g_qkv = pl.pallas_call(
        widen,
        grid=(steps,),
        out_shape=(
            shape((hidden, model), F32),
            shape((width, model), F32),
            shape((model, hidden), F32),
            shape((3, model, width), F32),
        ),
        in_specs=[
            pl.BlockSpec((model, down_cut), lambda i: (0, i)),
            pl.BlockSpec((out_cut, model), lambda i: (hidden // out_cut + i, 0)),
            pl.BlockSpec((up_cut, hidden), lambda i: ((hidden + width) // up_cut + i, 0)),
            pl.BlockSpec((3, row_cut, width), lambda i: (0, i, 0)),
        ],
        out_specs=(
            pl.BlockSpec((down_cut, model), lambda i: (i, 0)),
            pl.BlockSpec((out_cut, model), lambda i: (i, 0)),
            pl.BlockSpec((up_cut, hidden), lambda i: (i, 0)),
            pl.BlockSpec((3, row_cut, width), lambda i: (0, i, 0)),
        ),
        compiler_params=pltpu.CompilerParams(vmem_limit_bytes=24 * 2**20),
    )(grads, grads, grads, g_qkv)
    return (
        mixed_out,
        input_grad,
        norm_sums[0],
        norm_sums[1],
        norm_sums[2],
        norm_sums[3],
        g_qkv,
        g_out,
        g_up,
        g_down,
        feats[0],
        feats[1],
    )


def solution(mesh):
    placed = (
        P(("dp", "tensor"), None),
        P(),
        P(),
        P(),
        P(),
        P(None, None, "tensor"),
        P("tensor", None),
        P(None, "tensor"),
        P("tensor", None),
        P("tensor", None),
        P("tensor", None),
        P("dp", None),
        P(("dp", "tensor"), None),
    )
    return jax.shard_map(
        functools.partial(shards, mesh.shape["dp"] == 8),
        mesh=mesh,
        in_specs=placed,
        out_specs=(
            P(("dp", "tensor"), None),
            P(("dp", "tensor"), None),
            P(),
            P(),
            P(),
            P(),
            P(None, None, "tensor"),
            P("tensor", None),
            P(None, "tensor"),
            P("tensor", None),
            P("tensor", None),
            P("tensor", None),
        ),
        check_vma=False,
    )
```

```python
import functools
import math

import jax
import jax.numpy as jnp
import ml_dtypes
import numpy as np
from jax import lax
from jax.experimental import pallas as pl
from jax.experimental.pallas import tpu as pltpu
from jax.sharding import PartitionSpec as P

HEAD_DIM = 64
ROT = 16
BLOCK = 64
CHUNK = 128
TILE = 256
UNIT = 128
SUB = 32
BOXES_X = 9
BOXES_Z = 6
LATE = 18
MESH = pl.DeviceIdType.MESH
F32 = jnp.float32
BF = jnp.bfloat16
NN = (((1,), (0,)), ((), ()))
NT = (((1,), (1,)), ((), ()))
TN = (((0,), (0,)), ((), ()))


def dot(left, right, dims=NN):
    return lax.dot_general(left, right, dims, preferred_element_type=F32)


def split(value):
    high = value.astype(BF)
    return high, (value - high.astype(F32)).astype(BF)


def wide(parts, axis=1):
    return jnp.concatenate(parts, axis)


def tables(blocks, heads):
    width = heads * HEAD_DIM
    freq, dims = np.arange(HEAD_DIM)[:, None], np.arange(HEAD_DIM)[None, :]
    dct = np.cos(np.pi * (dims + 0.5) * freq / HEAD_DIM) * math.sqrt(2.0 / HEAD_DIM)
    dct[0] *= math.sqrt(0.5)
    dct = np.kron(np.eye(heads), dct).astype(np.float32)
    high = dct.astype(ml_dtypes.bfloat16)
    low = (dct - high.astype(np.float32)).astype(ml_dtypes.bfloat16)
    halves = np.concatenate([high, high, low], 1)
    half = ROT // 2
    lane = np.arange(2 * HEAD_DIM) % HEAD_DIM
    rate = np.where(lane < ROT, 10000.0 ** (-(lane % half) * 2.0 / ROT), 0.0)
    in_block = np.arange(BLOCK)[:, None] * rate[None]
    of_block = np.arange(blocks)[:, None] * BLOCK * rate[None]
    signs = np.stack([np.where(lane < half, -1.0, 0.0), np.where((lane >= half) & (lane < ROT), 1.0, 0.0)] + [0.0 * lane] * 6)
    angles = np.concatenate([np.cos(in_block), np.sin(in_block), np.cos(of_block), np.sin(of_block), signs], 0)
    diagonal = np.kron(np.eye(heads), np.ones((HEAD_DIM, HEAD_DIM)))
    masks = np.kron(np.eye(heads), np.ones((CHUNK, HEAD_DIM)))
    return (
        halves,
        angles.astype(np.float32),
        np.concatenate([diagonal, diagonal], 0).astype(ml_dtypes.bfloat16),
        masks.astype(ml_dtypes.bfloat16),
    )


def kernel(
    reduce_dp,
    lengths,
    tok_in,
    cot_in,
    gain_one_in,
    bias_one_in,
    gain_two_in,
    bias_two_in,
    w_qkv_in,
    w_out_in,
    w_up_in,
    w_down_in,
    feature_scale,
    feature_weight,
    dct,
    angles,
    diag_two,
    masks,
    mixed_out,
    input_grad,
    grads_out,
    qkv_out,
    slopes,
    own_part,
    tok_kept,
    small,
    feat_out,
    cot,
    n_one,
    n_two,
    hid,
    fqkv,
    spec,
    mixed,
    att,
    rden,
    states,
    ksums,
    state,
    krow,
    grads,
    recv_a,
    recv_b,
    rs_out,
    rs_in,
    y_in,
    temp,
    sums,
    feat_sums,
    small_in,
    small_wide,
    w_qkv,
    w_out,
    w_up,
    w_down,
    local_sem,
    send_sem,
    recv_sem,
    weight_sem,
    ar_send,
    ar_recv,
    rs_send,
    rs_recv,
    small_send,
    small_recv,
    grad_sem,
    temp_sem,
    tok_sem,
    result_sem,
    free_mate,
    free_peer,
):
    rows_own = tok_in.shape[0]
    rows = cot.shape[0]
    tok = grads
    width = w_out_in.shape[0]
    heads = width // HEAD_DIM
    chunks = rows // CHUNK
    me = lax.axis_index("tensor")
    core = lax.rem(me, 2)
    mate = me + 1 - 2 * core
    peer = lax.rem(me + 2, 4)
    cross = 3 - me
    group = lax.axis_index("dp")
    along_x = lax.rem(group, 2)
    across = group + 1 - 2 * along_x
    along_z = lax.div(group, 2)
    middle = along_z * (3 - along_z)

    def at_end(step):
        pl.when(middle == 0)(step)

    def at_mid(step):
        pl.when(middle > 0)(step)

    side = jnp.where(along_z < 2, 0, 1)
    inward = group + 2 - 4 * side
    outward = group - 2 + 4 * side
    units = grads.shape[0] // UNIT

    weight_copies = [
        pltpu.make_async_copy(source, target, weight_sem.at[k])
        for k, (source, target) in enumerate(
            ((w_qkv_in, w_qkv), (w_up_in, w_up), (w_out_in, w_out), (w_down_in, w_down))
        )
    ]
    for copy in weight_copies:
        copy.start()

    barrier = pltpu.get_barrier_semaphore()
    members = 8 if reduce_dp else 1
    for step in range(1, 4):
        other = lax.rem(me + step, 4)
        pl.semaphore_signal(barrier, inc=1, device_id={"tensor": other}, device_id_type=MESH)
    for step in range(1, members):
        other = lax.rem(group + step, members)
        pl.semaphore_signal(barrier, inc=1, device_id={"dp": other}, device_id_type=MESH)
    pl.semaphore_wait(barrier, 2 + members)

    def slot(buf, owner, piece=None, columns=False):
        if piece is None:
            return buf.at[pl.ds(pl.multiple_of(owner * rows_own, rows_own), rows_own)]
        if columns:
            here = pl.ds(pl.multiple_of(owner * rows_own, rows_own), rows_own)
            return buf.at[here, piece * TILE : (piece + 1) * TILE]
        return buf.at[pl.ds(pl.multiple_of(owner * rows_own + piece * UNIT, UNIT), UNIT)]

    class Gather:
        def __init__(self, source, buf, base, columns):
            self.source, self.buf, self.base, self.columns = source, buf, base, columns
            self.pieces = source.shape[1] // TILE if columns else source.shape[0] // UNIT

        def copy(self, number, src, dst, target):
            return pltpu.make_async_remote_copy(
                src_ref=src,
                dst_ref=dst,
                send_sem=send_sem.at[self.base + number],
                recv_sem=recv_sem.at[self.base + number],
                device_id={"tensor": target},
                device_id_type=MESH,
            )

        def local(self):
            return pltpu.make_async_copy(self.source, slot(self.buf, me), local_sem.at[self.base])

        def to_mate(self, owner):
            return self.copy(0, self.source, slot(self.buf, owner), mate)

        def to_peer(self, owner, piece):
            if self.columns:
                part = self.source.at[:, piece * TILE : (piece + 1) * TILE]
            else:
                part = self.source.at[pl.ds(piece * UNIT, UNIT)]
            return self.copy(1 + piece, part, slot(self.buf, owner, piece, self.columns), peer)

        def forward(self, owner, piece):
            part = slot(self.buf, owner, piece, self.columns)
            return self.copy(1 + self.pieces + piece, part, part, mate)

    g_tok, g_cot = Gather(tok_in, tok, 0, False), Gather(cot_in, cot, 1 + 2 * (rows_own // UNIT), True)
    g_tok.to_mate(me).start()
    for piece in range(g_tok.pieces):
        g_tok.to_peer(me, piece).start()
    g_tok.local().start()
    g_cot.to_mate(me).start()
    g_cot.local().start()

    start_one = lengths[0, 0]
    start_two = start_one + lengths[0, 1]

    def segment(block):
        return (block >= start_one).astype(jnp.int32) + (block >= start_two).astype(jnp.int32)

    def in_sequence(block):
        return block - jnp.where(block >= start_two, start_two, jnp.where(block >= start_one, start_one, 0))

    gain_one, bias_one, gain_two, bias_two = gain_one_in[...], bias_one_in[...], gain_two_in[...], bias_two_in[...]
    scale_row, weight_row = (
        wide([field[h : h + 1, :] for h in range(heads)]) for field in (feature_scale, feature_weight)
    )
    blocks = rows // BLOCK

    def rotation(row0, count):
        cos_in, sin_in = angles[0:BLOCK, :], angles[BLOCK : 2 * BLOCK, :]
        sign_a = angles[2 * BLOCK + 2 * blocks : 2 * BLOCK + 2 * blocks + 1, :]
        sign_b = angles[2 * BLOCK + 2 * blocks + 1 : 2 * BLOCK + 2 * blocks + 2, :]
        cosines, sines = [], []
        for k in range(count):
            place = in_sequence(lax.div(row0, BLOCK) + k)
            cos_at = angles[pl.ds(2 * BLOCK + place, 1), :]
            sin_at = angles[pl.ds(2 * BLOCK + blocks + place, 1), :]
            cosines.append(cos_in * cos_at - sin_in * sin_at)
            sines.append(sin_in * cos_at + cos_in * sin_at)
        cosine, sine = wide(cosines, 0), wide(sines, 0)
        return cosine, sine * sign_a, sine * sign_b

    def rotate(field, turn, back=False):
        cosine, sine_a, sine_b = turn
        parts = []
        for at in range(0, width, 2 * HEAD_DIM):
            part = field[:, at : at + 2 * HEAD_DIM]
            ahead = pltpu.roll(part, 2 * HEAD_DIM - ROT // 2, 1) * sine_a
            behind = pltpu.roll(part, ROT // 2, 1) * sine_b
            parts.append(part * cosine - (ahead + behind) if back else part * cosine + (ahead + behind))
        return wide(parts)

    def unit_rows(value):
        value = value - jnp.mean(value, -1, keepdims=True)
        deviation = lax.rsqrt(jnp.mean(value * value, -1, keepdims=True) + 1e-05)
        return value * deviation, deviation

    chip_row = pl.multiple_of(lax.div(me, 2) * 2 * rows_own, rows_own)

    def slope_copy(p, back=False):
        held = slopes.at[pl.ds(pl.multiple_of(p * TILE, TILE), TILE)]
        slot_of = temp.at[lax.rem(p, 2)]
        return pltpu.make_async_copy(*((held, slot_of) if back else (slot_of, held)), temp_sem.at[lax.rem(p, 2)])

    def project(j, carry):
        @pl.when(j == 0)
        def _():
            g_tok.local().wait()

            g_cot.local().wait()

        @pl.when(j == 2)
        def _():
            g_tok.to_mate(mate).wait_recv()
            g_cot.to_mate(mate).wait_recv()

        for piece in range(g_tok.pieces):

            @pl.when(j == 4 + piece)
            def _():
                g_tok.to_peer(peer, piece).wait_recv()
                g_tok.forward(peer, piece).start()
                g_cot.to_peer(me, piece).start()
                g_tok.forward(cross, piece).wait_recv()

        late = lax.div(j, 4)
        early_at = jnp.where(j < 2, me, mate) * rows_own + lax.rem(j, 2) * TILE
        row_a = pl.multiple_of(jnp.where(late == 0, early_at, peer * rows_own + (j - 4) * UNIT), UNIT)
        row_b = pl.multiple_of(jnp.where(late == 0, early_at + UNIT, cross * rows_own + (j - 4) * UNIT), UNIT)
        here = [pl.ds(row_a, UNIT), pl.ds(row_b, UNIT)]

        for at in here:
            pltpu.make_async_copy(tok.at[at], tok_kept.at[at], tok_sem.at[0]).start()
        unit, _ = unit_rows(wide([tok[at, :] for at in here], 0).astype(F32))
        first = (unit * gain_one + bias_one).astype(BF)
        second = (unit * gain_two + bias_two).astype(BF)
        for k, at in enumerate(here):
            n_one[at, :] = first[k * UNIT : (k + 1) * UNIT]
            n_two[at, :] = second[k * UNIT : (k + 1) * UNIT]
        turn = [wide(pair, 0) for pair in zip(*(rotation(at, UNIT // BLOCK) for at in (row_a, row_b)))]

        def keep(write, value):
            for k, at in enumerate(here):
                write(at, value[k * UNIT : (k + 1) * UNIT])

        def keep_field(s, value):
            def write(at, part):
                fqkv[at, s * width : (s + 1) * width] = part

            keep(write, value.astype(BF))

        for s in range(2):
            high, low = split(rotate(dot(first, w_qkv[s]), turn))
            spectrum = dot(wide([high, low]), dct[:, 0 : 2 * width], NT) + dot(high, dct[:, 2 * width :], NT)

            def keep_spectrum(at, part):
                spec[s, at, :] = part

            keep(keep_spectrum, spectrum)
            keep_field(s, weight_row * jnp.exp(scale_row * spectrum))
        keep_field(2, dot(first, w_qkv[2]))
        parity = lax.rem(j, 2)
        pl.when(j >= 6)(lambda: slope_copy(j - 6).wait())
        for at in range(0, w_up.shape[1], TILE):
            up = dot(second, w_up[:, at : at + TILE])
            below = 0.5 * (1.0 + lax.erf(up * math.sqrt(0.5)))

            def keep_hidden(rows_at, part):
                hid[rows_at, at : at + TILE] = part

            keep(keep_hidden, (up * below).astype(BF))
            temp[parity, :, at : at + TILE] = below + up * (
                jnp.exp(-0.5 * up * up) * (1.0 / math.sqrt(2.0 * math.pi))
            )

        @pl.when(late == 0)
        def _():
            turned = wide([cot[at, :] for at in here], 0)
            first_at = pl.multiple_of(rows + row_a - chip_row, TILE)
            for at in range(0, hid.shape[1], TILE):
                d_hidden = dot(turned, w_down[at : at + TILE, :], NT)
                grads[pl.ds(first_at, TILE), at : at + TILE] = (d_hidden * temp[parity, :, at : at + TILE]).astype(BF)

        pl.when(late == 1)(lambda: slope_copy(j - 4).start())
        return carry

    for copy in weight_copies:
        copy.wait()
    with jax.named_scope("project"):
        lax.fori_loop(0, rows // TILE, project, 0)
    for p in (2, 3):
        slope_copy(p).wait()

    grid_t = lax.broadcasted_iota(jnp.int32, (CHUNK, CHUNK), 0)
    grid_s = lax.broadcasted_iota(jnp.int32, (CHUNK, CHUNK), 1)
    together = (grid_t < BLOCK) == (grid_s < BLOCK)
    causal = wide([jnp.where((grid_t >= grid_s) & together, 1.0, 0.0).astype(F32)] * heads)
    causal_back = wide([jnp.where((grid_t <= grid_s) & together, 1.0, 0.0).astype(F32)] * heads)
    head_rows = jnp.where(
        lax.broadcasted_iota(jnp.int32, (8, width), 0) == lax.div(lax.broadcasted_iota(jnp.int32, (8, width), 1), HEAD_DIM),
        1.0,
        0.0,
    ).astype(BF)
    both_chunks = range(2)
    both_blocks = range(CHUNK // BLOCK)

    def joined(block):
        return jnp.where(segment(block) == segment(block - 1), jnp.float32(1.0), jnp.float32(0.0))

    def per_head(value):
        return wide([value * masks[h * CHUNK : (h + 1) * CHUNK, :] for h in range(heads)], 0)

    def halves(value):
        return [value[k * BLOCK : (k + 1) * BLOCK] for k in both_blocks]

    def chunk_rows(pair):
        return [pl.ds(pl.multiple_of((2 * pair + c) * CHUNK, CHUNK), CHUNK) for c in both_chunks]

    state[...] = jnp.zeros_like(state)
    krow[...] = jnp.zeros_like(krow)

    def mix(pair, carry):
        diag = diag_two[0:width, :].astype(F32)
        here = chunk_rows(pair)
        query, key, value = ([fqkv[at, s * width : (s + 1) * width] for at in here] for s in range(3))
        scores = [split(dot(query[c], per_head(key[c]), NT) * causal) for c in both_chunks]
        turned = [key[c].T for c in both_chunks]
        over = [dot(scores[c][0], per_head(value[c])) for c in both_chunks]
        under = [dot(scores[c][0], masks[...]) + dot(scores[c][1], masks[...]) for c in both_chunks]
        made = [
            dot(turned[c][:, k * BLOCK : (k + 1) * BLOCK], halves(value[c])[k]) * diag
            for c in both_chunks
            for k in both_blocks
        ]
        row_made = [jnp.sum(halves(key[c])[k].astype(F32), 0, keepdims=True) for c in both_chunks for k in both_blocks]
        now, row = state[...], krow[0:1, :]
        carried, rows_in = [], []
        for k in range(4):
            carried.append(now.astype(BF))
            rows_in.append(row)
            states[4 * pair + k] = sum(now[h * HEAD_DIM : (h + 1) * HEAD_DIM] for h in range(heads)).astype(BF)
            ksums[pl.ds(4 * pair + k, 1), :] = row
            keep = joined(4 * pair + k + 1)
            now = (now + made[k]) * keep
            row = (row + row_made[k]) * keep
        state[...] = now
        krow[0:1, :] = row
        for c in both_chunks:
            parts = halves(query[c])
            more = wide([dot(parts[k], carried[2 * c + k]) for k in both_blocks], 0)
            high, low = split(wide([parts[k].astype(F32) * rows_in[2 * c + k] for k in both_blocks], 0))
            inverse = 1.0 / (under[c] + dot(wide([high, low]), diag_two[...]))
            attended = (over[c] + more) * inverse
            att[here[c], :] = attended
            rden[here[c], :] = wide([inverse[:, h * HEAD_DIM : h * HEAD_DIM + HEAD_DIM // 2] for h in range(heads)])
            mixed[here[c], :] = attended.astype(BF)

        return carry

    def add_parts(base, first, count, sources):
        for at in range(0, count, SUB):
            total = base[pl.ds(first + at, SUB), :].astype(F32)
            for source, place in sources:
                total = total + source[pl.ds(place + at, SUB), :].astype(F32)
            base[pl.ds(first + at, SUB), :] = total.astype(BF)

    def bring(base, first, box, place, count):
        base[pl.ds(first, count), :] = box[pl.ds(place, count), :]

    half, quarter = UNIT // 2, UNIT // 4

    def rows_of(index, size):
        return pl.multiple_of(index * size, size)

    def unit_of(n):
        return grads.at[pl.ds(pl.multiple_of(n * UNIT, UNIT), UNIT)]

    def hop(n, kind, source, target, device):
        return pltpu.make_async_remote_copy(
            src_ref=source,
            dst_ref=target,
            send_sem=ar_send.at[n, kind],
            recv_sem=ar_recv.at[n, kind],
            device_id={"dp": device},
            device_id_type=MESH,
        )

    plain = units - 3 * width // UNIT

    class Copies:
        def __init__(self, n):
            self.n = n

        def whole(self):
            first = pl.multiple_of(self.n * UNIT, UNIT)
            return pltpu.make_async_copy(unit_of(self.n), grads_out.at[pl.ds(first, UNIT)], grad_sem.at[self.n])

        def piece(self, q):
            u = self.n - plain
            at = 4 * lax.div(u, 2) + q
            row = pl.multiple_of(lax.div(at, 3) * TILE + lax.rem(u, 2) * UNIT, UNIT)
            return pltpu.make_async_copy(
                unit_of(self.n).at[:, q * width : (q + 1) * width],
                qkv_out.at[lax.rem(at, 3), pl.ds(row, UNIT)],
                grad_sem.at[self.n],
            )

        def start(self):
            pl.when(self.n < plain)(lambda: self.whole().start())

            @pl.when(self.n >= plain)
            def _():
                for q in range(4):
                    self.piece(q).start()

        def wait(self):
            pl.when(self.n < plain)(lambda: self.whole().wait())

            @pl.when(self.n >= plain)
            def _():
                for q in range(4):
                    self.piece(q).wait()

    def kind_of(n):
        return jnp.where(n < LATE, lax.rem(n, 2), 0)

    def box_of(n):
        first = jnp.where(n < LATE, lax.div(n, 2), n - LATE // 2)
        return lax.rem(first, BOXES_X), lax.rem(lax.div(n, 2), BOXES_Z)

    def begin(n):
        place, place_b = box_of(n)
        code = 4 * kind_of(n) + middle

        @pl.when(code < 4)
        def _():
            theirs = unit_of(n).at[pl.ds(rows_of(1 - along_x, half), half)]
            hop(n, 0, theirs, recv_a.at[place, pl.ds(0, half)], across).start()

        @pl.when(code == 4)
        def _():
            hop(n, 0, unit_of(n), recv_b.at[place_b, pl.ds(0, UNIT)], inward).start()

    def advance(n, stage):
        kind = jnp.where(n < 0, 2, jnp.where(n >= units, 2, kind_of(n)))
        code = 4 * kind + middle
        place, place_b = box_of(n)

        def case(number):
            return pl.when(code == number)

        base, box = unit_of(n), recv_a.at[place]
        mine_at, theirs_at = rows_of(along_x, half), rows_of(1 - along_x, half)
        own_at = pl.multiple_of(along_x * half + side * quarter, quarter)
        other_at = pl.multiple_of(along_x * half + (1 - side) * quarter, quarter)
        own_in, other_in = rows_of(side, quarter), rows_of(1 - side, quarter)

        def rows(first, size):
            return base.at[pl.ds(first, size)]

        def x_one():
            return hop(n, 0, rows(theirs_at, half), box.at[pl.ds(0, half)], across)

        def z_one():
            return hop(n, 1, rows(mine_at, half), box.at[pl.ds(half, half)], inward)

        def z_two():
            return hop(n, 2, rows(other_at, quarter), box.at[pl.ds(2 * half, quarter)], inward)

        def z_swap():
            return hop(n, 3, rows(own_at, quarter), box.at[pl.ds(swap_at, quarter)], inward)

        def out(kind, first, place_in):
            return hop(n, kind, rows(first, quarter), box.at[pl.ds(half + place_in, quarter)], outward)

        def x_two():
            return hop(n, 6, rows(mine_at, half), box.at[pl.ds(last_at, half)], across)

        swap_at, last_at = 2 * half + quarter, 3 * half

        if stage == 1:

            @case(0)
            def _():
                x_one().wait_recv()
                add_parts(base, mine_at, half, [(box, 0)])
                z_one().start()

        if stage == 2:

            @case(2)
            def _():
                x_one().wait_recv()
                z_one().wait_recv()
                add_parts(base, other_at, quarter, [(box, other_in), (box, half + other_in)])
                z_two().start()

        if stage == 3:

            @case(2)
            def _():
                z_two().wait_recv()
                add_parts(base, own_at, quarter, [(box, own_in), (box, half + own_in), (box, 2 * half)])
                z_swap().start()
                out(4, own_at, own_in).start()

        if stage == 4:

            @case(2)
            def _():
                z_swap().wait_recv()
                z_two().wait_send()
                bring(base, other_at, box, swap_at, quarter)
                out(5, other_at, other_in).start()
                x_two().start()

        if stage == 5:

            @case(0)
            def _():
                z_one().wait_send()
                out(4, own_at, own_in).wait_recv()
                out(5, other_at, other_in).wait_recv()
                bring(base, mine_at, box, half, half)
                x_two().start()

        if stage == 6:

            @case(2)
            def _():
                z_swap().wait_send()
                out(4, own_at, own_in).wait_send()
                out(5, other_at, other_in).wait_send()

            @pl.when(kind == 0)
            def _():
                x_one().wait_send()
                x_two().wait()
                bring(base, theirs_at, box, last_at, half)

        box_b = recv_b.at[place_b]
        mine_z, theirs_z = rows_of(side, half), rows_of(1 - side, half)
        own_x = pl.multiple_of(side * half + along_x * quarter, quarter)
        other_x = pl.multiple_of(side * half + (1 - along_x) * quarter, quarter)
        own_part_at, other_part_at = rows_of(along_x, quarter), rows_of(1 - along_x, quarter)

        def z_in():
            return hop(n, 0, base, box_b.at[pl.ds(0, UNIT)], inward)

        def z_mid():
            return hop(n, 1, rows(theirs_z, half), box_b.at[pl.ds(UNIT, half)], inward)

        def x_mid():
            return hop(n, 2, rows(other_x, quarter), box_b.at[pl.ds(UNIT + half, quarter)], across)

        def x_swap():
            return hop(n, 3, rows(own_x, quarter), box_b.at[pl.ds(swap_at, quarter)], across)

        def z_share():
            return hop(n, 4, rows(mine_z, half), box_b.at[pl.ds(last_at, half)], inward)

        def z_out(kind, first):
            return hop(n, kind, rows(first, half), box_b.at[pl.ds(first, half)], outward)

        swap_at, last_at = UNIT + half + quarter, 2 * UNIT

        if stage == 1:

            @case(6)
            def _():
                z_in().wait_recv()
                add_parts(base, theirs_z, half, [(box_b, theirs_z)])
                z_mid().start()

        if stage == 2:

            @case(6)
            def _():
                z_mid().wait_recv()
                add_parts(base, other_x, quarter, [(box_b, other_x), (box_b, UNIT + other_part_at)])
                x_mid().start()

        if stage == 3:

            @case(6)
            def _():
                x_mid().wait_recv()
                add_parts(
                    base, own_x, quarter, [(box_b, own_x), (box_b, UNIT + own_part_at), (box_b, UNIT + half)]
                )
                x_swap().start()

        if stage == 4:

            @case(6)
            def _():
                x_swap().wait_recv()
                x_mid().wait_send()
                bring(base, other_x, box_b, swap_at, quarter)
                z_share().start()
                z_out(5, mine_z).start()

        if stage == 5:

            @case(6)
            def _():
                z_share().wait_recv()
                z_mid().wait_send()
                bring(base, theirs_z, box_b, last_at, half)
                z_out(6, theirs_z).start()

        if stage == 6:

            @case(6)
            def _():
                x_swap().wait_send()
                z_share().wait_send()
                z_out(5, mine_z).wait_send()
                z_out(6, theirs_z).wait_send()

            @case(4)
            def _():
                z_in().wait_send()
                z_out(5, mine_z).wait_recv()
                z_out(6, theirs_z).wait_recv()
                bring(base, 0, box_b, 0, UNIT)

            pl.when(kind < 2)(lambda: Copies(n).start())

    def at_ready(n):
        return jnp.where(n < 2, 1, jnp.where(n < plain, 0, jnp.where(n < plain + 2, 1, 0)))

    def ready(first, count):
        for n in (first + k for k in range(count)):
            if reduce_dp:
                pl.when(at_ready(n) == 1)(functools.partial(begin, n))
            else:
                Copies(n).start()

    def tick(t):
        if reduce_dp:
            with jax.named_scope("dp_tick"):
                move(t)

    def move(t):
        for stage in (6, 5, 4, 3, 2, 1):
            advance(t - 2 * (stage - 1), stage)
        later = t + 2

        @pl.when(jnp.where(later >= units, 1, at_ready(later)) == 0)
        def _():
            begin(later)

    def tick_at(j, every, first):
        @pl.when(lax.rem(j, every) == every - 1)
        def _():
            tick(first + lax.div(j, every))

    ticks = units + 10

    def to_mate(which, number):
        return pltpu.make_async_remote_copy(
            src_ref=rs_out.at[lax.rem(number, 2)],
            dst_ref=rs_in.at[number],
            send_sem=rs_send.at[which, number],
            recv_sem=rs_recv.at[which, number],
            device_id={"tensor": mate},
            device_id_type=MESH,
        )

    def to_peer(which, number):
        return pltpu.make_async_remote_copy(
            src_ref=rs_in.at[number],
            dst_ref=y_in.at[number],
            send_sem=rs_send.at[which, 4 + number],
            recv_sem=rs_recv.at[which, 4 + number],
            device_id={"tensor": peer},
            device_id_type=MESH,
        )

    def scatter(j, which, compute):
        owner = jnp.where(j < 2, cross, jnp.where(j < 4, peer, mate))
        number = lax.rem(j, 2)
        row0 = pl.multiple_of(owner * rows_own + number * TILE, TILE)

        @pl.when(lax.div(j, 2) != 1)
        def _():
            at = jnp.where(j < 2, j, j - 2)
            pl.when(j >= 4)(lambda: to_mate(which, number).wait_send())

            def put(columns, part):
                rs_out[number, :, columns] = part.astype(BF)

            compute(row0, put)
            to_mate(which, at).start()

        @pl.when(lax.div(j, 2) == 1)
        def _():
            to_mate(which, number).wait_recv()

            def put(columns, part):
                rs_in[number, :, columns] = (rs_in[number, :, columns].astype(F32) + part).astype(BF)

            compute(row0, put)
            to_peer(which, number).start()

    def gathered(which, number):
        to_mate(which, 2 + number).wait_recv()
        to_peer(which, number).wait_recv()

    def settle(which):
        for number in range(2):
            to_mate(which, 2 + number).wait_send()
            to_peer(which, number).wait_send()

    def stored(number, target):
        return pltpu.make_async_copy(rs_out.at[number], target, result_sem.at[number])

    pltpu.make_async_copy(tok.at[pl.ds(0, rows)], tok_kept, tok_sem.at[0]).wait()
    for piece in range(g_tok.pieces):
        g_tok.forward(peer, piece).wait_send()

    def keep_unit(n, value):
        grads[pl.ds(pl.multiple_of(n * UNIT, UNIT), value.shape[0]), :] = value
        ready(n, value.shape[0] // UNIT)

    per_tile = TILE // UNIT
    first_out = hid.shape[1] // UNIT
    first_up = first_out + width // UNIT

    def arrive(piece):
        g_cot.to_peer(peer, piece).wait_recv()
        g_cot.forward(peer, piece).start()

    def down(piece):
        g_cot.forward(cross, piece).wait_recv()
        tile = dot(cot[:, piece * TILE : (piece + 1) * TILE], hid[...], TN)
        keep_unit(per_tile * piece, tile.astype(BF))

    def mix_some(first, last):
        with jax.named_scope("mixer"):
            lax.fori_loop(first, last, mix, 0)

    pairs = chunks // 2
    with jax.named_scope("grad_down"):
        arrive(0)
        arrive(1)
        down(0)
        down(1)
    mix_some(0, pairs // 4)
    tick(jnp.int32(0))
    arrive(2)
    mix_some(pairs // 4, pairs // 2)
    with jax.named_scope("grad_down"):
        down(2)

    def pause(t, carry):
        tick(t)
        return carry

    lax.fori_loop(1, 3, pause, 0)
    mix_some(pairs // 2, 3 * pairs // 4)
    tick(jnp.int32(3))
    arrive(3)
    mix_some(3 * pairs // 4, pairs)
    with jax.named_scope("grad_down"):
        down(3)
    tick(jnp.int32(4))
    keep_unit(first_out, dot(mixed[...], cot[...], TN).astype(BF))
    tick(jnp.int32(5))

    column_tiles = [slice(at, at + TILE) for at in range(0, cot.shape[1], TILE)]

    def branch(row0, put):
        here = pl.ds(row0, TILE)
        left, right = mixed[here, :], hid[here, :]
        for columns in column_tiles:
            put(columns, dot(left, w_out[:, columns]) + dot(right, w_down[:, columns]))

    def keep_temp(number):
        def put(columns, part):
            temp[number, :, columns] = part

        return put

    def own_copy(number, back=False):
        held = own_part.at[pl.ds(pl.multiple_of(number * TILE, TILE), TILE)]
        if back:
            return pltpu.make_async_copy(held, temp.at[number], temp_sem.at[number])
        return pltpu.make_async_copy(temp.at[0], held, temp_sem.at[0])

    def produce(j, carry):
        @pl.when(j >= 2)
        def _():
            scatter(j - 2, 0, branch)

        @pl.when(j < 2)
        def _():
            branch(pl.multiple_of(me * rows_own + j * TILE, TILE), keep_temp(0))
            own_copy(j).start()
            own_copy(j).wait()

        pl.when(j == 1)(lambda: slope_copy(0, True).start())
        pl.when(j == 2)(lambda: slope_copy(1, True).start())

        @pl.when(lax.div(j, 2) == 1)
        def _():
            tick(4 + j)

        return carry

    with jax.named_scope("outputs"):
        lax.fori_loop(0, 8, produce, 0)
    bring_up = pltpu.make_async_copy(
        grads.at[pl.ds(rows, 2 * rows_own)], hid.at[pl.ds(chip_row, 2 * rows_own)], tok_sem.at[0]
    )
    bring_up.start()

    def descend(p, carry):
        here = [pl.ds(pl.multiple_of(owner * rows_own + p * UNIT, UNIT), UNIT) for owner in (peer, cross)]
        parity = lax.rem(p, 2)
        slope_copy(p, True).wait()
        turned = wide([cot[at, :] for at in here], 0)
        for at in range(0, hid.shape[1], TILE):
            d_hidden = dot(turned, w_down[at : at + TILE, :], NT)
            d_up = (d_hidden * temp[parity, :, at : at + TILE]).astype(BF)
            for k, rows_at in enumerate(here):
                hid[rows_at, at : at + TILE] = d_up[k * UNIT : (k + 1) * UNIT]
        pl.when(p < 2)(lambda: slope_copy(p + 2, True).start())
        return carry

    with jax.named_scope("grad_gelu"):
        lax.fori_loop(0, 4, descend, 0)
    bring_up.wait()

    def upward(j, carry):
        at = pl.ds(pl.multiple_of(j * TILE, TILE), TILE)
        keep_unit(first_up + per_tile * j, dot(n_two[:, at], hid[...], TN).astype(BF))
        tick_at(j, 2, 8)
        return carry

    with jax.named_scope("grad_up"):
        lax.fori_loop(0, n_two.shape[1] // TILE, upward, 0)

    state[...] = jnp.zeros_like(state)
    krow[...] = jnp.zeros_like(krow)
    feat_sums[...] = jnp.zeros_like(feat_sums)

    def unmix(step, carry):
        pair = chunks // 2 - 1 - step
        diag = diag_two[0:width, :].astype(F32)
        row_pair = pl.multiple_of(pair * 2 * CHUNK, 2 * CHUNK)
        d_mixed = dot(cot[pl.ds(row_pair, 2 * CHUNK), :], w_out[...], NT)
        here = chunk_rows(pair)
        query, key, value = ([fqkv[at, s * width : (s + 1) * width] for at in here] for s in range(3))
        d_over, under_parts = [], []
        for c in both_chunks:
            packed = rden[here[c], :]
            inverse = wide(
                [packed[:, h // 2 * HEAD_DIM // 2 : (h // 2 + 1) * HEAD_DIM // 2] for h in range(2 * heads)]
            )
            d_over.append(d_mixed[c * CHUNK : (c + 1) * CHUNK] * inverse)
            under_parts.append(wide(split(d_over[c] * att[here[c], :])))
        d_under = [-dot(under_parts[c], diag_two[...]) for c in both_chunks]
        under_row = [-dot(wide([head_rows, head_rows]), under_parts[c], NT) for c in both_chunks]
        over_split = [split(d_over[c]) for c in both_chunks]
        over_both = [wide(over_split[c]) for c in both_chunks]
        over_heads = [wide([per_head(part) for part in over_split[c]]) for c in both_chunks]
        query_heads, key_heads, value_heads = ([per_head(field[c]) for c in both_chunks] for field in (query, key, value))
        scores_back = [(dot(key[c], query_heads[c], NT) * causal_back).astype(BF) for c in both_chunks]
        d_scores = [dot(over_both[c], wide([value_heads[c]] * 2), NT) for c in both_chunks]
        d_back = [dot(wide([value[c]] * 2), over_heads[c], NT) for c in both_chunks]
        turned = [query[c].T for c in both_chunks]
        made = []
        for c in both_chunks:
            for k in both_blocks:
                left = turned[c][:, k * BLOCK : (k + 1) * BLOCK]
                made.append(dot(wide([left, left]), wide([halves(part)[k] for part in over_split[c]], 0)) * diag)
        d_scores = [
            wide(
                split(
                    (
                        d_scores[c]
                        + wide(
                            [
                                jnp.broadcast_to(d_under[c][:, h * HEAD_DIM : h * HEAD_DIM + 1], (CHUNK, CHUNK))
                                for h in range(heads)
                            ]
                        )
                    )
                    * causal
                )
            )
            for c in both_chunks
        ]
        d_back = [
            wide(split((d_back[c] + wide([under_row[c][h : h + 1, :] for h in range(heads)])) * causal_back))
            for c in both_chunks
        ]
        d_query = [dot(d_scores[c], wide([key_heads[c]] * 2, 0)) for c in both_chunks]
        d_key = [dot(d_back[c], wide([query_heads[c]] * 2, 0)) for c in both_chunks]
        d_value = [dot(scores_back[c], over_heads[c]) for c in both_chunks]
        later, later_row = state[...], krow[0:1, :]
        more = {}
        for at in reversed(range(4)):
            c, k = divmod(at, 2)
            block = 4 * pair + at
            query_k, key_k, value_k, both_k, under_k = (
                halves(field[c])[k] for field in (query, key, value, over_both, d_under)
            )
            carried = wide([states[block]] * heads, 0) * diag_two[0:width, :]
            keep = joined(block + 1)
            later, later_row = later * keep, later_row * keep
            high, low = split(later)
            more[at] = (
                dot(both_k, wide([carried, carried]), NT) + under_k * ksums[pl.ds(block, 1), :],
                dot(wide([value_k, value_k]), wide([high, low]), NT) + later_row,
                dot(wide([key_k, key_k]), wide([high, low], 0)),
            )
            later = later + made[at]
            later_row = later_row + jnp.sum(query_k.astype(F32) * under_k, 0, keepdims=True)
        state[...] = later
        krow[0:1, :] = later_row
        turn = rotation(row_pair, 2 * CHUNK // BLOCK)
        here = pl.ds(row_pair, 2 * CHUNK)
        for s, found in enumerate((d_query, d_key)):
            grad = wide(found, 0) + wide([more[at][s] for at in range(4)], 0)
            spectrum = spec[s, here, :]
            grad = grad * (weight_row * jnp.exp(scale_row * spectrum))
            feat_sums[0:1, :] += jnp.sum(grad * spectrum, 0, keepdims=True)
            feat_sums[1:2, :] += jnp.sum(grad, 0, keepdims=True)
            high, low = split(grad * scale_row)
            back = dot(high, dct[:, 0:width]) + dot(low, dct[:, 0:width]) + dot(high, dct[:, 2 * width :])
            fqkv[here, s * width : (s + 1) * width] = rotate(back, turn, True).astype(BF)
        d_value = wide([d_value[c][:, :width] + d_value[c][:, width:] for c in both_chunks], 0)
        fqkv[here, 2 * width : 3 * width] = (d_value + wide([more[at][2] for at in range(4)], 0)).astype(BF)
        tick(10 + step)

        return carry

    with jax.named_scope("mixer_back"):
        lax.fori_loop(0, chunks // 2, unmix, 0)

    def own_tok(number):
        return pltpu.make_async_copy(tok_in.at[pl.ds(number * TILE, TILE)], rs_out.at[number], result_sem.at[number])

    settle(0)
    for number in range(2):
        own_copy(number, True).start()
        own_tok(number).start()

    for j in range(n_one.shape[1] // TILE):
        tile = dot(n_one[:, j * TILE : (j + 1) * TILE], fqkv[...], TN).astype(BF)
        for s in range(3):
            at = 3 * j + s
            first = plain * UNIT + at // 4 * TILE
            grads[first : first + TILE, at % 4 * width : (at % 4 + 1) * width] = tile[:, s * width : (s + 1) * width]
        if j:
            ready(plain + (j - 1) * per_tile, per_tile)


    tick(jnp.int32(18))

    sums[...] = jnp.zeros_like(sums)

    def row_of(j):
        owner = jnp.where(j < 2, cross, jnp.where(j < 4, peer, jnp.where(j < 6, mate, me)))
        return pl.multiple_of(owner * rows_own + lax.rem(j, 2) * TILE, TILE)

    def tok_copy(j):
        which = lax.rem(j, 2)
        return pltpu.make_async_copy(
            tok_kept.at[pl.ds(row_of(j), TILE)], n_two.at[pl.ds(pl.multiple_of(which * TILE, TILE), TILE)], tok_sem.at[which]
        )

    def row_grads(j):
        def compute(row0, put):
            here = pl.ds(row0, TILE)
            unit, _ = unit_rows(n_two[pl.ds(pl.multiple_of(lax.rem(j, 2) * TILE, TILE), TILE), :].astype(F32))
            fields = [fqkv[here, s * width : (s + 1) * width] for s in range(3)]
            right = hid[here, :]
            for columns in column_tiles:
                one = sum(dot(fields[s], w_qkv[s, columns, :], NT) for s in range(3))
                two = dot(right, w_up[columns, :], NT)
                part = unit[:, columns]
                for number, term in enumerate((one * part, one, two * part, two)):
                    sums[number, :, columns] += jnp.sum(term.reshape(TILE // 8, 8, TILE), 0)
                put(columns, one * gain_one[:, columns] + two * gain_two[:, columns])

        return compute

    def finish(number, carry):
        own_copy(number, True).wait()
        own_tok(number).wait()
        gathered(0, number)

        def step(i, inner):
            at = pl.ds(pl.multiple_of(i * SUB, SUB), SUB)
            total = temp[number, at, :] + rs_in[2 + number, at, :].astype(F32) + y_in[number, at, :].astype(F32)
            rs_out[number, at, :] = (total + rs_out[number, at, :].astype(F32)).astype(BF)
            return inner

        lax.fori_loop(0, TILE // SUB, step, 0)
        stored(number, mixed_out.at[pl.ds(pl.multiple_of(number * TILE, TILE), TILE)]).start()
        return carry

    with jax.named_scope("finish"):
        lax.fori_loop(0, 2, finish, 0)
    pl.semaphore_signal(free_mate, inc=1, device_id={"tensor": mate}, device_id_type=MESH)
    pl.semaphore_signal(free_peer, inc=1, device_id={"tensor": peer}, device_id_type=MESH)
    tok_copy(0).start()
    for number in range(2):
        stored(number, mixed_out.at[pl.ds(0, TILE)]).wait()
    pl.semaphore_wait(free_mate, 1)
    pl.semaphore_wait(free_peer, 1)

    def inputs(j, carry):
        tok_copy(j).wait()
        pl.when(j < 7)(lambda: tok_copy(j + 1).start())

        @pl.when(j < 6)
        def _():
            scatter(j, 1, row_grads(j))

        @pl.when(j >= 6)
        def _():
            row_grads(j)(row_of(j), keep_temp(lax.rem(j, 2)))

        tick(19 + j)
        return carry

    with jax.named_scope("row_grads"):
        lax.fori_loop(0, 8, inputs, 0)
    settle(1)
    for number in range(2):
        own_tok(number).start()

    def conclude(number):
        own_tok(number).wait()
        gathered(1, number)

        def step(i, inner):
            at = pl.ds(pl.multiple_of(i * SUB, SUB), SUB)
            group_at = pl.multiple_of(me * rows_own + number * TILE + i * SUB, SUB)
            unit, deviation = unit_rows(rs_out[number, at, :].astype(F32))
            total = temp[number, at, :] + rs_in[2 + number, at, :].astype(F32) + y_in[number, at, :].astype(F32)
            along = jnp.mean(total * unit, -1, keepdims=True)
            total = total - jnp.mean(total, -1, keepdims=True) - unit * along
            total = cot[pl.ds(group_at, SUB), :].astype(F32) + deviation * total
            rs_out[number, at, :] = total.astype(BF)
            return inner

        lax.fori_loop(0, TILE // SUB, step, 0)
        stored(number, input_grad.at[pl.ds(number * TILE, TILE)]).start()

    small[...] = jnp.zeros_like(small)
    for number in range(4):
        small[number : number + 1, :] = jnp.sum(sums[number], 0, keepdims=True)
    small[4:5, 0:width] = feat_sums[0:1, :]
    small[5:6, 0:width] = feat_sums[1:2, :] / weight_row

    def small_hops(axis, own, count, boxes, first):
        hops = []
        for step in range(1, count):
            hops.append(
                pltpu.make_async_remote_copy(
                    src_ref=small,
                    dst_ref=boxes.at[own],
                    send_sem=small_send.at[first + step - 1],
                    recv_sem=small_recv.at[first + step - 1],
                    device_id={axis: lax.rem(own + step, count)},
                    device_id_type=MESH,
                )
            )
        return hops

    over_tensor = small_hops("tensor", me, 4, small_in, 0)
    over_dp = small_hops("dp", group, members, small_wide, 3)

    def small_step(k):
        if k == 0:
            for copy in over_tensor:
                copy.start()
            small_in[me] = small[...]
        if k == 1:
            for copy in over_tensor:
                copy.wait()
            total = small_in[0]
            for member in range(1, 4):
                total = total + small_in[member]
            small[0:4, :] = total[0:4, :]
        if k == 1 and reduce_dp:
            for copy in over_dp:
                copy.start()
            small_wide[group] = small[...]
        if k == 2 and reduce_dp:
            for copy in over_dp:
                copy.wait()
            total = small_wide[0]
            for member in range(1, members):
                total = total + small_wide[member]
            small[...] = total

    settle_at, late = 28, {27: 0, 29: 1, 32: 2}
    if reduce_dp:

        def rest(t, carry):
            for at, k in late.items():
                pl.when(t == at)(functools.partial(small_step, k))
            for number in range(2):

                @pl.when(t == settle_at + 2 * number)
                def _():
                    conclude(number)

            tick(t)
            return carry

        lax.fori_loop(27, ticks, rest, 0)
    else:
        for k in range(2):
            small_step(k)
        for number in range(2):
            conclude(number)
    for h in range(heads):
        at = slice(h * HEAD_DIM, (h + 1) * HEAD_DIM)
        feat_out[0, h : h + 1, :] = small[4:5, at]
        feat_out[1, h : h + 1, :] = small[5:6, at]

    def copied(n, carry):
        Copies(n).wait()
        return carry

    lax.fori_loop(0, units, copied, 0)
    for number in range(2):
        stored(number, input_grad.at[pl.ds(0, TILE)]).wait()

    for gather in (g_tok, g_cot):
        gather.to_mate(me).wait_send()
        for piece in range(gather.pieces):
            gather.to_peer(me, piece).wait_send()
    for piece in range(g_cot.pieces):
        g_cot.forward(peer, piece).wait_send()


def widen(down_in, out_in, up_in, qkv_in, *outs):
    down, out, up, qkv = outs
    down[...] = down_in[...].astype(F32).T
    out[...] = out_in[...].astype(F32)
    up[...] = up_in[...].astype(F32)
    qkv[...] = qkv_in[...].astype(F32)


def shards(
    reduce_dp,
    tokens,
    ln1_gain,
    ln1_bias,
    ln2_gain,
    ln2_bias,
    w_qkv,
    w_out,
    w_up,
    w_down,
    feature_scale,
    feature_weight,
    lengths,
    cotangent,
):
    rows_own, model = tokens.shape
    rows = 4 * rows_own
    heads = feature_scale.shape[0]
    width = heads * HEAD_DIM
    hidden = w_up.shape[1]
    consts = tables(rows // BLOCK, heads)
    norms = [value.reshape(1, model) for value in (ln1_gain, ln1_bias, ln2_gain, ln2_bias)]
    anywhere = pl.BlockSpec(memory_space=pl.ANY)
    vmem = pl.BlockSpec(memory_space=pltpu.VMEM)
    smem = pl.BlockSpec(memory_space=pltpu.SMEM)
    shape = jax.ShapeDtypeStruct
    plain = 2 * hidden + width
    units = (plain + 3 * width) // UNIT
    mixed_out, input_grad, grads, g_qkv, _, _, _, small, feats = pl.pallas_call(
        functools.partial(kernel, reduce_dp),
        out_shape=(
            shape((rows_own, model), BF),
            shape((rows_own, model), BF),
            shape((plain, model), BF),
            shape((3, model, width), BF),
            shape((rows // 2, hidden), F32),
            shape((rows_own, model), F32),
            shape((rows, model), BF),
            shape((8, model), F32),
            shape((2, heads, HEAD_DIM), F32),
        ),
        in_specs=[smem, anywhere, anywhere] + [vmem] * 4 + [anywhere] * 4 + [vmem] * 6,
        out_specs=(anywhere,) * 7 + (vmem, vmem),
        scratch_shapes=[
            pltpu.VMEM((rows, model), BF),
            pltpu.VMEM((rows, model), BF),
            pltpu.VMEM((rows, model), BF),
            pltpu.VMEM((rows, hidden), BF),
            pltpu.VMEM((rows, 3 * width), BF),
            pltpu.VMEM((2, rows, width), F32),
            pltpu.VMEM((rows, width), BF),
            pltpu.VMEM((rows, width), F32),
            pltpu.VMEM((rows, width // 2), F32),
            pltpu.VMEM((rows // BLOCK, HEAD_DIM, width), BF),
            pltpu.VMEM((rows // BLOCK, width), F32),
            pltpu.VMEM((width, width), F32),
            pltpu.VMEM((8, width), F32),
            pltpu.VMEM((units * UNIT, model), BF),
            pltpu.VMEM((BOXES_X, 2 * UNIT, model), BF),
            pltpu.VMEM((BOXES_Z, 5 * UNIT // 2, model), BF),
            pltpu.VMEM((2, TILE, model), BF),
            pltpu.VMEM((4, TILE, model), BF),
            pltpu.VMEM((2, TILE, model), BF),
            pltpu.VMEM((2, TILE, model), F32),
            pltpu.VMEM((4, 8, model), F32),
            pltpu.VMEM((8, width), F32),
            pltpu.VMEM((4, 8, model), F32),
            pltpu.VMEM((8, 8, model), F32),
            pltpu.VMEM(w_qkv.shape, BF),
            pltpu.VMEM(w_out.shape, BF),
            pltpu.VMEM(w_up.shape, BF),
            pltpu.VMEM(w_down.shape, BF),
            pltpu.SemaphoreType.DMA((2 + 2 * rows_own // UNIT,)),
            pltpu.SemaphoreType.DMA((2 + 2 * rows_own // UNIT + 2 * model // TILE,)),
            pltpu.SemaphoreType.DMA((2 + 2 * rows_own // UNIT + 2 * model // TILE,)),
            pltpu.SemaphoreType.DMA((4,)),
            pltpu.SemaphoreType.DMA((units, 7)),
            pltpu.SemaphoreType.DMA((units, 7)),
            pltpu.SemaphoreType.DMA((2, 6)),
            pltpu.SemaphoreType.DMA((2, 6)),
            pltpu.SemaphoreType.DMA((10,)),
            pltpu.SemaphoreType.DMA((10,)),
            pltpu.SemaphoreType.DMA((units,)),
            pltpu.SemaphoreType.DMA((2,)),
            pltpu.SemaphoreType.DMA((2,)),
            pltpu.SemaphoreType.DMA((2,)),
            pltpu.SemaphoreType.REGULAR,
            pltpu.SemaphoreType.REGULAR,
        ],
        compiler_params=pltpu.CompilerParams(
            collective_id=0, has_side_effects=True, vmem_limit_bytes=62 * 2**20
        ),
    )(lengths, tokens, cotangent, *norms, w_qkv, w_out, w_up, w_down, feature_scale, feature_weight, *consts)
    norm_sums = small[0:4]
    if not reduce_dp:
        grads, g_qkv, norm_sums, feats = lax.psum(
            (*lax.optimization_barrier((grads.astype(F32), g_qkv.astype(F32))), norm_sums, feats), "dp"
        )
    steps = 8
    down_cut, out_cut, up_cut, row_cut = hidden // steps, width // steps, model // steps, model // steps
    g_down, g_out, g_up, g_qkv = pl.pallas_call(
        widen,
        grid=(steps,),
        out_shape=(
            shape((hidden, model), F32),
            shape((width, model), F32),
            shape((model, hidden), F32),
            shape((3, model, width), F32),
        ),
        in_specs=[
            pl.BlockSpec((model, down_cut), lambda i: (0, i)),
            pl.BlockSpec((out_cut, model), lambda i: (hidden // out_cut + i, 0)),
            pl.BlockSpec((up_cut, hidden), lambda i: ((hidden + width) // up_cut + i, 0)),
            pl.BlockSpec((3, row_cut, width), lambda i: (0, i, 0)),
        ],
        out_specs=(
            pl.BlockSpec((down_cut, model), lambda i: (i, 0)),
            pl.BlockSpec((out_cut, model), lambda i: (i, 0)),
            pl.BlockSpec((up_cut, hidden), lambda i: (i, 0)),
            pl.BlockSpec((3, row_cut, width), lambda i: (0, i, 0)),
        ),
        compiler_params=pltpu.CompilerParams(vmem_limit_bytes=24 * 2**20),
    )(grads, grads, grads, g_qkv)
    return (
        mixed_out,
        input_grad,
        norm_sums[0],
        norm_sums[1],
        norm_sums[2],
        norm_sums[3],
        g_qkv,
        g_out,
        g_up,
        g_down,
        feats[0],
        feats[1],
    )


def solution(mesh):
    placed = (
        P(("dp", "tensor"), None),
        P(),
        P(),
        P(),
        P(),
        P(None, None, "tensor"),
        P("tensor", None),
        P(None, "tensor"),
        P("tensor", None),
        P("tensor", None),
        P("tensor", None),
        P("dp", None),
        P(("dp", "tensor"), None),
    )
    return jax.shard_map(
        functools.partial(shards, mesh.shape["dp"] == 8),
        mesh=mesh,
        in_specs=placed,
        out_specs=(
            P(("dp", "tensor"), None),
            P(("dp", "tensor"), None),
            P(),
            P(),
            P(),
            P(),
            P(None, None, "tensor"),
            P("tensor", None),
            P(None, "tensor"),
            P("tensor", None),
            P("tensor", None),
            P("tensor", None),
        ),
        check_vma=False,
    )
```

```python
import functools
import math

import jax
import jax.numpy as jnp
import ml_dtypes
import numpy as np
from jax import lax
from jax.experimental import pallas as pl
from jax.experimental.pallas import tpu as pltpu
from jax.sharding import PartitionSpec as P

HEAD_DIM = 64
ROT = 16
BLOCK = 64
CHUNK = 128
TILE = 256
PIECE = 128
UNIT = 64
SUB = 32
LEAD = 2
LAG = 2
BOXES_X = 12
BOXES_Z = 6
LATE = 36
MESH = pl.DeviceIdType.MESH
F32 = jnp.float32
BF = jnp.bfloat16
NN = (((1,), (0,)), ((), ()))
NT = (((1,), (1,)), ((), ()))
TN = (((0,), (0,)), ((), ()))


def dot(left, right, dims=NN):
    return lax.dot_general(left, right, dims, preferred_element_type=F32)


def split(value):
    high = value.astype(BF)
    return high, (value - high.astype(F32)).astype(BF)


def wide(parts, axis=1):
    return jnp.concatenate(parts, axis)


def tables(blocks, heads):
    width = heads * HEAD_DIM
    freq, dims = np.arange(HEAD_DIM)[:, None], np.arange(HEAD_DIM)[None, :]
    dct = np.cos(np.pi * (dims + 0.5) * freq / HEAD_DIM) * math.sqrt(2.0 / HEAD_DIM)
    dct[0] *= math.sqrt(0.5)
    dct = np.kron(np.eye(heads), dct).astype(np.float32)
    high = dct.astype(ml_dtypes.bfloat16)
    low = (dct - high.astype(np.float32)).astype(ml_dtypes.bfloat16)
    halves = np.concatenate([high, high, low], 1)
    half = ROT // 2
    lane = np.arange(2 * HEAD_DIM) % HEAD_DIM
    rate = np.where(lane < ROT, 10000.0 ** (-(lane % half) * 2.0 / ROT), 0.0)
    in_block = np.arange(BLOCK)[:, None] * rate[None]
    of_block = np.arange(blocks)[:, None] * BLOCK * rate[None]
    signs = np.stack([np.where(lane < half, -1.0, 0.0), np.where((lane >= half) & (lane < ROT), 1.0, 0.0)] + [0.0 * lane] * 6)
    angles = np.concatenate([np.cos(in_block), np.sin(in_block), np.cos(of_block), np.sin(of_block), signs], 0)
    diagonal = np.kron(np.eye(heads), np.ones((HEAD_DIM, HEAD_DIM)))
    masks = np.kron(np.eye(heads), np.ones((CHUNK, HEAD_DIM)))
    return (
        halves,
        angles.astype(np.float32),
        np.concatenate([diagonal, diagonal], 0).astype(ml_dtypes.bfloat16),
        masks.astype(ml_dtypes.bfloat16),
    )


def kernel(
    reduce_dp,
    lengths,
    tok_in,
    cot_in,
    gain_one_in,
    bias_one_in,
    gain_two_in,
    bias_two_in,
    w_qkv_in,
    w_out_in,
    w_up_in,
    w_down_in,
    feature_scale,
    feature_weight,
    dct,
    angles,
    diag_two,
    masks,
    mixed_out,
    input_grad,
    grads_out,
    qkv_out,
    slopes,
    own_part,
    tok_kept,
    small,
    feat_out,
    cot,
    n_one,
    n_two,
    hid,
    fqkv,
    spec,
    mixed,
    att,
    rden,
    states,
    ksums,
    state,
    krow,
    grads,
    recv_a,
    recv_b,
    rs_out,
    rs_in,
    y_in,
    temp,
    sums,
    feat_sums,
    small_in,
    small_wide,
    w_qkv,
    w_out,
    w_up,
    w_down,
    local_sem,
    send_sem,
    recv_sem,
    weight_sem,
    ar_send,
    ar_recv,
    rs_send,
    rs_recv,
    small_send,
    small_recv,
    grad_sem,
    temp_sem,
    tok_sem,
    result_sem,
    free_mate,
    free_peer,
):
    rows_own = tok_in.shape[0]
    rows = cot.shape[0]
    tok = grads
    width = w_out_in.shape[0]
    heads = width // HEAD_DIM
    chunks = rows // CHUNK
    me = lax.axis_index("tensor")
    core = lax.rem(me, 2)
    mate = me + 1 - 2 * core
    peer = lax.rem(me + 2, 4)
    cross = 3 - me
    group = lax.axis_index("dp")
    along_x = lax.rem(group, 2)
    across = group + 1 - 2 * along_x
    along_z = lax.div(group, 2)
    middle = along_z * (3 - along_z)

    def at_end(step):
        pl.when(middle == 0)(step)

    def at_mid(step):
        pl.when(middle > 0)(step)

    side = jnp.where(along_z < 2, 0, 1)
    inward = group + 2 - 4 * side
    outward = group - 2 + 4 * side
    units = grads.shape[0] // UNIT

    weight_copies = [
        pltpu.make_async_copy(source, target, weight_sem.at[k])
        for k, (source, target) in enumerate(
            ((w_qkv_in, w_qkv), (w_up_in, w_up), (w_out_in, w_out), (w_down_in, w_down))
        )
    ]
    for copy in weight_copies:
        copy.start()

    barrier = pltpu.get_barrier_semaphore()
    members = 8 if reduce_dp else 1
    for step in range(1, 4):
        other = lax.rem(me + step, 4)
        pl.semaphore_signal(barrier, inc=1, device_id={"tensor": other}, device_id_type=MESH)
    for step in range(1, members):
        other = lax.rem(group + step, members)
        pl.semaphore_signal(barrier, inc=1, device_id={"dp": other}, device_id_type=MESH)
    pl.semaphore_wait(barrier, 2 + members)

    def slot(buf, owner, piece=None, columns=False):
        if piece is None:
            return buf.at[pl.ds(pl.multiple_of(owner * rows_own, rows_own), rows_own)]
        if columns:
            here = pl.ds(pl.multiple_of(owner * rows_own, rows_own), rows_own)
            return buf.at[here, piece * TILE : (piece + 1) * TILE]
        return buf.at[pl.ds(pl.multiple_of(owner * rows_own + piece * PIECE, PIECE), PIECE)]

    class Gather:
        def __init__(self, source, buf, base, columns):
            self.source, self.buf, self.base, self.columns = source, buf, base, columns
            self.pieces = source.shape[1] // TILE if columns else source.shape[0] // PIECE

        def copy(self, number, src, dst, target):
            return pltpu.make_async_remote_copy(
                src_ref=src,
                dst_ref=dst,
                send_sem=send_sem.at[self.base + number],
                recv_sem=recv_sem.at[self.base + number],
                device_id={"tensor": target},
                device_id_type=MESH,
            )

        def local(self):
            return pltpu.make_async_copy(self.source, slot(self.buf, me), local_sem.at[self.base])

        def to_mate(self, owner):
            return self.copy(0, self.source, slot(self.buf, owner), mate)

        def to_peer(self, owner, piece):
            if self.columns:
                part = self.source.at[:, piece * TILE : (piece + 1) * TILE]
            else:
                part = self.source.at[pl.ds(piece * PIECE, PIECE)]
            return self.copy(1 + piece, part, slot(self.buf, owner, piece, self.columns), peer)

        def forward(self, owner, piece):
            part = slot(self.buf, owner, piece, self.columns)
            return self.copy(1 + self.pieces + piece, part, part, mate)

    g_tok, g_cot = Gather(tok_in, tok, 0, False), Gather(cot_in, cot, 1 + 2 * (rows_own // PIECE), True)
    g_tok.to_mate(me).start()
    for piece in range(g_tok.pieces):
        g_tok.to_peer(me, piece).start()
    g_tok.local().start()
    g_cot.to_mate(me).start()
    g_cot.local().start()

    start_one = lengths[0, 0]
    start_two = start_one + lengths[0, 1]

    def segment(block):
        return (block >= start_one).astype(jnp.int32) + (block >= start_two).astype(jnp.int32)

    def in_sequence(block):
        return block - jnp.where(block >= start_two, start_two, jnp.where(block >= start_one, start_one, 0))

    gain_one, bias_one, gain_two, bias_two = gain_one_in[...], bias_one_in[...], gain_two_in[...], bias_two_in[...]
    scale_row, weight_row = (
        wide([field[h : h + 1, :] for h in range(heads)]) for field in (feature_scale, feature_weight)
    )
    blocks = rows // BLOCK

    def rotation(row0, count):
        cos_in, sin_in = angles[0:BLOCK, :], angles[BLOCK : 2 * BLOCK, :]
        sign_a = angles[2 * BLOCK + 2 * blocks : 2 * BLOCK + 2 * blocks + 1, :]
        sign_b = angles[2 * BLOCK + 2 * blocks + 1 : 2 * BLOCK + 2 * blocks + 2, :]
        cosines, sines = [], []
        for k in range(count):
            place = in_sequence(lax.div(row0, BLOCK) + k)
            cos_at = angles[pl.ds(2 * BLOCK + place, 1), :]
            sin_at = angles[pl.ds(2 * BLOCK + blocks + place, 1), :]
            cosines.append(cos_in * cos_at - sin_in * sin_at)
            sines.append(sin_in * cos_at + cos_in * sin_at)
        cosine, sine = wide(cosines, 0), wide(sines, 0)
        return cosine, sine * sign_a, sine * sign_b

    def rotate(field, turn, back=False):
        cosine, sine_a, sine_b = turn
        parts = []
        for at in range(0, width, 2 * HEAD_DIM):
            part = field[:, at : at + 2 * HEAD_DIM]
            ahead = pltpu.roll(part, 2 * HEAD_DIM - ROT // 2, 1) * sine_a
            behind = pltpu.roll(part, ROT // 2, 1) * sine_b
            parts.append(part * cosine - (ahead + behind) if back else part * cosine + (ahead + behind))
        return wide(parts)

    def unit_rows(value):
        value = value - jnp.mean(value, -1, keepdims=True)
        deviation = lax.rsqrt(jnp.mean(value * value, -1, keepdims=True) + 1e-05)
        return value * deviation, deviation

    chip_row = pl.multiple_of(lax.div(me, 2) * 2 * rows_own, rows_own)

    def slope_copy(p, back=False):
        held = slopes.at[pl.ds(pl.multiple_of(p * TILE, TILE), TILE)]
        slot_of = temp.at[lax.rem(p, 2)]
        return pltpu.make_async_copy(*((held, slot_of) if back else (slot_of, held)), temp_sem.at[lax.rem(p, 2)])

    def project(j, carry):
        @pl.when(j == 0)
        def _():
            g_tok.local().wait()

            g_cot.local().wait()

        @pl.when(j == 2)
        def _():
            g_tok.to_mate(mate).wait_recv()
            g_cot.to_mate(mate).wait_recv()

        for piece in range(g_tok.pieces):

            @pl.when(j == 4 + piece)
            def _():
                g_tok.to_peer(peer, piece).wait_recv()
                g_tok.forward(peer, piece).start()
                g_cot.to_peer(me, piece).start()
                g_tok.forward(cross, piece).wait_recv()

        late = lax.div(j, 4)
        early_at = jnp.where(j < 2, me, mate) * rows_own + lax.rem(j, 2) * TILE
        row_a = pl.multiple_of(jnp.where(late == 0, early_at, peer * rows_own + (j - 4) * PIECE), PIECE)
        row_b = pl.multiple_of(jnp.where(late == 0, early_at + PIECE, cross * rows_own + (j - 4) * PIECE), PIECE)
        here = [pl.ds(row_a, PIECE), pl.ds(row_b, PIECE)]

        for at in here:
            pltpu.make_async_copy(tok.at[at], tok_kept.at[at], tok_sem.at[0]).start()
        unit, _ = unit_rows(wide([tok[at, :] for at in here], 0).astype(F32))
        first = (unit * gain_one + bias_one).astype(BF)
        second = (unit * gain_two + bias_two).astype(BF)
        for k, at in enumerate(here):
            n_one[at, :] = first[k * PIECE : (k + 1) * PIECE]
            n_two[at, :] = second[k * PIECE : (k + 1) * PIECE]
        turn = [wide(pair, 0) for pair in zip(*(rotation(at, PIECE // BLOCK) for at in (row_a, row_b)))]

        def keep(write, value):
            for k, at in enumerate(here):
                write(at, value[k * PIECE : (k + 1) * PIECE])

        def keep_field(s, value):
            def write(at, part):
                fqkv[at, s * width : (s + 1) * width] = part

            keep(write, value.astype(BF))

        for s in range(2):
            high, low = split(rotate(dot(first, w_qkv[s]), turn))
            spectrum = dot(wide([high, low]), dct[:, 0 : 2 * width], NT) + dot(high, dct[:, 2 * width :], NT)

            def keep_spectrum(at, part):
                spec[s, at, :] = part

            keep(keep_spectrum, spectrum)
            keep_field(s, weight_row * jnp.exp(scale_row * spectrum))
        keep_field(2, dot(first, w_qkv[2]))
        parity = lax.rem(j, 2)
        pl.when(j >= 6)(lambda: slope_copy(j - 6).wait())
        for at in range(0, w_up.shape[1], TILE):
            up = dot(second, w_up[:, at : at + TILE])
            below = 0.5 * (1.0 + lax.erf(up * math.sqrt(0.5)))

            def keep_hidden(rows_at, part):
                hid[rows_at, at : at + TILE] = part

            keep(keep_hidden, (up * below).astype(BF))
            temp[parity, :, at : at + TILE] = below + up * (
                jnp.exp(-0.5 * up * up) * (1.0 / math.sqrt(2.0 * math.pi))
            )

        @pl.when(late == 0)
        def _():
            turned = wide([cot[at, :] for at in here], 0)
            first_at = pl.multiple_of(rows + row_a - chip_row, TILE)
            for at in range(0, hid.shape[1], TILE):
                d_hidden = dot(turned, w_down[at : at + TILE, :], NT)
                grads[pl.ds(first_at, TILE), at : at + TILE] = (d_hidden * temp[parity, :, at : at + TILE]).astype(BF)

        pl.when(late == 1)(lambda: slope_copy(j - 4).start())
        return carry

    for copy in weight_copies:
        copy.wait()
    with jax.named_scope("project"):
        lax.fori_loop(0, rows // TILE, project, 0)
    for p in (2, 3):
        slope_copy(p).wait()

    grid_t = lax.broadcasted_iota(jnp.int32, (CHUNK, CHUNK), 0)
    grid_s = lax.broadcasted_iota(jnp.int32, (CHUNK, CHUNK), 1)
    together = (grid_t < BLOCK) == (grid_s < BLOCK)
    causal = wide([jnp.where((grid_t >= grid_s) & together, 1.0, 0.0).astype(F32)] * heads)
    causal_back = wide([jnp.where((grid_t <= grid_s) & together, 1.0, 0.0).astype(F32)] * heads)
    head_rows = jnp.where(
        lax.broadcasted_iota(jnp.int32, (8, width), 0) == lax.div(lax.broadcasted_iota(jnp.int32, (8, width), 1), HEAD_DIM),
        1.0,
        0.0,
    ).astype(BF)
    both_chunks = range(2)
    both_blocks = range(CHUNK // BLOCK)

    def joined(block):
        return jnp.where(segment(block) == segment(block - 1), jnp.float32(1.0), jnp.float32(0.0))

    def per_head(value):
        return wide([value * masks[h * CHUNK : (h + 1) * CHUNK, :] for h in range(heads)], 0)

    def halves(value):
        return [value[k * BLOCK : (k + 1) * BLOCK] for k in both_blocks]

    def chunk_rows(pair):
        return [pl.ds(pl.multiple_of((2 * pair + c) * CHUNK, CHUNK), CHUNK) for c in both_chunks]

    state[...] = jnp.zeros_like(state)
    krow[...] = jnp.zeros_like(krow)

    def mix(pair, carry):
        diag = diag_two[0:width, :].astype(F32)
        here = chunk_rows(pair)
        query, key, value = ([fqkv[at, s * width : (s + 1) * width] for at in here] for s in range(3))
        scores = [split(dot(query[c], per_head(key[c]), NT) * causal) for c in both_chunks]
        turned = [key[c].T for c in both_chunks]
        over = [dot(scores[c][0], per_head(value[c])) for c in both_chunks]
        under = [dot(scores[c][0], masks[...]) + dot(scores[c][1], masks[...]) for c in both_chunks]
        made = [
            dot(turned[c][:, k * BLOCK : (k + 1) * BLOCK], halves(value[c])[k]) * diag
            for c in both_chunks
            for k in both_blocks
        ]
        row_made = [jnp.sum(halves(key[c])[k].astype(F32), 0, keepdims=True) for c in both_chunks for k in both_blocks]
        now, row = state[...], krow[0:1, :]
        carried, rows_in = [], []
        for k in range(4):
            carried.append(now.astype(BF))
            rows_in.append(row)
            states[4 * pair + k] = sum(now[h * HEAD_DIM : (h + 1) * HEAD_DIM] for h in range(heads)).astype(BF)
            ksums[pl.ds(4 * pair + k, 1), :] = row
            keep = joined(4 * pair + k + 1)
            now = (now + made[k]) * keep
            row = (row + row_made[k]) * keep
        state[...] = now
        krow[0:1, :] = row
        for c in both_chunks:
            parts = halves(query[c])
            more = wide([dot(parts[k], carried[2 * c + k]) for k in both_blocks], 0)
            high, low = split(wide([parts[k].astype(F32) * rows_in[2 * c + k] for k in both_blocks], 0))
            inverse = 1.0 / (under[c] + dot(wide([high, low]), diag_two[...]))
            attended = (over[c] + more) * inverse
            att[here[c], :] = attended
            rden[here[c], :] = wide([inverse[:, h * HEAD_DIM : h * HEAD_DIM + HEAD_DIM // 2] for h in range(heads)])
            mixed[here[c], :] = attended.astype(BF)

        return carry

    def add_parts(base, first, count, sources):
        cut = min(SUB, count)
        for at in range(0, count, cut):
            total = base[pl.ds(first + at, cut), :].astype(F32)
            for source, place in sources:
                total = total + source[pl.ds(place + at, cut), :].astype(F32)
            base[pl.ds(first + at, cut), :] = total.astype(BF)

    def bring(base, first, box, place, count):
        base[pl.ds(first, count), :] = box[pl.ds(place, count), :]

    half, quarter = UNIT // 2, UNIT // 4

    def rows_of(index, size):
        return pl.multiple_of(index * size, size)

    def unit_of(n):
        return grads.at[pl.ds(pl.multiple_of(n * UNIT, UNIT), UNIT)]

    def hop(box, kind, source, target, device):
        return pltpu.make_async_remote_copy(
            src_ref=source,
            dst_ref=target,
            send_sem=ar_send.at[box, kind],
            recv_sem=ar_recv.at[box, kind],
            device_id={"dp": device},
            device_id_type=MESH,
        )

    plain = units - 3 * width // UNIT
    per_tile = TILE // UNIT

    class Copies:
        def __init__(self, n):
            self.n = n

        def whole(self):
            first = pl.multiple_of(self.n * UNIT, UNIT)
            return pltpu.make_async_copy(unit_of(self.n), grads_out.at[pl.ds(first, UNIT)], grad_sem.at[0])

        def piece(self, q):
            u = self.n - plain
            at = 4 * lax.div(u, per_tile) + q
            row = pl.multiple_of(lax.div(at, 3) * TILE + lax.rem(u, per_tile) * UNIT, UNIT)
            return pltpu.make_async_copy(
                unit_of(self.n).at[:, q * width : (q + 1) * width],
                qkv_out.at[lax.rem(at, 3), pl.ds(row, UNIT)],
                grad_sem.at[1],
            )

        def start(self):
            pl.when(self.n < plain)(lambda: self.whole().start())

            @pl.when(self.n >= plain)
            def _():
                for q in range(4):
                    self.piece(q).start()

    def kind_of(n):
        return jnp.where(n < LATE, lax.rem(n, 2), 0)

    def box_of(n):
        first = jnp.where(n < LATE, lax.div(n, 2), n - LATE // 2)
        return lax.rem(first, BOXES_X), lax.rem(lax.div(n, 2), BOXES_Z)

    def begin(n):
        place, place_b = box_of(n)
        code = 4 * kind_of(n) + middle

        @pl.when(code < 4)
        def _():
            theirs = unit_of(n).at[pl.ds(rows_of(1 - along_x, half), half)]
            hop(place, 0, theirs, recv_a.at[place, pl.ds(0, half)], across).start()

        @pl.when(code == 4)
        def _():
            hop(BOXES_X + place_b, 0, unit_of(n), recv_b.at[place_b, pl.ds(0, UNIT)], inward).start()

    def advance(n, stage):
        kind = jnp.where(n < 0, 2, jnp.where(n >= units, 2, kind_of(n)))
        code = 4 * kind + middle
        place, place_b = box_of(n)

        def case(number):
            return pl.when(code == number)

        base, box = unit_of(n), recv_a.at[place]
        mine_at, theirs_at = rows_of(along_x, half), rows_of(1 - along_x, half)
        own_at = pl.multiple_of(along_x * half + side * quarter, quarter)
        other_at = pl.multiple_of(along_x * half + (1 - side) * quarter, quarter)
        own_in, other_in = rows_of(side, quarter), rows_of(1 - side, quarter)

        def rows(first, size):
            return base.at[pl.ds(first, size)]

        def x_one():
            return hop(place, 0, rows(theirs_at, half), box.at[pl.ds(0, half)], across)

        def z_one():
            return hop(place, 1, rows(mine_at, half), box.at[pl.ds(half, half)], inward)

        def z_two():
            return hop(place, 2, rows(other_at, quarter), box.at[pl.ds(2 * half, quarter)], inward)

        def z_swap():
            return hop(place, 3, rows(own_at, quarter), box.at[pl.ds(swap_at, quarter)], inward)

        def out(kind, first, place_in):
            return hop(place, kind, rows(first, quarter), box.at[pl.ds(half + place_in, quarter)], outward)

        def x_two():
            return hop(place, 6, rows(mine_at, half), box.at[pl.ds(last_at, half)], across)

        swap_at, last_at = 2 * half + quarter, 3 * half

        if stage == 1:

            @case(0)
            def _():
                x_one().wait_recv()
                add_parts(base, mine_at, half, [(box, 0)])
                z_one().start()

        if stage == 2:

            @case(2)
            def _():
                x_one().wait_recv()
                z_one().wait_recv()
                add_parts(base, other_at, quarter, [(box, other_in), (box, half + other_in)])
                z_two().start()

        if stage == 3:

            @case(2)
            def _():
                z_two().wait_recv()
                add_parts(base, own_at, quarter, [(box, own_in), (box, half + own_in), (box, 2 * half)])
                z_swap().start()
                out(4, own_at, own_in).start()

        if stage == 4:

            @case(2)
            def _():
                z_swap().wait_recv()
                z_two().wait_send()
                bring(base, other_at, box, swap_at, quarter)
                out(5, other_at, other_in).start()
                x_two().start()

        if stage == 5:

            @case(0)
            def _():
                z_one().wait_send()
                out(4, own_at, own_in).wait_recv()
                out(5, other_at, other_in).wait_recv()
                bring(base, mine_at, box, half, half)
                x_two().start()

        if stage == 6:

            @case(2)
            def _():
                z_swap().wait_send()
                out(4, own_at, own_in).wait_send()
                out(5, other_at, other_in).wait_send()

            @pl.when(kind == 0)
            def _():
                x_one().wait_send()
                x_two().wait()
                bring(base, theirs_at, box, last_at, half)

        box_b = recv_b.at[place_b]
        mine_z, theirs_z = rows_of(side, half), rows_of(1 - side, half)
        own_x = pl.multiple_of(side * half + along_x * quarter, quarter)
        other_x = pl.multiple_of(side * half + (1 - along_x) * quarter, quarter)
        own_part_at, other_part_at = rows_of(along_x, quarter), rows_of(1 - along_x, quarter)

        def z_in():
            return hop(BOXES_X + place_b, 0, base, box_b.at[pl.ds(0, UNIT)], inward)

        def z_mid():
            return hop(BOXES_X + place_b, 1, rows(theirs_z, half), box_b.at[pl.ds(UNIT, half)], inward)

        def x_mid():
            return hop(BOXES_X + place_b, 2, rows(other_x, quarter), box_b.at[pl.ds(UNIT + half, quarter)], across)

        def x_swap():
            return hop(BOXES_X + place_b, 3, rows(own_x, quarter), box_b.at[pl.ds(swap_at, quarter)], across)

        def z_share():
            return hop(BOXES_X + place_b, 4, rows(mine_z, half), box_b.at[pl.ds(last_at, half)], inward)

        def z_out(kind, first):
            return hop(BOXES_X + place_b, kind, rows(first, half), box_b.at[pl.ds(first, half)], outward)

        swap_at, last_at = UNIT + half + quarter, 2 * UNIT

        if stage == 1:

            @case(6)
            def _():
                z_in().wait_recv()
                add_parts(base, theirs_z, half, [(box_b, theirs_z)])
                z_mid().start()

        if stage == 2:

            @case(6)
            def _():
                z_mid().wait_recv()
                add_parts(base, other_x, quarter, [(box_b, other_x), (box_b, UNIT + other_part_at)])
                x_mid().start()

        if stage == 3:

            @case(6)
            def _():
                x_mid().wait_recv()
                add_parts(
                    base, own_x, quarter, [(box_b, own_x), (box_b, UNIT + own_part_at), (box_b, UNIT + half)]
                )
                x_swap().start()

        if stage == 4:

            @case(6)
            def _():
                x_swap().wait_recv()
                x_mid().wait_send()
                bring(base, other_x, box_b, swap_at, quarter)
                z_share().start()
                z_out(5, mine_z).start()

        if stage == 5:

            @case(6)
            def _():
                z_share().wait_recv()
                z_mid().wait_send()
                bring(base, theirs_z, box_b, last_at, half)
                z_out(6, theirs_z).start()

        if stage == 6:

            @case(6)
            def _():
                x_swap().wait_send()
                z_share().wait_send()
                z_out(5, mine_z).wait_send()
                z_out(6, theirs_z).wait_send()

            @case(4)
            def _():
                z_in().wait_send()
                z_out(5, mine_z).wait_recv()
                z_out(6, theirs_z).wait_recv()
                bring(base, 0, box_b, 0, UNIT)

            pl.when(kind < 2)(lambda: Copies(n).start())

    def at_ready(n):
        return jnp.where(n < LEAD, 1, jnp.where(n < plain, 0, jnp.where(n < plain + LEAD, 1, 0)))

    def ready(first, count):
        for n in (first + k for k in range(count)):
            if reduce_dp:
                pl.when(at_ready(n) == 1)(functools.partial(begin, n))
            else:
                Copies(n).start()

    def tick(t):
        if reduce_dp:
            with jax.named_scope("dp_tick"):
                move(t)

    def move(t):
        for stage in (6, 5, 4, 3, 2, 1):
            advance(t - LAG * (stage - 1), stage)
        later = t + LEAD

        @pl.when(jnp.where(later >= units, 1, at_ready(later)) == 0)
        def _():
            begin(later)

    def tick_at(j, every, first):
        @pl.when(lax.rem(j, every) == every - 1)
        def _():
            tick(first + lax.div(j, every))

    ticks = units + 5 * LAG

    def run_ticks(first, last):
        lax.fori_loop(first, last, pause, 0)

    def pause(t, carry):
        tick(t)
        return carry

    def to_mate(which, number):
        return pltpu.make_async_remote_copy(
            src_ref=rs_out.at[lax.rem(number, 2)],
            dst_ref=rs_in.at[number],
            send_sem=rs_send.at[which, number],
            recv_sem=rs_recv.at[which, number],
            device_id={"tensor": mate},
            device_id_type=MESH,
        )

    def to_peer(which, number):
        return pltpu.make_async_remote_copy(
            src_ref=rs_in.at[number],
            dst_ref=y_in.at[number],
            send_sem=rs_send.at[which, 4 + number],
            recv_sem=rs_recv.at[which, 4 + number],
            device_id={"tensor": peer},
            device_id_type=MESH,
        )

    def scatter(j, which, compute):
        owner = jnp.where(j < 2, cross, jnp.where(j < 4, peer, mate))
        number = lax.rem(j, 2)
        row0 = pl.multiple_of(owner * rows_own + number * TILE, TILE)

        @pl.when(lax.div(j, 2) != 1)
        def _():
            at = jnp.where(j < 2, j, j - 2)
            pl.when(j >= 4)(lambda: to_mate(which, number).wait_send())

            def put(columns, part):
                rs_out[number, :, columns] = part.astype(BF)

            compute(row0, put)
            to_mate(which, at).start()

        @pl.when(lax.div(j, 2) == 1)
        def _():
            to_mate(which, number).wait_recv()

            def put(columns, part):
                rs_in[number, :, columns] = (rs_in[number, :, columns].astype(F32) + part).astype(BF)

            compute(row0, put)
            to_peer(which, number).start()

    def gathered(which, number):
        to_mate(which, 2 + number).wait_recv()
        to_peer(which, number).wait_recv()

    def settle(which):
        for number in range(2):
            to_mate(which, 2 + number).wait_send()
            to_peer(which, number).wait_send()

    def stored(number, target):
        return pltpu.make_async_copy(rs_out.at[number], target, result_sem.at[number])

    pltpu.make_async_copy(tok.at[pl.ds(0, rows)], tok_kept, tok_sem.at[0]).wait()
    for piece in range(g_tok.pieces):
        g_tok.forward(peer, piece).wait_send()

    def keep_unit(n, value):
        grads[pl.ds(pl.multiple_of(n * UNIT, UNIT), value.shape[0]), :] = value
        ready(n, value.shape[0] // UNIT)

    first_out = hid.shape[1] // UNIT
    first_up = first_out + width // UNIT

    def arrive(piece):
        g_cot.to_peer(peer, piece).wait_recv()
        g_cot.forward(peer, piece).start()

    def down(piece):
        g_cot.forward(cross, piece).wait_recv()
        tile = dot(cot[:, piece * TILE : (piece + 1) * TILE], hid[...], TN)
        keep_unit(per_tile * piece, tile.astype(BF))

    def mix_some(first, last):
        with jax.named_scope("mixer"):
            lax.fori_loop(first, last, mix, 0)

    pairs = chunks // 2
    with jax.named_scope("grad_down"):
        arrive(0)
        arrive(1)
        down(0)
        down(1)
    mix_some(0, pairs // 4)
    run_ticks(0, 1)
    arrive(2)
    mix_some(pairs // 4, pairs // 2)
    run_ticks(1, 3)
    with jax.named_scope("grad_down"):
        down(2)

    run_ticks(3, 5)
    mix_some(pairs // 2, 3 * pairs // 4)
    run_ticks(5, 7)
    arrive(3)
    mix_some(3 * pairs // 4, pairs)
    with jax.named_scope("grad_down"):
        down(3)
    run_ticks(7, 9)
    keep_unit(first_out, dot(mixed[...], cot[...], TN).astype(BF))
    run_ticks(9, 11)

    column_tiles = [slice(at, at + TILE) for at in range(0, cot.shape[1], TILE)]

    def branch(row0, put):
        here = pl.ds(row0, TILE)
        left, right = mixed[here, :], hid[here, :]
        for columns in column_tiles:
            put(columns, dot(left, w_out[:, columns]) + dot(right, w_down[:, columns]))

    def keep_temp(number):
        def put(columns, part):
            temp[number, :, columns] = part

        return put

    def own_copy(number, back=False):
        held = own_part.at[pl.ds(pl.multiple_of(number * TILE, TILE), TILE)]
        if back:
            return pltpu.make_async_copy(held, temp.at[number], temp_sem.at[number])
        return pltpu.make_async_copy(temp.at[0], held, temp_sem.at[0])

    def produce(j, carry):
        @pl.when(j >= 2)
        def _():
            scatter(j - 2, 0, branch)

        @pl.when(j < 2)
        def _():
            branch(pl.multiple_of(me * rows_own + j * TILE, TILE), keep_temp(0))
            own_copy(j).start()
            own_copy(j).wait()

        pl.when(j == 1)(lambda: slope_copy(0, True).start())
        pl.when(j == 2)(lambda: slope_copy(1, True).start())
        tick_at(j, 2, 11)

        return carry

    with jax.named_scope("outputs"):
        lax.fori_loop(0, 8, produce, 0)
    bring_up = pltpu.make_async_copy(
        grads.at[pl.ds(rows, 2 * rows_own)], hid.at[pl.ds(chip_row, 2 * rows_own)], tok_sem.at[0]
    )
    bring_up.start()

    def descend(p, carry):
        here = [pl.ds(pl.multiple_of(owner * rows_own + p * PIECE, PIECE), PIECE) for owner in (peer, cross)]
        parity = lax.rem(p, 2)
        slope_copy(p, True).wait()
        turned = wide([cot[at, :] for at in here], 0)
        for at in range(0, hid.shape[1], TILE):
            d_hidden = dot(turned, w_down[at : at + TILE, :], NT)
            d_up = (d_hidden * temp[parity, :, at : at + TILE]).astype(BF)
            for k, rows_at in enumerate(here):
                hid[rows_at, at : at + TILE] = d_up[k * PIECE : (k + 1) * PIECE]
        pl.when(p < 2)(lambda: slope_copy(p + 2, True).start())
        tick_at(p, 2, 15)
        return carry

    with jax.named_scope("grad_gelu"):
        lax.fori_loop(0, 4, descend, 0)
    bring_up.wait()

    def upward(j, carry):
        at = pl.ds(pl.multiple_of(j * TILE, TILE), TILE)
        keep_unit(first_up + per_tile * j, dot(n_two[:, at], hid[...], TN).astype(BF))
        run_ticks(17 + j, 18 + j)
        return carry

    with jax.named_scope("grad_up"):
        lax.fori_loop(0, n_two.shape[1] // TILE, upward, 0)

    state[...] = jnp.zeros_like(state)
    krow[...] = jnp.zeros_like(krow)
    feat_sums[...] = jnp.zeros_like(feat_sums)

    def unmix(step, carry):
        pair = chunks // 2 - 1 - step
        diag = diag_two[0:width, :].astype(F32)
        row_pair = pl.multiple_of(pair * 2 * CHUNK, 2 * CHUNK)
        d_mixed = dot(cot[pl.ds(row_pair, 2 * CHUNK), :], w_out[...], NT)
        here = chunk_rows(pair)
        query, key, value = ([fqkv[at, s * width : (s + 1) * width] for at in here] for s in range(3))
        d_over, under_parts = [], []
        for c in both_chunks:
            packed = rden[here[c], :]
            inverse = wide(
                [packed[:, h // 2 * HEAD_DIM // 2 : (h // 2 + 1) * HEAD_DIM // 2] for h in range(2 * heads)]
            )
            d_over.append(d_mixed[c * CHUNK : (c + 1) * CHUNK] * inverse)
            under_parts.append(wide(split(d_over[c] * att[here[c], :])))
        d_under = [-dot(under_parts[c], diag_two[...]) for c in both_chunks]
        under_row = [-dot(wide([head_rows, head_rows]), under_parts[c], NT) for c in both_chunks]
        over_split = [split(d_over[c]) for c in both_chunks]
        over_both = [wide(over_split[c]) for c in both_chunks]
        over_heads = [wide([per_head(part) for part in over_split[c]]) for c in both_chunks]
        query_heads, key_heads, value_heads = ([per_head(field[c]) for c in both_chunks] for field in (query, key, value))
        scores_back = [(dot(key[c], query_heads[c], NT) * causal_back).astype(BF) for c in both_chunks]
        d_scores = [dot(over_both[c], wide([value_heads[c]] * 2), NT) for c in both_chunks]
        d_back = [dot(wide([value[c]] * 2), over_heads[c], NT) for c in both_chunks]
        turned = [query[c].T for c in both_chunks]
        made = []
        for c in both_chunks:
            for k in both_blocks:
                left = turned[c][:, k * BLOCK : (k + 1) * BLOCK]
                made.append(dot(wide([left, left]), wide([halves(part)[k] for part in over_split[c]], 0)) * diag)
        d_scores = [
            wide(
                split(
                    (
                        d_scores[c]
                        + wide(
                            [
                                jnp.broadcast_to(d_under[c][:, h * HEAD_DIM : h * HEAD_DIM + 1], (CHUNK, CHUNK))
                                for h in range(heads)
                            ]
                        )
                    )
                    * causal
                )
            )
            for c in both_chunks
        ]
        d_back = [
            wide(split((d_back[c] + wide([under_row[c][h : h + 1, :] for h in range(heads)])) * causal_back))
            for c in both_chunks
        ]
        d_query = [dot(d_scores[c], wide([key_heads[c]] * 2, 0)) for c in both_chunks]
        d_key = [dot(d_back[c], wide([query_heads[c]] * 2, 0)) for c in both_chunks]
        d_value = [dot(scores_back[c], over_heads[c]) for c in both_chunks]
        later, later_row = state[...], krow[0:1, :]
        more = {}
        for at in reversed(range(4)):
            c, k = divmod(at, 2)
            block = 4 * pair + at
            query_k, key_k, value_k, both_k, under_k = (
                halves(field[c])[k] for field in (query, key, value, over_both, d_under)
            )
            carried = wide([states[block]] * heads, 0) * diag_two[0:width, :]
            keep = joined(block + 1)
            later, later_row = later * keep, later_row * keep
            high, low = split(later)
            more[at] = (
                dot(both_k, wide([carried, carried]), NT) + under_k * ksums[pl.ds(block, 1), :],
                dot(wide([value_k, value_k]), wide([high, low]), NT) + later_row,
                dot(wide([key_k, key_k]), wide([high, low], 0)),
            )
            later = later + made[at]
            later_row = later_row + jnp.sum(query_k.astype(F32) * under_k, 0, keepdims=True)
        state[...] = later
        krow[0:1, :] = later_row
        turn = rotation(row_pair, 2 * CHUNK // BLOCK)
        here = pl.ds(row_pair, 2 * CHUNK)
        for s, found in enumerate((d_query, d_key)):
            grad = wide(found, 0) + wide([more[at][s] for at in range(4)], 0)
            spectrum = spec[s, here, :]
            grad = grad * (weight_row * jnp.exp(scale_row * spectrum))
            feat_sums[0:1, :] += jnp.sum(grad * spectrum, 0, keepdims=True)
            feat_sums[1:2, :] += jnp.sum(grad, 0, keepdims=True)
            high, low = split(grad * scale_row)
            back = dot(high, dct[:, 0:width]) + dot(low, dct[:, 0:width]) + dot(high, dct[:, 2 * width :])
            fqkv[here, s * width : (s + 1) * width] = rotate(back, turn, True).astype(BF)
        d_value = wide([d_value[c][:, :width] + d_value[c][:, width:] for c in both_chunks], 0)
        fqkv[here, 2 * width : 3 * width] = (d_value + wide([more[at][2] for at in range(4)], 0)).astype(BF)
        run_ticks(21 + lax.div(15 * step, chunks // 2), 21 + lax.div(15 * (step + 1), chunks // 2))

        return carry

    with jax.named_scope("mixer_back"):
        lax.fori_loop(0, chunks // 2, unmix, 0)

    def own_tok(number):
        return pltpu.make_async_copy(tok_in.at[pl.ds(number * TILE, TILE)], rs_out.at[number], result_sem.at[number])

    settle(0)
    for number in range(2):
        own_copy(number, True).start()
        own_tok(number).start()

    for j in range(n_one.shape[1] // TILE):
        tile = dot(n_one[:, j * TILE : (j + 1) * TILE], fqkv[...], TN).astype(BF)
        for s in range(3):
            at = 3 * j + s
            first = plain * UNIT + at // 4 * TILE
            grads[first : first + TILE, at % 4 * width : (at % 4 + 1) * width] = tile[:, s * width : (s + 1) * width]
        if j:
            ready(plain + (j - 1) * per_tile, per_tile)


    run_ticks(36, 38)

    sums[...] = jnp.zeros_like(sums)

    def row_of(j):
        owner = jnp.where(j < 2, cross, jnp.where(j < 4, peer, jnp.where(j < 6, mate, me)))
        return pl.multiple_of(owner * rows_own + lax.rem(j, 2) * TILE, TILE)

    def tok_copy(j):
        which = lax.rem(j, 2)
        return pltpu.make_async_copy(
            tok_kept.at[pl.ds(row_of(j), TILE)], n_two.at[pl.ds(pl.multiple_of(which * TILE, TILE), TILE)], tok_sem.at[which]
        )

    def row_grads(j):
        def compute(row0, put):
            here = pl.ds(row0, TILE)
            unit, _ = unit_rows(n_two[pl.ds(pl.multiple_of(lax.rem(j, 2) * TILE, TILE), TILE), :].astype(F32))
            fields = [fqkv[here, s * width : (s + 1) * width] for s in range(3)]
            right = hid[here, :]
            for columns in column_tiles:
                one = sum(dot(fields[s], w_qkv[s, columns, :], NT) for s in range(3))
                two = dot(right, w_up[columns, :], NT)
                part = unit[:, columns]
                for number, term in enumerate((one * part, one, two * part, two)):
                    sums[number, :, columns] += jnp.sum(term.reshape(TILE // 8, 8, TILE), 0)
                put(columns, one * gain_one[:, columns] + two * gain_two[:, columns])

        return compute

    def finish(number, carry):
        own_copy(number, True).wait()
        own_tok(number).wait()
        gathered(0, number)

        def step(i, inner):
            at = pl.ds(pl.multiple_of(i * SUB, SUB), SUB)
            total = temp[number, at, :] + rs_in[2 + number, at, :].astype(F32) + y_in[number, at, :].astype(F32)
            rs_out[number, at, :] = (total + rs_out[number, at, :].astype(F32)).astype(BF)
            return inner

        lax.fori_loop(0, TILE // SUB, step, 0)
        stored(number, mixed_out.at[pl.ds(pl.multiple_of(number * TILE, TILE), TILE)]).start()
        return carry

    with jax.named_scope("finish"):
        lax.fori_loop(0, 2, finish, 0)
    pl.semaphore_signal(free_mate, inc=1, device_id={"tensor": mate}, device_id_type=MESH)
    pl.semaphore_signal(free_peer, inc=1, device_id={"tensor": peer}, device_id_type=MESH)
    tok_copy(0).start()
    for number in range(2):
        stored(number, mixed_out.at[pl.ds(0, TILE)]).wait()
    pl.semaphore_wait(free_mate, 1)
    pl.semaphore_wait(free_peer, 1)

    def inputs(j, carry):
        tok_copy(j).wait()
        pl.when(j < 7)(lambda: tok_copy(j + 1).start())

        @pl.when(j < 6)
        def _():
            scatter(j, 1, row_grads(j))

        @pl.when(j >= 6)
        def _():
            row_grads(j)(row_of(j), keep_temp(lax.rem(j, 2)))

        run_ticks(38 + 2 * j, 40 + 2 * j)
        return carry

    with jax.named_scope("row_grads"):
        lax.fori_loop(0, 8, inputs, 0)
    settle(1)
    for number in range(2):
        own_tok(number).start()

    def conclude(number):
        own_tok(number).wait()
        gathered(1, number)

        def step(i, inner):
            at = pl.ds(pl.multiple_of(i * SUB, SUB), SUB)
            group_at = pl.multiple_of(me * rows_own + number * TILE + i * SUB, SUB)
            unit, deviation = unit_rows(rs_out[number, at, :].astype(F32))
            total = temp[number, at, :] + rs_in[2 + number, at, :].astype(F32) + y_in[number, at, :].astype(F32)
            along = jnp.mean(total * unit, -1, keepdims=True)
            total = total - jnp.mean(total, -1, keepdims=True) - unit * along
            total = cot[pl.ds(group_at, SUB), :].astype(F32) + deviation * total
            rs_out[number, at, :] = total.astype(BF)
            return inner

        lax.fori_loop(0, TILE // SUB, step, 0)
        stored(number, input_grad.at[pl.ds(number * TILE, TILE)]).start()

    small[...] = jnp.zeros_like(small)
    for number in range(4):
        small[number : number + 1, :] = jnp.sum(sums[number], 0, keepdims=True)
    small[4:5, 0:width] = feat_sums[0:1, :]
    small[5:6, 0:width] = feat_sums[1:2, :] / weight_row

    def small_hops(axis, own, count, boxes, first):
        hops = []
        for step in range(1, count):
            hops.append(
                pltpu.make_async_remote_copy(
                    src_ref=small,
                    dst_ref=boxes.at[own],
                    send_sem=small_send.at[first + step - 1],
                    recv_sem=small_recv.at[first + step - 1],
                    device_id={axis: lax.rem(own + step, count)},
                    device_id_type=MESH,
                )
            )
        return hops

    over_tensor = small_hops("tensor", me, 4, small_in, 0)
    over_dp = small_hops("dp", group, members, small_wide, 3)

    def small_step(k):
        if k == 0:
            for copy in over_tensor:
                copy.start()
            small_in[me] = small[...]
        if k == 1:
            for copy in over_tensor:
                copy.wait()
            total = small_in[0]
            for member in range(1, 4):
                total = total + small_in[member]
            small[0:4, :] = total[0:4, :]
        if k == 1 and reduce_dp:
            for copy in over_dp:
                copy.start()
            small_wide[group] = small[...]
        if k == 2 and reduce_dp:
            for copy in over_dp:
                copy.wait()
            total = small_wide[0]
            for member in range(1, members):
                total = total + small_wide[member]
            small[...] = total

    small_step(0)
    run_ticks(54, 55)
    conclude(0)
    small_step(1)
    run_ticks(55, 56)
    conclude(1)
    run_ticks(56, 57)
    small_step(2)
    if reduce_dp:
        run_ticks(57, ticks)
    for h in range(heads):
        at = slice(h * HEAD_DIM, (h + 1) * HEAD_DIM)
        feat_out[0, h : h + 1, :] = small[4:5, at]
        feat_out[1, h : h + 1, :] = small[5:6, at]

    pltpu.make_async_copy(grads.at[pl.ds(0, plain * UNIT)], grads_out, grad_sem.at[0]).wait()
    pltpu.make_async_copy(w_qkv, qkv_out, grad_sem.at[1]).wait()
    for number in range(2):
        stored(number, input_grad.at[pl.ds(0, TILE)]).wait()

    for gather in (g_tok, g_cot):
        gather.to_mate(me).wait_send()
        for piece in range(gather.pieces):
            gather.to_peer(me, piece).wait_send()
    for piece in range(g_cot.pieces):
        g_cot.forward(peer, piece).wait_send()


def widen(down_in, out_in, up_in, qkv_in, small_in, feats_in, mixed_in, input_in, *outs):
    down, out, up, qkv, *norms, scale, weight, mixed, input_grad = outs
    down[...] = down_in[...].astype(F32).T
    out[...] = out_in[...].astype(F32)
    up[...] = up_in[...].astype(F32)
    qkv[...] = qkv_in[...].astype(F32)
    for number, norm in enumerate(norms):
        norm[...] = small_in[number : number + 1, :]
    scale[...] = feats_in[0]
    weight[...] = feats_in[1]
    mixed[...] = mixed_in[...]
    input_grad[...] = input_in[...]


def shards(
    reduce_dp,
    tokens,
    ln1_gain,
    ln1_bias,
    ln2_gain,
    ln2_bias,
    w_qkv,
    w_out,
    w_up,
    w_down,
    feature_scale,
    feature_weight,
    lengths,
    cotangent,
):
    rows_own, model = tokens.shape
    rows = 4 * rows_own
    heads = feature_scale.shape[0]
    width = heads * HEAD_DIM
    hidden = w_up.shape[1]
    consts = tables(rows // BLOCK, heads)
    norms = [value.reshape(1, model) for value in (ln1_gain, ln1_bias, ln2_gain, ln2_bias)]
    anywhere = pl.BlockSpec(memory_space=pl.ANY)
    vmem = pl.BlockSpec(memory_space=pltpu.VMEM)
    smem = pl.BlockSpec(memory_space=pltpu.SMEM)
    shape = jax.ShapeDtypeStruct
    plain = 2 * hidden + width
    units = (plain + 3 * width) // UNIT
    mixed_out, input_grad, grads, g_qkv, _, _, _, small, feats = pl.pallas_call(
        functools.partial(kernel, reduce_dp),
        out_shape=(
            shape((rows_own, model), BF),
            shape((rows_own, model), BF),
            shape((plain, model), BF),
            shape((3, model, width), BF),
            shape((rows // 2, hidden), F32),
            shape((rows_own, model), F32),
            shape((rows, model), BF),
            shape((8, model), F32),
            shape((2, heads, HEAD_DIM), F32),
        ),
        in_specs=[smem, anywhere, anywhere] + [vmem] * 4 + [anywhere] * 4 + [vmem] * 6,
        out_specs=(anywhere,) * 7 + (vmem, vmem),
        scratch_shapes=[
            pltpu.VMEM((rows, model), BF),
            pltpu.VMEM((rows, model), BF),
            pltpu.VMEM((rows, model), BF),
            pltpu.VMEM((rows, hidden), BF),
            pltpu.VMEM((rows, 3 * width), BF),
            pltpu.VMEM((2, rows, width), F32),
            pltpu.VMEM((rows, width), BF),
            pltpu.VMEM((rows, width), F32),
            pltpu.VMEM((rows, width // 2), F32),
            pltpu.VMEM((rows // BLOCK, HEAD_DIM, width), BF),
            pltpu.VMEM((rows // BLOCK, width), F32),
            pltpu.VMEM((width, width), F32),
            pltpu.VMEM((8, width), F32),
            pltpu.VMEM((units * UNIT, model), BF),
            pltpu.VMEM((BOXES_X, 2 * UNIT, model), BF),
            pltpu.VMEM((BOXES_Z, 5 * UNIT // 2, model), BF),
            pltpu.VMEM((2, TILE, model), BF),
            pltpu.VMEM((4, TILE, model), BF),
            pltpu.VMEM((2, TILE, model), BF),
            pltpu.VMEM((2, TILE, model), F32),
            pltpu.VMEM((4, 8, model), F32),
            pltpu.VMEM((8, width), F32),
            pltpu.VMEM((4, 8, model), F32),
            pltpu.VMEM((8, 8, model), F32),
            pltpu.VMEM(w_qkv.shape, BF),
            pltpu.VMEM(w_out.shape, BF),
            pltpu.VMEM(w_up.shape, BF),
            pltpu.VMEM(w_down.shape, BF),
            pltpu.SemaphoreType.DMA((2 + 2 * rows_own // PIECE,)),
            pltpu.SemaphoreType.DMA((2 + 2 * rows_own // PIECE + 2 * model // TILE,)),
            pltpu.SemaphoreType.DMA((2 + 2 * rows_own // PIECE + 2 * model // TILE,)),
            pltpu.SemaphoreType.DMA((4,)),
            pltpu.SemaphoreType.DMA((BOXES_X + BOXES_Z, 7)),
            pltpu.SemaphoreType.DMA((BOXES_X + BOXES_Z, 7)),
            pltpu.SemaphoreType.DMA((2, 6)),
            pltpu.SemaphoreType.DMA((2, 6)),
            pltpu.SemaphoreType.DMA((10,)),
            pltpu.SemaphoreType.DMA((10,)),
            pltpu.SemaphoreType.DMA((2,)),
            pltpu.SemaphoreType.DMA((2,)),
            pltpu.SemaphoreType.DMA((2,)),
            pltpu.SemaphoreType.DMA((2,)),
            pltpu.SemaphoreType.REGULAR,
            pltpu.SemaphoreType.REGULAR,
        ],
        compiler_params=pltpu.CompilerParams(
            collective_id=0, has_side_effects=True, vmem_limit_bytes=62 * 2**20
        ),
    )(lengths, tokens, cotangent, *norms, w_qkv, w_out, w_up, w_down, feature_scale, feature_weight, *consts)
    if not reduce_dp:
        grads, g_qkv, small, feats = lax.psum(
            (*lax.optimization_barrier((grads.astype(F32), g_qkv.astype(F32))), small, feats), "dp"
        )
    steps = 4
    down_cut, out_cut, up_cut, row_cut, own_cut = (
        size // steps for size in (hidden, width, model, model, rows_own)
    )
    rows_spec = pl.BlockSpec((own_cut, model), lambda i: (i, 0))
    row_spec = pl.BlockSpec((1, model), lambda i: (0, 0))
    feat_spec = pl.BlockSpec((heads, HEAD_DIM), lambda i: (0, 0))
    g_down, g_out, g_up, g_qkv, *norm_sums, g_scale, g_weight, mixed_out, input_grad = pl.pallas_call(
        widen,
        grid=(steps,),
        out_shape=(
            shape((hidden, model), F32),
            shape((width, model), F32),
            shape((model, hidden), F32),
            shape((3, model, width), F32),
            *[shape((1, model), F32)] * 4,
            *[shape((heads, HEAD_DIM), F32)] * 2,
            *[shape((rows_own, model), BF)] * 2,
        ),
        in_specs=[
            pl.BlockSpec((model, down_cut), lambda i: (0, i)),
            pl.BlockSpec((out_cut, model), lambda i: (hidden // out_cut + i, 0)),
            pl.BlockSpec((up_cut, hidden), lambda i: ((hidden + width) // up_cut + i, 0)),
            pl.BlockSpec((3, row_cut, width), lambda i: (0, i, 0)),
            pl.BlockSpec((8, model), lambda i: (0, 0)),
            pl.BlockSpec((2, heads, HEAD_DIM), lambda i: (0, 0, 0)),
            rows_spec,
            rows_spec,
        ],
        out_specs=(
            pl.BlockSpec((down_cut, model), lambda i: (i, 0)),
            pl.BlockSpec((out_cut, model), lambda i: (i, 0)),
            pl.BlockSpec((up_cut, hidden), lambda i: (i, 0)),
            pl.BlockSpec((3, row_cut, width), lambda i: (0, i, 0)),
            *[row_spec] * 4,
            *[feat_spec] * 2,
            *[rows_spec] * 2,
        ),
        compiler_params=pltpu.CompilerParams(vmem_limit_bytes=60 * 2**20),
    )(grads, grads, grads, g_qkv, small, feats, mixed_out, input_grad)
    return (
        mixed_out,
        input_grad,
        *[value.reshape(model) for value in norm_sums],
        g_qkv,
        g_out,
        g_up,
        g_down,
        g_scale,
        g_weight,
    )


def solution(mesh):
    placed = (
        P(("dp", "tensor"), None),
        P(),
        P(),
        P(),
        P(),
        P(None, None, "tensor"),
        P("tensor", None),
        P(None, "tensor"),
        P("tensor", None),
        P("tensor", None),
        P("tensor", None),
        P("dp", None),
        P(("dp", "tensor"), None),
    )
    return jax.shard_map(
        functools.partial(shards, mesh.shape["dp"] == 8),
        mesh=mesh,
        in_specs=placed,
        out_specs=(
            P(("dp", "tensor"), None),
            P(("dp", "tensor"), None),
            P(),
            P(),
            P(),
            P(),
            P(None, None, "tensor"),
            P("tensor", None),
            P(None, "tensor"),
            P("tensor", None),
            P("tensor", None),
            P("tensor", None),
        ),
        check_vma=False,
    )
```

```python
import functools
import math

import jax
import jax.numpy as jnp
import ml_dtypes
import numpy as np
from jax import lax
from jax.experimental import pallas as pl
from jax.experimental.pallas import tpu as pltpu
from jax.sharding import PartitionSpec as P

HEAD_DIM = 64
ROT = 16
BLOCK = 64
CHUNK = 128
TILE = 256
PIECE = 128
UNIT = 64
SUB = 32
LEAD = 2
LAG = 2
BOXES_X = 6
BOXES_Z = 6
MESH = pl.DeviceIdType.MESH
F32 = jnp.float32
BF = jnp.bfloat16
NN = (((1,), (0,)), ((), ()))
NT = (((1,), (1,)), ((), ()))
TN = (((0,), (0,)), ((), ()))


def dot(left, right, dims=NN):
    return lax.dot_general(left, right, dims, preferred_element_type=F32)


def split(value):
    high = value.astype(BF)
    return high, (value - high.astype(F32)).astype(BF)


def wide(parts, axis=1):
    return jnp.concatenate(parts, axis)


def tables(blocks, heads):
    width = heads * HEAD_DIM
    freq, dims = np.arange(HEAD_DIM)[:, None], np.arange(HEAD_DIM)[None, :]
    dct = np.cos(np.pi * (dims + 0.5) * freq / HEAD_DIM) * math.sqrt(2.0 / HEAD_DIM)
    dct[0] *= math.sqrt(0.5)
    dct = np.kron(np.eye(heads), dct).astype(np.float32)
    high = dct.astype(ml_dtypes.bfloat16)
    low = (dct - high.astype(np.float32)).astype(ml_dtypes.bfloat16)
    halves = np.concatenate([high, low], 1)
    half = ROT // 2
    lane = np.arange(2 * HEAD_DIM) % HEAD_DIM
    rate = np.where(lane < ROT, 10000.0 ** (-(lane % half) * 2.0 / ROT), 0.0)
    in_block = np.arange(BLOCK)[:, None] * rate[None]
    of_block = np.arange(blocks)[:, None] * BLOCK * rate[None]
    signs = np.stack([np.where(lane < half, -1.0, 0.0), np.where((lane >= half) & (lane < ROT), 1.0, 0.0)] + [0.0 * lane] * 6)
    angles = np.concatenate([np.cos(in_block), np.sin(in_block), np.cos(of_block), np.sin(of_block), signs], 0)
    block_ones = np.kron(np.eye(heads), np.ones((HEAD_DIM, HEAD_DIM)))
    masks = np.kron(np.eye(heads), np.ones((CHUNK, HEAD_DIM)))
    return (
        halves,
        angles.astype(np.float32),
        block_ones.astype(ml_dtypes.bfloat16),
        masks.astype(ml_dtypes.bfloat16),
    )


def kernel(
    reduce_dp,
    lengths,
    tok_in,
    cot_in,
    gain_one_in,
    bias_one_in,
    gain_two_in,
    bias_two_in,
    w_qkv_in,
    w_out_in,
    w_up_in,
    w_down_in,
    feature_scale,
    feature_weight,
    dct,
    angles,
    diagonal,
    masks,
    mixed_out,
    input_grad,
    grads_out,
    qkv_out,
    slopes,
    tok_kept,
    small,
    feat_out,
    cot,
    n_one,
    n_two,
    hid,
    d_up,
    fqkv,
    spec,
    mixed,
    att,
    rden,
    states,
    ksums,
    state,
    krow,
    grads,
    recv_a,
    recv_b,
    rs_out,
    rs_in,
    y_in,
    temp,
    sums,
    feat_sums,
    small_in,
    small_wide,
    w_qkv,
    w_out,
    w_up,
    w_down,
    local_sem,
    send_sem,
    recv_sem,
    weight_sem,
    ar_send,
    ar_recv,
    rs_send,
    rs_recv,
    small_send,
    small_recv,
    grad_sem,
    temp_sem,
    tok_sem,
    result_sem,
    free_mate,
    free_peer,
):
    rows_own = tok_in.shape[0]
    rows = cot.shape[0]
    tok = grads
    width = w_out_in.shape[0]
    heads = width // HEAD_DIM
    chunks = rows // CHUNK
    me = lax.axis_index("tensor")
    core = lax.rem(me, 2)
    mate = me + 1 - 2 * core
    peer = lax.rem(me + 2, 4)
    cross = 3 - me
    group = lax.axis_index("dp")
    along_x = lax.rem(group, 2)
    across = group + 1 - 2 * along_x
    along_z = lax.div(group, 2)
    middle = along_z * (3 - along_z)

    def at_end(step):
        pl.when(middle == 0)(step)

    def at_mid(step):
        pl.when(middle > 0)(step)

    side = jnp.where(along_z < 2, 0, 1)
    inward = group + 2 - 4 * side
    outward = group - 2 + 4 * side
    units = grads.shape[0] // UNIT

    weight_copies = [
        pltpu.make_async_copy(source, target, weight_sem.at[k])
        for k, (source, target) in enumerate(
            ((w_qkv_in, w_qkv), (w_up_in, w_up), (w_out_in, w_out), (w_down_in, w_down))
        )
    ]
    for copy in weight_copies:
        copy.start()

    barrier = pltpu.get_barrier_semaphore()
    members = 8 if reduce_dp else 1
    for step in range(1, 4):
        other = lax.rem(me + step, 4)
        pl.semaphore_signal(barrier, inc=1, device_id={"tensor": other}, device_id_type=MESH)
    for step in range(1, members):
        other = lax.rem(group + step, members)
        pl.semaphore_signal(barrier, inc=1, device_id={"dp": other}, device_id_type=MESH)
    pl.semaphore_wait(barrier, 2 + members)

    def slot(buf, owner, piece=None, columns=False):
        if piece is None:
            return buf.at[pl.ds(pl.multiple_of(owner * rows_own, rows_own), rows_own)]
        if columns:
            here = pl.ds(pl.multiple_of(owner * rows_own, rows_own), rows_own)
            return buf.at[here, piece * TILE : (piece + 1) * TILE]
        return buf.at[pl.ds(pl.multiple_of(owner * rows_own + piece * PIECE, PIECE), PIECE)]

    class Gather:
        def __init__(self, source, buf, base, columns):
            self.source, self.buf, self.base, self.columns = source, buf, base, columns
            self.pieces = source.shape[1] // TILE if columns else source.shape[0] // PIECE

        def copy(self, number, src, dst, target):
            return pltpu.make_async_remote_copy(
                src_ref=src,
                dst_ref=dst,
                send_sem=send_sem.at[self.base + number],
                recv_sem=recv_sem.at[self.base + number],
                device_id={"tensor": target},
                device_id_type=MESH,
            )

        def local(self):
            return pltpu.make_async_copy(self.source, slot(self.buf, me), local_sem.at[self.base])

        def to_mate(self, owner):
            return self.copy(0, self.source, slot(self.buf, owner), mate)

        def to_peer(self, owner, piece):
            if self.columns:
                part = self.source.at[:, piece * TILE : (piece + 1) * TILE]
            else:
                part = self.source.at[pl.ds(piece * PIECE, PIECE)]
            return self.copy(1 + piece, part, slot(self.buf, owner, piece, self.columns), peer)

        def forward(self, owner, piece):
            part = slot(self.buf, owner, piece, self.columns)
            return self.copy(1 + self.pieces + piece, part, part, mate)

    g_tok, g_cot = Gather(tok_in, tok, 0, False), Gather(cot_in, cot, 1 + 2 * (rows_own // PIECE), True)
    g_tok.to_mate(me).start()
    for piece in range(g_tok.pieces):
        g_tok.to_peer(me, piece).start()
    g_tok.local().start()
    g_cot.to_mate(me).start()
    g_cot.local().start()

    start_one = lengths[0, 0]
    start_two = start_one + lengths[0, 1]

    def segment(block):
        return (block >= start_one).astype(jnp.int32) + (block >= start_two).astype(jnp.int32)

    def in_sequence(block):
        return block - jnp.where(block >= start_two, start_two, jnp.where(block >= start_one, start_one, 0))

    gain_one, bias_one, gain_two, bias_two = gain_one_in[...], bias_one_in[...], gain_two_in[...], bias_two_in[...]
    scale_row, weight_row = (
        wide([field[h : h + 1, :] for h in range(heads)]) for field in (feature_scale, feature_weight)
    )
    blocks = rows // BLOCK

    def rotation(row0, count):
        cos_in, sin_in = angles[0:BLOCK, :], angles[BLOCK : 2 * BLOCK, :]
        sign_a = angles[2 * BLOCK + 2 * blocks : 2 * BLOCK + 2 * blocks + 1, :]
        sign_b = angles[2 * BLOCK + 2 * blocks + 1 : 2 * BLOCK + 2 * blocks + 2, :]
        cosines, sines = [], []
        for k in range(count):
            place = in_sequence(lax.div(row0, BLOCK) + k)
            cos_at = angles[pl.ds(2 * BLOCK + place, 1), :]
            sin_at = angles[pl.ds(2 * BLOCK + blocks + place, 1), :]
            cosines.append(cos_in * cos_at - sin_in * sin_at)
            sines.append(sin_in * cos_at + cos_in * sin_at)
        cosine, sine = wide(cosines, 0), wide(sines, 0)
        return cosine, sine * sign_a, sine * sign_b

    def rotate(field, turn, back=False):
        cosine, sine_a, sine_b = turn
        parts = []
        for at in range(0, width, 2 * HEAD_DIM):
            part = field[:, at : at + 2 * HEAD_DIM]
            ahead = pltpu.roll(part, 2 * HEAD_DIM - ROT // 2, 1) * sine_a
            behind = pltpu.roll(part, ROT // 2, 1) * sine_b
            parts.append(part * cosine - (ahead + behind) if back else part * cosine + (ahead + behind))
        return wide(parts)

    def unit_rows(value):
        value = value - jnp.mean(value, -1, keepdims=True)
        deviation = lax.rsqrt(jnp.mean(value * value, -1, keepdims=True) + 1e-05)
        return value * deviation, deviation

    def slope_copy(p, back=False):
        held = slopes.at[pl.ds(pl.multiple_of(p * TILE, TILE), TILE)]
        slot_of = temp.at[lax.rem(p, 2)]
        return pltpu.make_async_copy(*((held, slot_of) if back else (slot_of, held)), temp_sem.at[lax.rem(p, 2)])

    def tile_rows(j):
        late = lax.div(j, 4)
        early_at = jnp.where(j < 2, me, mate) * rows_own + lax.rem(j, 2) * TILE
        row_a = pl.multiple_of(jnp.where(late == 0, early_at, peer * rows_own + (j - 4) * PIECE), PIECE)
        row_b = pl.multiple_of(jnp.where(late == 0, early_at + PIECE, cross * rows_own + (j - 4) * PIECE), PIECE)
        return late, row_a, row_b, [pl.ds(row_a, PIECE), pl.ds(row_b, PIECE)]

    def keep_rows(here, write, value):
        for k, at in enumerate(here):
            write(at, value[k * PIECE : (k + 1) * PIECE])

    def attend(j, carry):
        _, row_a, row_b, here = tile_rows(j)
        first = wide([n_one[at, :] for at in here], 0)
        turn = [wide(pair, 0) for pair in zip(*(rotation(at, PIECE // BLOCK) for at in (row_a, row_b)))]

        def keep_field(s, value):
            def write(at, part):
                fqkv[at, s * width : (s + 1) * width] = part

            keep_rows(here, write, value.astype(BF))

        for s in range(2):
            high, low = split(rotate(dot(first, w_qkv[s]), turn))
            table = dct[:, 0:width]
            spectrum = dot(high, table, NT) + dot(low, table, NT) + dot(high, dct[:, width:], NT)

            def keep_spectrum(at, part):
                spec[s, at, :] = part

            keep_rows(here, keep_spectrum, spectrum)
            keep_field(s, weight_row * jnp.exp(scale_row * spectrum))
        keep_field(2, dot(first, w_qkv[2]))
        return carry

    def project(j, carry):
        pl.when(j >= 4)(lambda: attend(j - 4, None))

        @pl.when(j == 0)
        def _():
            g_tok.local().wait()

            g_cot.local().wait()

        @pl.when(j == 2)
        def _():
            g_tok.to_mate(mate).wait_recv()
            g_cot.to_mate(mate).wait_recv()

        for piece in range(g_tok.pieces):

            @pl.when(j == 4 + piece)
            def _():
                g_tok.to_peer(peer, piece).wait_recv()
                g_tok.forward(peer, piece).start()
                g_cot.to_peer(me, piece).start()
                g_tok.forward(cross, piece).wait_recv()

        late, row_a, _, here = tile_rows(j)
        for at in here:
            pltpu.make_async_copy(tok.at[at], tok_kept.at[at], tok_sem.at[0]).start()
        unit, _ = unit_rows(wide([tok[at, :] for at in here], 0).astype(F32))
        first = (unit * gain_one + bias_one).astype(BF)
        second = (unit * gain_two + bias_two).astype(BF)
        for k, at in enumerate(here):
            n_one[at, :] = first[k * PIECE : (k + 1) * PIECE]
            n_two[at, :] = second[k * PIECE : (k + 1) * PIECE]
        parity = lax.rem(j, 2)
        pl.when(j >= 6)(lambda: slope_copy(j - 6).wait())
        for at in range(0, w_up.shape[1], TILE):
            up = dot(second, w_up[:, at : at + TILE])
            below = 0.5 * (1.0 + lax.erf(up * math.sqrt(0.5)))

            def keep_hidden(rows_at, part):
                hid[rows_at, at : at + TILE] = part

            keep_rows(here, keep_hidden, (up * below).astype(BF))
            temp[parity, :, at : at + TILE] = below + up * (
                jnp.exp(-0.5 * up * up) * (1.0 / math.sqrt(2.0 * math.pi))
            )

        @pl.when(late == 0)
        def _():
            turned = wide([cot[at, :] for at in here], 0)
            first_at = pl.multiple_of(row_a, TILE)
            for at in range(0, hid.shape[1], TILE):
                d_hidden = dot(turned, w_down[at : at + TILE, :], NT)
                d_up[pl.ds(first_at, TILE), at : at + TILE] = (d_hidden * temp[parity, :, at : at + TILE]).astype(BF)

        pl.when(late == 1)(lambda: slope_copy(j - 4).start())
        return carry

    for copy in weight_copies:
        copy.wait()
    with jax.named_scope("project"):
        lax.fori_loop(0, rows // TILE, project, 0)
    for p in (2, 3):
        slope_copy(p).wait()
    for p in range(2):
        slope_copy(p, True).start()

    grid_t = lax.broadcasted_iota(jnp.int32, (CHUNK, CHUNK), 0)
    grid_s = lax.broadcasted_iota(jnp.int32, (CHUNK, CHUNK), 1)
    together = (grid_t < BLOCK) == (grid_s < BLOCK)
    causal = wide([jnp.where((grid_t >= grid_s) & together, 1.0, 0.0).astype(F32)] * heads)
    causal_back = wide([jnp.where((grid_t <= grid_s) & together, 1.0, 0.0).astype(F32)] * heads)
    head_rows = jnp.where(
        lax.broadcasted_iota(jnp.int32, (8, width), 0) == lax.div(lax.broadcasted_iota(jnp.int32, (8, width), 1), HEAD_DIM),
        1.0,
        0.0,
    ).astype(BF)
    both_chunks = range(2)
    both_blocks = range(CHUNK // BLOCK)

    def joined(block):
        return jnp.where(segment(block) == segment(block - 1), jnp.float32(1.0), jnp.float32(0.0))

    def per_head(value):
        return wide([value * masks[h * CHUNK : (h + 1) * CHUNK, :] for h in range(heads)], 0)

    def halves(value):
        return [value[k * BLOCK : (k + 1) * BLOCK] for k in both_blocks]

    def chunk_rows(pair):
        return [pl.ds(pl.multiple_of((2 * pair + c) * CHUNK, CHUNK), CHUNK) for c in both_chunks]

    state[...] = jnp.zeros_like(state)
    krow[...] = jnp.zeros_like(krow)

    def mix(pair, carry):
        diag = diagonal[...].astype(F32)
        here = chunk_rows(pair)
        query, key, value = ([fqkv[at, s * width : (s + 1) * width] for at in here] for s in range(3))
        scores = [split(dot(query[c], per_head(key[c]), NT) * causal) for c in both_chunks]
        turned = [key[c].T for c in both_chunks]
        over = [dot(scores[c][0], per_head(value[c])) for c in both_chunks]
        under = [dot(scores[c][0], masks[...]) + dot(scores[c][1], masks[...]) for c in both_chunks]
        made = [
            dot(turned[c][:, k * BLOCK : (k + 1) * BLOCK], halves(value[c])[k]) * diag
            for c in both_chunks
            for k in both_blocks
        ]
        row_made = [jnp.sum(halves(key[c])[k].astype(F32), 0, keepdims=True) for c in both_chunks for k in both_blocks]
        now, row = state[...], krow[0:1, :]
        carried, rows_in = [], []
        for k in range(4):
            carried.append(now.astype(BF))
            rows_in.append(row)
            states[4 * pair + k] = sum(now[h * HEAD_DIM : (h + 1) * HEAD_DIM] for h in range(heads)).astype(BF)
            ksums[pl.ds(4 * pair + k, 1), :] = row
            keep = joined(4 * pair + k + 1)
            now = (now + made[k]) * keep
            row = (row + row_made[k]) * keep
        state[...] = now
        krow[0:1, :] = row
        for c in both_chunks:
            parts = halves(query[c])
            more = wide([dot(parts[k], carried[2 * c + k]) for k in both_blocks], 0)
            high, low = split(wide([parts[k].astype(F32) * rows_in[2 * c + k] for k in both_blocks], 0))
            inverse = 1.0 / (under[c] + dot(high, diagonal[...]) + dot(low, diagonal[...]))
            attended = (over[c] + more) * inverse
            att[here[c], :] = attended
            rden[here[c], :] = wide([inverse[:, h * HEAD_DIM : h * HEAD_DIM + HEAD_DIM // 2] for h in range(heads)])
            mixed[here[c], :] = attended.astype(BF)

        return carry

    def add_parts(base, first, count, sources):
        cut = min(SUB, count)
        for at in range(0, count, cut):
            total = base[pl.ds(first + at, cut), :].astype(F32)
            for source, place in sources:
                total = total + source[pl.ds(place + at, cut), :].astype(F32)
            base[pl.ds(first + at, cut), :] = total.astype(BF)

    def bring(base, first, box, place, count):
        base[pl.ds(first, count), :] = box[pl.ds(place, count), :]

    half, quarter = UNIT // 2, UNIT // 4

    def rows_of(index, size):
        return pl.multiple_of(index * size, size)

    def unit_of(n):
        return grads.at[pl.ds(pl.multiple_of(n * UNIT, UNIT), UNIT)]

    def hop(box, kind, source, target, device):
        return pltpu.make_async_remote_copy(
            src_ref=source,
            dst_ref=target,
            send_sem=ar_send.at[box, kind],
            recv_sem=ar_recv.at[box, kind],
            device_id={"dp": device},
            device_id_type=MESH,
        )

    plain = units - 3 * width // UNIT
    per_tile = TILE // UNIT

    class Copies:
        def __init__(self, n):
            self.n = n

        def whole(self):
            first = pl.multiple_of(self.n * UNIT, UNIT)
            return pltpu.make_async_copy(unit_of(self.n), grads_out.at[pl.ds(first, UNIT)], grad_sem.at[0])

        def piece(self, q):
            u = self.n - plain
            at = 4 * lax.div(u, per_tile) + q
            row = pl.multiple_of(lax.div(at, 3) * TILE + lax.rem(u, per_tile) * UNIT, UNIT)
            return pltpu.make_async_copy(
                unit_of(self.n).at[:, q * width : (q + 1) * width],
                qkv_out.at[lax.rem(at, 3), pl.ds(row, UNIT)],
                grad_sem.at[1],
            )

        def start(self):
            pl.when(self.n < plain)(lambda: self.whole().start())

            @pl.when(self.n >= plain)
            def _():
                for q in range(4):
                    self.piece(q).start()

    def kind_of(n):
        return lax.rem(n, 2)

    def box_of(n):
        return lax.rem(lax.div(n, 2), BOXES_X), lax.rem(lax.div(n, 2), BOXES_Z)

    def begin(n):
        place, place_b = box_of(n)
        code = 4 * kind_of(n) + middle

        @pl.when(code < 4)
        def _():
            theirs = unit_of(n).at[pl.ds(rows_of(1 - along_x, half), half)]
            hop(place, 0, theirs, recv_a.at[place, pl.ds(0, half)], across).start()

        @pl.when(code == 4)
        def _():
            hop(BOXES_X + place_b, 0, unit_of(n), recv_b.at[place_b, pl.ds(0, UNIT)], inward).start()

    def advance(n, stage):
        kind = jnp.where(n < 0, 2, jnp.where(n >= units, 2, kind_of(n)))
        code = 4 * kind + middle
        place, place_b = box_of(n)

        def case(number):
            return pl.when(code == number)

        base, box = unit_of(n), recv_a.at[place]
        mine_at, theirs_at = rows_of(along_x, half), rows_of(1 - along_x, half)
        own_at = pl.multiple_of(along_x * half + side * quarter, quarter)
        other_at = pl.multiple_of(along_x * half + (1 - side) * quarter, quarter)
        own_in, other_in = rows_of(side, quarter), rows_of(1 - side, quarter)

        def rows(first, size):
            return base.at[pl.ds(first, size)]

        def x_one():
            return hop(place, 0, rows(theirs_at, half), box.at[pl.ds(0, half)], across)

        def z_one():
            return hop(place, 1, rows(mine_at, half), box.at[pl.ds(half, half)], inward)

        def z_two():
            return hop(place, 2, rows(other_at, quarter), box.at[pl.ds(2 * half, quarter)], inward)

        def z_swap():
            return hop(place, 3, rows(own_at, quarter), box.at[pl.ds(swap_at, quarter)], inward)

        def out(kind, first, place_in):
            return hop(place, kind, rows(first, quarter), box.at[pl.ds(half + place_in, quarter)], outward)

        def x_two():
            return hop(place, 6, rows(mine_at, half), box.at[pl.ds(last_at, half)], across)

        swap_at, last_at = 2 * half + quarter, 3 * half

        if stage == 1:

            @case(0)
            def _():
                x_one().wait_recv()
                add_parts(base, mine_at, half, [(box, 0)])
                z_one().start()

        if stage == 2:

            @case(2)
            def _():
                x_one().wait_recv()
                z_one().wait_recv()
                add_parts(base, other_at, quarter, [(box, other_in), (box, half + other_in)])
                z_two().start()

        if stage == 3:

            @case(2)
            def _():
                z_two().wait_recv()
                add_parts(base, own_at, quarter, [(box, own_in), (box, half + own_in), (box, 2 * half)])
                z_swap().start()
                out(4, own_at, own_in).start()

        if stage == 4:

            @case(2)
            def _():
                z_swap().wait_recv()
                z_two().wait_send()
                bring(base, other_at, box, swap_at, quarter)
                out(5, other_at, other_in).start()
                x_two().start()

        if stage == 5:

            @case(0)
            def _():
                z_one().wait_send()
                out(4, own_at, own_in).wait_recv()
                out(5, other_at, other_in).wait_recv()
                bring(base, mine_at, box, half, half)
                x_two().start()

        if stage == 6:

            @case(2)
            def _():
                z_swap().wait_send()
                out(4, own_at, own_in).wait_send()
                out(5, other_at, other_in).wait_send()

            @pl.when(kind == 0)
            def _():
                x_one().wait_send()
                x_two().wait()
                bring(base, theirs_at, box, last_at, half)

        box_b = recv_b.at[place_b]
        mine_z, theirs_z = rows_of(side, half), rows_of(1 - side, half)
        own_x = pl.multiple_of(side * half + along_x * quarter, quarter)
        other_x = pl.multiple_of(side * half + (1 - along_x) * quarter, quarter)
        own_part_at, other_part_at = rows_of(along_x, quarter), rows_of(1 - along_x, quarter)

        def z_in():
            return hop(BOXES_X + place_b, 0, base, box_b.at[pl.ds(0, UNIT)], inward)

        def z_mid():
            return hop(BOXES_X + place_b, 1, rows(theirs_z, half), box_b.at[pl.ds(UNIT, half)], inward)

        def x_mid():
            return hop(BOXES_X + place_b, 2, rows(other_x, quarter), box_b.at[pl.ds(UNIT + half, quarter)], across)

        def x_swap():
            return hop(BOXES_X + place_b, 3, rows(own_x, quarter), box_b.at[pl.ds(swap_at, quarter)], across)

        def z_share():
            return hop(BOXES_X + place_b, 4, rows(mine_z, half), box_b.at[pl.ds(last_at, half)], inward)

        def z_out(kind, first):
            return hop(BOXES_X + place_b, kind, rows(first, half), box_b.at[pl.ds(first, half)], outward)

        swap_at, last_at = UNIT + half + quarter, 2 * UNIT

        if stage == 1:

            @case(6)
            def _():
                z_in().wait_recv()
                add_parts(base, theirs_z, half, [(box_b, theirs_z)])
                z_mid().start()

        if stage == 2:

            @case(6)
            def _():
                z_mid().wait_recv()
                add_parts(base, other_x, quarter, [(box_b, other_x), (box_b, UNIT + other_part_at)])
                x_mid().start()

        if stage == 3:

            @case(6)
            def _():
                x_mid().wait_recv()
                add_parts(
                    base, own_x, quarter, [(box_b, own_x), (box_b, UNIT + own_part_at), (box_b, UNIT + half)]
                )
                x_swap().start()

        if stage == 4:

            @case(6)
            def _():
                x_swap().wait_recv()
                x_mid().wait_send()
                bring(base, other_x, box_b, swap_at, quarter)
                z_share().start()
                z_out(5, mine_z).start()

        if stage == 5:

            @case(6)
            def _():
                z_share().wait_recv()
                z_mid().wait_send()
                bring(base, theirs_z, box_b, last_at, half)
                z_out(6, theirs_z).start()

        if stage == 6:

            @case(6)
            def _():
                x_swap().wait_send()
                z_share().wait_send()
                z_out(5, mine_z).wait_send()
                z_out(6, theirs_z).wait_send()

            @case(4)
            def _():
                z_in().wait_send()
                z_out(5, mine_z).wait_recv()
                z_out(6, theirs_z).wait_recv()
                bring(base, 0, box_b, 0, UNIT)

            pl.when(kind < 2)(lambda: Copies(n).start())

    def at_ready(n):
        return jnp.where(n < LEAD, 1, jnp.where(n < plain, 0, jnp.where(n < plain + LEAD, 1, 0)))

    def ready(first, count):
        for n in (first + k for k in range(count)):
            if reduce_dp:
                pl.when(at_ready(n) == 1)(functools.partial(begin, n))
            else:
                Copies(n).start()

    def tick(t):
        if reduce_dp:
            with jax.named_scope("dp_tick"):
                move(t)

    def move(t):
        for stage in (6, 5, 4, 3, 2, 1):
            advance(t - LAG * (stage - 1), stage)
        later = t + LEAD

        @pl.when(jnp.where(later >= units, 1, at_ready(later)) == 0)
        def _():
            begin(later)

    def tick_at(j, every, first):
        @pl.when(lax.rem(j, every) == every - 1)
        def _():
            tick(first + lax.div(j, every))

    ticks = units + 5 * LAG

    def run_ticks(first, last):
        lax.fori_loop(first, last, pause, 0)

    def pause(t, carry):
        tick(t)
        return carry

    def landed(which, number):
        if which:
            return n_one.at[pl.ds(pl.multiple_of(number * TILE, TILE), TILE)]
        return rs_in.at[number]

    def late_landed(number):
        return n_one.at[pl.ds(pl.multiple_of((6 + number) * TILE, TILE), TILE)]

    def crossed(which, number):
        at = pl.multiple_of((4 + number) * TILE, TILE)
        return n_one.at[pl.ds(at, TILE)] if which else y_in.at[number]

    def to_mate(which, number, late=False):
        return pltpu.make_async_remote_copy(
            src_ref=rs_out.at[lax.rem(number, 2)],
            dst_ref=late_landed(number - 2) if late else landed(which, number),
            send_sem=rs_send.at[which, number],
            recv_sem=rs_recv.at[which, number],
            device_id={"tensor": mate},
            device_id_type=MESH,
        )

    def to_peer(which, number):
        return pltpu.make_async_remote_copy(
            src_ref=landed(which, number),
            dst_ref=crossed(which, number),
            send_sem=rs_send.at[which, 4 + number],
            recv_sem=rs_recv.at[which, 4 + number],
            device_id={"tensor": peer},
            device_id_type=MESH,
        )

    def scatter(j, which, compute):
        owner = jnp.where(j < 2, cross, jnp.where(j < 4, peer, mate))
        number = lax.rem(j, 2)
        row0 = pl.multiple_of(owner * rows_own + number * TILE, TILE)

        @pl.when(lax.div(j, 2) != 1)
        def _():
            at = jnp.where(j < 2, j, j - 2)
            pl.when(j >= 4)(lambda: to_mate(which, number).wait_send())

            def put(columns, part):
                rs_out[number, :, columns] = part.astype(BF)

            compute(row0, put)
            if which:
                to_mate(which, at).start()
            else:
                pl.when(j < 2)(lambda: to_mate(0, at).start())
                pl.when(j >= 4)(lambda: to_mate(0, at, True).start())

        @pl.when(lax.div(j, 2) == 1)
        def _():
            to_mate(which, number).wait_recv()

            here = landed(which, number)

            def put(columns, part):
                here[:, columns] = (here[:, columns].astype(F32) + part).astype(BF)

            compute(row0, put)
            to_peer(which, number).start()

    def gathered(which, number):
        to_mate(which, 2 + number, not which).wait_recv()
        to_peer(which, number).wait_recv()

    def stored(which, number):
        result = input_grad if which else mixed_out
        here = rs_out.at[number] if which else late_landed(number)
        target = result.at[pl.ds(pl.multiple_of(number * TILE, TILE), TILE)]
        return pltpu.make_async_copy(here, target, result_sem.at[which, number])

    pltpu.make_async_copy(tok.at[pl.ds(0, rows)], tok_kept, tok_sem.at[0]).wait()
    for piece in range(g_tok.pieces):
        g_tok.forward(peer, piece).wait_send()

    def keep_unit(n, value):
        grads[pl.ds(pl.multiple_of(n * UNIT, UNIT), value.shape[0]), :] = value
        ready(n, value.shape[0] // UNIT)

    first_out = hid.shape[1] // UNIT
    first_up = first_out + width // UNIT

    def arrive(piece):
        g_cot.to_peer(peer, piece).wait_recv()
        g_cot.forward(peer, piece).start()

    def down(piece):
        g_cot.forward(cross, piece).wait_recv()
        tile = dot(cot[:, piece * TILE : (piece + 1) * TILE], hid[...], TN)
        keep_unit(per_tile * piece, tile.astype(BF))

    def mix_some(first, last):
        with jax.named_scope("mixer"):
            lax.fori_loop(first, last, mix, 0)

    pairs = chunks // 2
    tiles = rows // TILE
    with jax.named_scope("grad_down"):
        lax.fori_loop(tiles - 4, tiles - 2, attend, 0)
        arrive(0)
        down(0)
        lax.fori_loop(tiles - 2, tiles, attend, 0)
        arrive(1)
        run_ticks(0, 2)
        down(1)
    mix_some(0, pairs // 4)
    run_ticks(2, 4)
    arrive(2)
    mix_some(pairs // 4, pairs // 2)
    run_ticks(4, 5)
    with jax.named_scope("grad_down"):
        down(2)
    run_ticks(5, 7)
    mix_some(pairs // 2, 3 * pairs // 4)
    run_ticks(7, 8)
    arrive(3)
    mix_some(3 * pairs // 4, pairs)
    run_ticks(8, 10)
    with jax.named_scope("grad_down"):
        down(3)
    run_ticks(10, 12)
    keep_unit(first_out, dot(mixed[...], cot[...], TN).astype(BF))
    run_ticks(12, 14)

    column_tiles = [slice(at, at + TILE) for at in range(0, cot.shape[1], TILE)]

    def branch(row0, put):
        here = pl.ds(row0, TILE)
        left, right = mixed[here, :], hid[here, :]
        for columns in column_tiles:
            put(columns, dot(left, w_out[:, columns]) + dot(right, w_down[:, columns]))

    def keep_temp(number):
        def put(columns, part):
            temp[number, :, columns] = part

        return put

    def produce(j, carry):
        scatter(j, 0, branch)
        run_ticks(14 + j, 15 + j)
        return carry

    with jax.named_scope("outputs"):
        lax.fori_loop(0, 4, produce, 0)

    def descend(p, carry):
        here = [pl.ds(pl.multiple_of(owner * rows_own + p * PIECE, PIECE), PIECE) for owner in (peer, cross)]
        parity = lax.rem(p, 2)
        slope_copy(p, True).wait()
        turned = wide([cot[at, :] for at in here], 0)
        for at in range(0, hid.shape[1], TILE):
            d_hidden = dot(turned, w_down[at : at + TILE, :], NT)
            value = (d_hidden * temp[parity, :, at : at + TILE]).astype(BF)
            for k, rows_at in enumerate(here):
                d_up[rows_at, at : at + TILE] = value[k * PIECE : (k + 1) * PIECE]
        pl.when(p < 2)(lambda: slope_copy(p + 2, True).start())
        return carry

    with jax.named_scope("grad_gelu"):
        lax.fori_loop(0, 4, descend, 0)
    def upward(j, carry):
        at = pl.ds(pl.multiple_of(j * TILE, TILE), TILE)
        keep_unit(first_up + per_tile * j, dot(n_two[:, at], d_up[...], TN).astype(BF))
        run_ticks(18 + j, 19 + j)
        return carry

    with jax.named_scope("grad_up"):
        lax.fori_loop(0, n_two.shape[1] // TILE, upward, 0)

    state[...] = jnp.zeros_like(state)
    krow[...] = jnp.zeros_like(krow)
    feat_sums[...] = jnp.zeros_like(feat_sums)

    def unmix(step, carry):
        pair = chunks // 2 - 1 - step
        diag = diagonal[...].astype(F32)
        row_pair = pl.multiple_of(pair * 2 * CHUNK, 2 * CHUNK)
        d_mixed = dot(cot[pl.ds(row_pair, 2 * CHUNK), :], w_out[...], NT)
        here = chunk_rows(pair)
        query, key, value = ([fqkv[at, s * width : (s + 1) * width] for at in here] for s in range(3))
        d_over, under_parts = [], []
        for c in both_chunks:
            packed = rden[here[c], :]
            inverse = wide(
                [packed[:, h // 2 * HEAD_DIM // 2 : (h // 2 + 1) * HEAD_DIM // 2] for h in range(2 * heads)]
            )
            d_over.append(d_mixed[c * CHUNK : (c + 1) * CHUNK] * inverse)
            under_parts.append(split(d_over[c] * att[here[c], :]))
        d_under = [-dot(part[0], diagonal[...]) - dot(part[1], diagonal[...]) for part in under_parts]
        under_row = [-dot(head_rows, under_parts[c][0], NT) - dot(head_rows, under_parts[c][1], NT) for c in both_chunks]
        over_split = [split(d_over[c]) for c in both_chunks]
        over_both = [wide(over_split[c]) for c in both_chunks]
        over_heads = [wide([per_head(part) for part in over_split[c]]) for c in both_chunks]
        query_heads, key_heads, value_heads = ([per_head(field[c]) for c in both_chunks] for field in (query, key, value))
        scores_back = [(dot(key[c], query_heads[c], NT) * causal_back).astype(BF) for c in both_chunks]
        d_scores = [dot(over_both[c], wide([value_heads[c]] * 2), NT) for c in both_chunks]
        d_back = [dot(wide([value[c]] * 2), over_heads[c], NT) for c in both_chunks]
        turned = [query[c].T for c in both_chunks]
        made = []
        for c in both_chunks:
            for k in both_blocks:
                left = turned[c][:, k * BLOCK : (k + 1) * BLOCK]
                made.append(dot(wide([left, left]), wide([halves(part)[k] for part in over_split[c]], 0)) * diag)
        d_scores = [
            wide(
                split(
                    (
                        d_scores[c]
                        + wide(
                            [
                                jnp.broadcast_to(d_under[c][:, h * HEAD_DIM : h * HEAD_DIM + 1], (CHUNK, CHUNK))
                                for h in range(heads)
                            ]
                        )
                    )
                    * causal
                )
            )
            for c in both_chunks
        ]
        d_back = [
            wide(split((d_back[c] + wide([under_row[c][h : h + 1, :] for h in range(heads)])) * causal_back))
            for c in both_chunks
        ]
        d_query = [dot(d_scores[c], wide([key_heads[c]] * 2, 0)) for c in both_chunks]
        d_key = [dot(d_back[c], wide([query_heads[c]] * 2, 0)) for c in both_chunks]
        d_value = [dot(scores_back[c], over_heads[c]) for c in both_chunks]
        later, later_row = state[...], krow[0:1, :]
        more = {}
        for at in reversed(range(4)):
            c, k = divmod(at, 2)
            block = 4 * pair + at
            query_k, key_k, value_k, both_k, under_k = (
                halves(field[c])[k] for field in (query, key, value, over_both, d_under)
            )
            carried = wide([states[block]] * heads, 0) * diagonal[...]
            keep = joined(block + 1)
            later, later_row = later * keep, later_row * keep
            high, low = split(later)
            more[at] = (
                dot(both_k, wide([carried, carried]), NT) + under_k * ksums[pl.ds(block, 1), :],
                dot(wide([value_k, value_k]), wide([high, low]), NT) + later_row,
                dot(wide([key_k, key_k]), wide([high, low], 0)),
            )
            later = later + made[at]
            later_row = later_row + jnp.sum(query_k.astype(F32) * under_k, 0, keepdims=True)
        state[...] = later
        krow[0:1, :] = later_row
        turn = rotation(row_pair, 2 * CHUNK // BLOCK)
        here = pl.ds(row_pair, 2 * CHUNK)
        for s, found in enumerate((d_query, d_key)):
            grad = wide(found, 0) + wide([more[at][s] for at in range(4)], 0)
            spectrum = spec[s, here, :]
            grad = grad * (weight_row * jnp.exp(scale_row * spectrum))
            feat_sums[0:1, :] += jnp.sum(grad * spectrum, 0, keepdims=True)
            feat_sums[1:2, :] += jnp.sum(grad, 0, keepdims=True)
            high, low = split(grad * scale_row)
            back = dot(high, dct[:, 0:width]) + dot(low, dct[:, 0:width]) + dot(high, dct[:, width:])
            fqkv[here, s * width : (s + 1) * width] = rotate(back, turn, True).astype(BF)
        d_value = wide([d_value[c][:, :width] + d_value[c][:, width:] for c in both_chunks], 0)
        fqkv[here, 2 * width : 3 * width] = (d_value + wide([more[at][2] for at in range(4)], 0)).astype(BF)
        run_ticks(22 + lax.div(14 * step, chunks // 2), 22 + lax.div(14 * (step + 1), chunks // 2))

        return carry

    with jax.named_scope("mixer_back"):
        lax.fori_loop(0, chunks // 2, unmix, 0)

    def projected(j, carry):
        tile = dot(n_one[:, pl.ds(pl.multiple_of(j * TILE, TILE), TILE)], fqkv[...], TN).astype(BF)
        for s in range(3):
            at = 3 * j + s
            first = pl.multiple_of(plain * UNIT + lax.div(at, 4) * TILE, TILE)
            columns = pl.ds(pl.multiple_of(lax.rem(at, 4) * width, width), width)
            grads[pl.ds(first, TILE), columns] = tile[:, s * width : (s + 1) * width]

        @pl.when(j >= 1)
        def _():
            ready(plain + (j - 1) * per_tile, per_tile)

        return carry

    with jax.named_scope("grad_qkv"):
        lax.fori_loop(0, n_one.shape[1] // TILE, projected, 0)
    pl.semaphore_signal(free_mate, inc=1, device_id={"tensor": mate}, device_id_type=MESH)
    pl.semaphore_signal(free_peer, inc=1, device_id={"tensor": peer}, device_id_type=MESH)
    run_ticks(36, 38)

    sums[...] = jnp.zeros_like(sums)

    def row_of(j):
        owner = jnp.where(j < 2, cross, jnp.where(j < 4, peer, jnp.where(j < 6, mate, me)))
        return pl.multiple_of(owner * rows_own + lax.rem(j, 2) * TILE, TILE)

    def tok_copy(j):
        which = lax.rem(j, 2)
        return pltpu.make_async_copy(
            tok_kept.at[pl.ds(row_of(j), TILE)], n_two.at[pl.ds(pl.multiple_of(which * TILE, TILE), TILE)], tok_sem.at[which]
        )

    def row_grads(j):
        def compute(row0, put):
            here = pl.ds(row0, TILE)
            unit, _ = unit_rows(n_two[pl.ds(pl.multiple_of(lax.rem(j, 2) * TILE, TILE), TILE), :].astype(F32))
            fields = [fqkv[here, s * width : (s + 1) * width] for s in range(3)]
            right = d_up[here, :]
            for columns in column_tiles:
                one = sum(dot(fields[s], w_qkv[s, columns, :], NT) for s in range(3))
                two = dot(right, w_up[columns, :], NT)
                part = unit[:, columns]
                for number, term in enumerate((one * part, one, two * part, two)):
                    sums[number, :, columns] += jnp.sum(term.reshape(TILE // 8, 8, TILE), 0)
                put(columns, one * gain_one[:, columns] + two * gain_two[:, columns])

        return compute

    tok_copy(0).start()

    def own_tok(number):
        here = n_two.at[pl.ds((2 + number) * TILE, TILE)]
        return pltpu.make_async_copy(tok_in.at[pl.ds(number * TILE, TILE)], here, local_sem.at[number])

    for number in range(2):
        own_tok(number).start()

    def finish(number):
        gathered(0, number)
        tokens, result = n_two.at[pl.ds((2 + number) * TILE, TILE)], late_landed(number)

        def put(columns, part):
            total = part + result[:, columns].astype(F32) + y_in[number, :, columns].astype(F32)
            result[:, columns] = (total + tokens[:, columns].astype(F32)).astype(BF)

        branch(pl.multiple_of(me * rows_own + number * TILE, TILE), put)
        stored(0, number).start()

    pl.semaphore_wait(free_mate, 1)
    pl.semaphore_wait(free_peer, 1)

    def produce_late(j, carry):
        scatter(j, 0, branch)
        return carry

    with jax.named_scope("outputs"):
        lax.fori_loop(4, 6, produce_late, 0)
    for number in range(2):
        to_mate(0, 2 + number, True).wait_send()

    def inputs(j, carry):
        tok_copy(j).wait()
        pl.when(j < 7)(lambda: tok_copy(j + 1).start())

        @pl.when(j < 6)
        def _():
            scatter(j, 1, row_grads(j))

        @pl.when(j >= 6)
        def _():
            row_grads(j)(row_of(j), keep_temp(lax.rem(j, 2)))

        run_ticks(38 + 2 * j, 40 + 2 * j)
        return carry

    with jax.named_scope("row_grads"):
        lax.fori_loop(0, 8, inputs, 0)
    def conclude(number):
        gathered(1, number)
        tokens = n_two.at[pl.ds((2 + number) * TILE, TILE)]
        from_mate, from_peer = landed(1, 2 + number), crossed(1, number)

        def step(i, inner):
            at = pl.ds(pl.multiple_of(i * PIECE, PIECE), PIECE)
            group_at = pl.multiple_of(me * rows_own + number * TILE + i * PIECE, PIECE)
            unit, deviation = unit_rows(tokens[at, :].astype(F32))
            total = temp[number, at, :] + from_mate[at, :].astype(F32) + from_peer[at, :].astype(F32)
            along = jnp.mean(total * unit, -1, keepdims=True)
            total = total - jnp.mean(total, -1, keepdims=True) - unit * along
            total = cot[pl.ds(group_at, PIECE), :].astype(F32) + deviation * total
            rs_out[number, at, :] = total.astype(BF)
            return inner

        lax.fori_loop(0, TILE // PIECE, step, 0)
        stored(1, number).start()

    small[...] = jnp.zeros_like(small)
    for number in range(4):
        small[number : number + 1, :] = jnp.sum(sums[number], 0, keepdims=True)
    small[4:5, 0:width] = feat_sums[0:1, :]
    small[5:6, 0:width] = feat_sums[1:2, :] / weight_row

    def small_hops(axis, own, count, boxes, first):
        hops = []
        for step in range(1, count):
            hops.append(
                pltpu.make_async_remote_copy(
                    src_ref=small,
                    dst_ref=boxes.at[own],
                    send_sem=small_send.at[first + step - 1],
                    recv_sem=small_recv.at[first + step - 1],
                    device_id={axis: lax.rem(own + step, count)},
                    device_id_type=MESH,
                )
            )
        return hops

    over_tensor = small_hops("tensor", me, 4, small_in, 0)
    over_dp = small_hops("dp", group, members, small_wide, 3)

    def small_step(k):
        if k == 0:
            for copy in over_tensor:
                copy.start()
            small_in[me] = small[...]
        if k == 1:
            for copy in over_tensor:
                copy.wait()
            total = small_in[0]
            for member in range(1, 4):
                total = total + small_in[member]
            small[0:4, :] = total[0:4, :]
        if k == 1 and reduce_dp:
            for copy in over_dp:
                copy.start()
            small_wide[group] = small[...]
        if k == 2 and reduce_dp:
            for copy in over_dp:
                copy.wait()
            total = small_wide[0]
            for member in range(1, members):
                total = total + small_wide[member]
            small[...] = total

    for number in range(2):
        to_mate(1, 2 + number).wait_send()
        own_tok(number).wait()
    small_step(0)
    run_ticks(54, 56)
    finish(0)
    small_step(1)
    run_ticks(56, 58)
    finish(1)
    conclude(0)
    run_ticks(58, 60)
    conclude(1)
    small_step(2)
    if reduce_dp:
        run_ticks(60, ticks)
    for h in range(heads):
        at = slice(h * HEAD_DIM, (h + 1) * HEAD_DIM)
        feat_out[0, h : h + 1, :] = small[4:5, at]
        feat_out[1, h : h + 1, :] = small[5:6, at]

    pltpu.make_async_copy(grads.at[pl.ds(0, plain * UNIT)], grads_out, grad_sem.at[0]).wait()
    pltpu.make_async_copy(w_qkv, qkv_out, grad_sem.at[1]).wait()
    for number in range(2):
        to_peer(0, number).wait_send()
        to_peer(1, number).wait_send()
        for which in range(2):
            stored(which, number).wait()

    for gather in (g_tok, g_cot):
        gather.to_mate(me).wait_send()
        for piece in range(gather.pieces):
            gather.to_peer(me, piece).wait_send()
    for piece in range(g_cot.pieces):
        g_cot.forward(peer, piece).wait_send()


def widen(down_in, out_in, up_in, qkv_in, small_in, feats_in, mixed_in, input_in, *outs):
    down, out, up, qkv, *norms, scale, weight, mixed, input_grad = outs
    down[...] = down_in[...].astype(F32).T
    out[...] = out_in[...].astype(F32)
    up[...] = up_in[...].astype(F32)
    qkv[...] = qkv_in[...].astype(F32)
    for number, norm in enumerate(norms):
        norm[...] = small_in[number : number + 1, :]
    scale[...] = feats_in[0]
    weight[...] = feats_in[1]
    mixed[...] = mixed_in[...]
    input_grad[...] = input_in[...]


def shards(
    reduce_dp,
    tokens,
    ln1_gain,
    ln1_bias,
    ln2_gain,
    ln2_bias,
    w_qkv,
    w_out,
    w_up,
    w_down,
    feature_scale,
    feature_weight,
    lengths,
    cotangent,
):
    rows_own, model = tokens.shape
    rows = 4 * rows_own
    heads = feature_scale.shape[0]
    width = heads * HEAD_DIM
    hidden = w_up.shape[1]
    consts = tables(rows // BLOCK, heads)
    norms = [value.reshape(1, model) for value in (ln1_gain, ln1_bias, ln2_gain, ln2_bias)]
    anywhere = pl.BlockSpec(memory_space=pl.ANY)
    vmem = pl.BlockSpec(memory_space=pltpu.VMEM)
    smem = pl.BlockSpec(memory_space=pltpu.SMEM)
    shape = jax.ShapeDtypeStruct
    plain = 2 * hidden + width
    units = (plain + 3 * width) // UNIT
    mixed_out, input_grad, grads, g_qkv, _, _, small, feats = pl.pallas_call(
        functools.partial(kernel, reduce_dp),
        out_shape=(
            shape((rows_own, model), BF),
            shape((rows_own, model), BF),
            shape((plain, model), BF),
            shape((3, model, width), BF),
            shape((rows // 2, hidden), F32),
            shape((rows, model), BF),
            shape((8, model), F32),
            shape((2, heads, HEAD_DIM), F32),
        ),
        in_specs=[smem, anywhere, anywhere] + [vmem] * 4 + [anywhere] * 4 + [vmem] * 6,
        out_specs=(anywhere,) * 6 + (vmem, vmem),
        scratch_shapes=[
            pltpu.VMEM((rows, model), BF),
            pltpu.VMEM((rows, model), BF),
            pltpu.VMEM((rows, model), BF),
            pltpu.VMEM((rows, hidden), BF),
            pltpu.VMEM((rows, hidden), BF),
            pltpu.VMEM((rows, 3 * width), BF),
            pltpu.VMEM((2, rows, width), F32),
            pltpu.VMEM((rows, width), BF),
            pltpu.VMEM((rows, width), F32),
            pltpu.VMEM((rows, width // 2), F32),
            pltpu.VMEM((rows // BLOCK, HEAD_DIM, width), BF),
            pltpu.VMEM((rows // BLOCK, width), F32),
            pltpu.VMEM((width, width), F32),
            pltpu.VMEM((8, width), F32),
            pltpu.VMEM((units * UNIT, model), BF),
            pltpu.VMEM((BOXES_X, 2 * UNIT, model), BF),
            pltpu.VMEM((BOXES_Z, 5 * UNIT // 2, model), BF),
            pltpu.VMEM((2, TILE, model), BF),
            pltpu.VMEM((2, TILE, model), BF),
            pltpu.VMEM((2, TILE, model), BF),
            pltpu.VMEM((2, TILE, model), F32),
            pltpu.VMEM((4, 8, model), F32),
            pltpu.VMEM((8, width), F32),
            pltpu.VMEM((4, 8, model), F32),
            pltpu.VMEM((8, 8, model), F32),
            pltpu.VMEM(w_qkv.shape, BF),
            pltpu.VMEM(w_out.shape, BF),
            pltpu.VMEM(w_up.shape, BF),
            pltpu.VMEM(w_down.shape, BF),
            pltpu.SemaphoreType.DMA((2 + 2 * rows_own // PIECE,)),
            pltpu.SemaphoreType.DMA((2 + 2 * rows_own // PIECE + 2 * model // TILE,)),
            pltpu.SemaphoreType.DMA((2 + 2 * rows_own // PIECE + 2 * model // TILE,)),
            pltpu.SemaphoreType.DMA((4,)),
            pltpu.SemaphoreType.DMA((BOXES_X + BOXES_Z, 7)),
            pltpu.SemaphoreType.DMA((BOXES_X + BOXES_Z, 7)),
            pltpu.SemaphoreType.DMA((2, 6)),
            pltpu.SemaphoreType.DMA((2, 6)),
            pltpu.SemaphoreType.DMA((10,)),
            pltpu.SemaphoreType.DMA((10,)),
            pltpu.SemaphoreType.DMA((2,)),
            pltpu.SemaphoreType.DMA((2,)),
            pltpu.SemaphoreType.DMA((2,)),
            pltpu.SemaphoreType.DMA((2, 2)),
            pltpu.SemaphoreType.REGULAR,
            pltpu.SemaphoreType.REGULAR,
        ],
        compiler_params=pltpu.CompilerParams(
            collective_id=0, has_side_effects=True, vmem_limit_bytes=62 * 2**20
        ),
    )(lengths, tokens, cotangent, *norms, w_qkv, w_out, w_up, w_down, feature_scale, feature_weight, *consts)
    if not reduce_dp:
        grads, g_qkv, small, feats = lax.psum(
            (*lax.optimization_barrier((grads.astype(F32), g_qkv.astype(F32))), small, feats), "dp"
        )
    steps = 4
    down_cut, out_cut, up_cut, row_cut, own_cut = (
        size // steps for size in (hidden, width, model, model, rows_own)
    )
    rows_spec = pl.BlockSpec((own_cut, model), lambda i: (i, 0))
    row_spec = pl.BlockSpec((1, model), lambda i: (0, 0))
    feat_spec = pl.BlockSpec((heads, HEAD_DIM), lambda i: (0, 0))
    g_down, g_out, g_up, g_qkv, *norm_sums, g_scale, g_weight, mixed_out, input_grad = pl.pallas_call(
        widen,
        grid=(steps,),
        out_shape=(
            shape((hidden, model), F32),
            shape((width, model), F32),
            shape((model, hidden), F32),
            shape((3, model, width), F32),
            *[shape((1, model), F32)] * 4,
            *[shape((heads, HEAD_DIM), F32)] * 2,
            *[shape((rows_own, model), BF)] * 2,
        ),
        in_specs=[
            pl.BlockSpec((model, down_cut), lambda i: (0, i)),
            pl.BlockSpec((out_cut, model), lambda i: (hidden // out_cut + i, 0)),
            pl.BlockSpec((up_cut, hidden), lambda i: ((hidden + width) // up_cut + i, 0)),
            pl.BlockSpec((3, row_cut, width), lambda i: (0, i, 0)),
            pl.BlockSpec((8, model), lambda i: (0, 0)),
            pl.BlockSpec((2, heads, HEAD_DIM), lambda i: (0, 0, 0)),
            rows_spec,
            rows_spec,
        ],
        out_specs=(
            pl.BlockSpec((down_cut, model), lambda i: (i, 0)),
            pl.BlockSpec((out_cut, model), lambda i: (i, 0)),
            pl.BlockSpec((up_cut, hidden), lambda i: (i, 0)),
            pl.BlockSpec((3, row_cut, width), lambda i: (0, i, 0)),
            *[row_spec] * 4,
            *[feat_spec] * 2,
            *[rows_spec] * 2,
        ),
        compiler_params=pltpu.CompilerParams(vmem_limit_bytes=60 * 2**20),
    )(grads, grads, grads, g_qkv, small, feats, mixed_out, input_grad)
    return (
        mixed_out,
        input_grad,
        *[value.reshape(model) for value in norm_sums],
        g_qkv,
        g_out,
        g_up,
        g_down,
        g_scale,
        g_weight,
    )


def solution(mesh):
    placed = (
        P(("dp", "tensor"), None),
        P(),
        P(),
        P(),
        P(),
        P(None, None, "tensor"),
        P("tensor", None),
        P(None, "tensor"),
        P("tensor", None),
        P("tensor", None),
        P("tensor", None),
        P("dp", None),
        P(("dp", "tensor"), None),
    )
    return jax.shard_map(
        functools.partial(shards, mesh.shape["dp"] == 8),
        mesh=mesh,
        in_specs=placed,
        out_specs=(
            P(("dp", "tensor"), None),
            P(("dp", "tensor"), None),
            P(),
            P(),
            P(),
            P(),
            P(None, None, "tensor"),
            P("tensor", None),
            P(None, "tensor"),
            P("tensor", None),
            P("tensor", None),
            P("tensor", None),
        ),
        check_vma=False,
    )
```

```python
import functools
import math

import jax
import jax.numpy as jnp
import ml_dtypes
import numpy as np
from jax import lax
from jax.experimental import pallas as pl
from jax.experimental.pallas import tpu as pltpu
from jax.sharding import PartitionSpec as P

HEAD_DIM = 64
ROT = 16
BLOCK = 64
CHUNK = 128
TILE = 256
PIECE = 128
UNIT = 64
SUB = 32
LEAD = 2
LAG = 2
BOXES_X = 6
BOXES_Z = 6
MESH = pl.DeviceIdType.MESH
F32 = jnp.float32
BF = jnp.bfloat16
NN = (((1,), (0,)), ((), ()))
NT = (((1,), (1,)), ((), ()))
TN = (((0,), (0,)), ((), ()))


def dot(left, right, dims=NN):
    return lax.dot_general(left, right, dims, preferred_element_type=F32)


def split(value):
    high = value.astype(BF)
    return high, (value - high.astype(F32)).astype(BF)


def wide(parts, axis=1):
    return jnp.concatenate(parts, axis)


def tables(blocks, heads):
    width = heads * HEAD_DIM
    freq, dims = np.arange(HEAD_DIM)[:, None], np.arange(HEAD_DIM)[None, :]
    dct = np.cos(np.pi * (dims + 0.5) * freq / HEAD_DIM) * math.sqrt(2.0 / HEAD_DIM)
    dct[0] *= math.sqrt(0.5)
    dct = np.kron(np.eye(heads), dct).astype(np.float32)
    high = dct.astype(ml_dtypes.bfloat16)
    low = (dct - high.astype(np.float32)).astype(ml_dtypes.bfloat16)
    halves = np.concatenate([high, low], 1)
    half = ROT // 2
    lane = np.arange(2 * HEAD_DIM) % HEAD_DIM
    rate = np.where(lane < ROT, 10000.0 ** (-(lane % half) * 2.0 / ROT), 0.0)
    in_block = np.arange(BLOCK)[:, None] * rate[None]
    of_block = np.arange(blocks)[:, None] * BLOCK * rate[None]
    signs = np.stack([np.where(lane < half, -1.0, 0.0), np.where((lane >= half) & (lane < ROT), 1.0, 0.0)] + [0.0 * lane] * 6)
    angles = np.concatenate([np.cos(in_block), np.sin(in_block), np.cos(of_block), np.sin(of_block), signs], 0)
    block_ones = np.kron(np.eye(heads), np.ones((HEAD_DIM, HEAD_DIM)))
    masks = np.kron(np.eye(heads), np.ones((CHUNK, HEAD_DIM)))
    return (
        halves,
        angles.astype(np.float32),
        block_ones.astype(ml_dtypes.bfloat16),
        masks.astype(ml_dtypes.bfloat16),
    )


def kernel(
    reduce_dp,
    lengths,
    tok_in,
    cot_in,
    gain_one_in,
    bias_one_in,
    gain_two_in,
    bias_two_in,
    w_qkv_in,
    w_out_in,
    w_up_in,
    w_down_in,
    feature_scale,
    feature_weight,
    dct,
    angles,
    diagonal,
    masks,
    mixed_out,
    input_grad,
    grads_out,
    qkv_out,
    slopes,
    tok_kept,
    small,
    feat_out,
    cot,
    n_one,
    n_two,
    hid,
    d_up,
    fqkv,
    spec,
    mixed,
    att,
    rden,
    states,
    ksums,
    state,
    krow,
    grads,
    recv_a,
    recv_b,
    rs_out,
    rs_in,
    y_in,
    temp,
    sums,
    feat_sums,
    small_in,
    small_wide,
    w_qkv,
    w_out,
    w_up,
    w_down,
    local_sem,
    send_sem,
    recv_sem,
    weight_sem,
    ar_send,
    ar_recv,
    rs_send,
    rs_recv,
    small_send,
    small_recv,
    grad_sem,
    temp_sem,
    tok_sem,
    result_sem,
    free_mate,
    free_peer,
):
    rows_own = tok_in.shape[0]
    rows = cot.shape[0]
    tok = grads
    width = w_out_in.shape[0]
    heads = width // HEAD_DIM
    chunks = rows // CHUNK
    me = lax.axis_index("tensor")
    core = lax.rem(me, 2)
    mate = me + 1 - 2 * core
    peer = lax.rem(me + 2, 4)
    cross = 3 - me
    group = lax.axis_index("dp")
    along_x = lax.rem(group, 2)
    across = group + 1 - 2 * along_x
    along_z = lax.div(group, 2)
    middle = along_z * (3 - along_z)

    def at_end(step):
        pl.when(middle == 0)(step)

    def at_mid(step):
        pl.when(middle > 0)(step)

    side = jnp.where(along_z < 2, 0, 1)
    inward = group + 2 - 4 * side
    outward = jnp.where(middle == 0, inward, group - 2 + 4 * side)
    units = grads.shape[0] // UNIT

    weight_copies = [
        pltpu.make_async_copy(source, target, weight_sem.at[k])
        for k, (source, target) in enumerate(
            ((w_qkv_in, w_qkv), (w_up_in, w_up), (w_out_in, w_out), (w_down_in, w_down))
        )
    ]
    for copy in weight_copies:
        copy.start()

    barrier = pltpu.get_barrier_semaphore()
    members = 8 if reduce_dp else 1
    for step in range(1, 4):
        other = lax.rem(me + step, 4)
        pl.semaphore_signal(barrier, inc=1, device_id={"tensor": other}, device_id_type=MESH)
    for step in range(1, members):
        other = lax.rem(group + step, members)
        pl.semaphore_signal(barrier, inc=1, device_id={"dp": other}, device_id_type=MESH)
    pl.semaphore_wait(barrier, 2 + members)

    def slot(buf, owner, piece=None, columns=False):
        if piece is None:
            return buf.at[pl.ds(pl.multiple_of(owner * rows_own, rows_own), rows_own)]
        if columns:
            here = pl.ds(pl.multiple_of(owner * rows_own, rows_own), rows_own)
            return buf.at[here, piece * TILE : (piece + 1) * TILE]
        return buf.at[pl.ds(pl.multiple_of(owner * rows_own + piece * PIECE, PIECE), PIECE)]

    class Gather:
        def __init__(self, source, buf, base, columns):
            self.source, self.buf, self.base, self.columns = source, buf, base, columns
            self.pieces = source.shape[1] // TILE if columns else source.shape[0] // PIECE

        def copy(self, number, src, dst, target):
            return pltpu.make_async_remote_copy(
                src_ref=src,
                dst_ref=dst,
                send_sem=send_sem.at[self.base + number],
                recv_sem=recv_sem.at[self.base + number],
                device_id={"tensor": target},
                device_id_type=MESH,
            )

        def local(self):
            return pltpu.make_async_copy(self.source, slot(self.buf, me), local_sem.at[self.base])

        def to_mate(self, owner):
            return self.copy(0, self.source, slot(self.buf, owner), mate)

        def to_peer(self, owner, piece):
            if self.columns:
                part = self.source.at[:, piece * TILE : (piece + 1) * TILE]
            else:
                part = self.source.at[pl.ds(piece * PIECE, PIECE)]
            return self.copy(1 + piece, part, slot(self.buf, owner, piece, self.columns), peer)

        def forward(self, owner, piece):
            part = slot(self.buf, owner, piece, self.columns)
            return self.copy(1 + self.pieces + piece, part, part, mate)

    g_tok, g_cot = Gather(tok_in, tok, 0, False), Gather(cot_in, cot, 1 + 2 * (rows_own // PIECE), True)
    g_tok.to_mate(me).start()
    for piece in range(g_tok.pieces):
        g_tok.to_peer(me, piece).start()
    g_tok.local().start()
    g_cot.to_mate(me).start()
    g_cot.local().start()

    start_one = lengths[0, 0]
    start_two = start_one + lengths[0, 1]

    def segment(block):
        return (block >= start_one).astype(jnp.int32) + (block >= start_two).astype(jnp.int32)

    def in_sequence(block):
        return block - jnp.where(block >= start_two, start_two, jnp.where(block >= start_one, start_one, 0))

    gain_one, bias_one, gain_two, bias_two = gain_one_in[...], bias_one_in[...], gain_two_in[...], bias_two_in[...]
    scale_row, weight_row = (
        wide([field[h : h + 1, :] for h in range(heads)]) for field in (feature_scale, feature_weight)
    )
    blocks = rows // BLOCK

    def rotation(row0, count):
        cos_in, sin_in = angles[0:BLOCK, :], angles[BLOCK : 2 * BLOCK, :]
        sign_a = angles[2 * BLOCK + 2 * blocks : 2 * BLOCK + 2 * blocks + 1, :]
        sign_b = angles[2 * BLOCK + 2 * blocks + 1 : 2 * BLOCK + 2 * blocks + 2, :]
        cosines, sines = [], []
        for k in range(count):
            place = in_sequence(lax.div(row0, BLOCK) + k)
            cos_at = angles[pl.ds(2 * BLOCK + place, 1), :]
            sin_at = angles[pl.ds(2 * BLOCK + blocks + place, 1), :]
            cosines.append(cos_in * cos_at - sin_in * sin_at)
            sines.append(sin_in * cos_at + cos_in * sin_at)
        cosine, sine = wide(cosines, 0), wide(sines, 0)
        return cosine, sine * sign_a, sine * sign_b

    def rotate(field, turn, back=False):
        cosine, sine_a, sine_b = turn
        parts = []
        for at in range(0, width, 2 * HEAD_DIM):
            part = field[:, at : at + 2 * HEAD_DIM]
            ahead = pltpu.roll(part, 2 * HEAD_DIM - ROT // 2, 1) * sine_a
            behind = pltpu.roll(part, ROT // 2, 1) * sine_b
            parts.append(part * cosine - (ahead + behind) if back else part * cosine + (ahead + behind))
        return wide(parts)

    def unit_rows(value):
        value = value - jnp.mean(value, -1, keepdims=True)
        deviation = lax.rsqrt(jnp.mean(value * value, -1, keepdims=True) + 1e-05)
        return value * deviation, deviation

    def slope_copy(p, back=False):
        held = slopes.at[pl.ds(pl.multiple_of(p * TILE, TILE), TILE)]
        slot_of = temp.at[lax.rem(p, 2)]
        return pltpu.make_async_copy(*((held, slot_of) if back else (slot_of, held)), temp_sem.at[lax.rem(p, 2)])

    def tile_rows(j):
        late = lax.div(j, 4)
        early_at = jnp.where(j < 2, me, mate) * rows_own + lax.rem(j, 2) * TILE
        row_a = pl.multiple_of(jnp.where(late == 0, early_at, peer * rows_own + (j - 4) * PIECE), PIECE)
        row_b = pl.multiple_of(jnp.where(late == 0, early_at + PIECE, cross * rows_own + (j - 4) * PIECE), PIECE)
        return late, row_a, row_b, [pl.ds(row_a, PIECE), pl.ds(row_b, PIECE)]

    def keep_rows(here, write, value):
        for k, at in enumerate(here):
            write(at, value[k * PIECE : (k + 1) * PIECE])

    def attend(j, carry):
        _, row_a, row_b, here = tile_rows(j)
        first = wide([n_one[at, :] for at in here], 0)
        turn = [wide(pair, 0) for pair in zip(*(rotation(at, PIECE // BLOCK) for at in (row_a, row_b)))]

        def keep_field(s, value):
            def write(at, part):
                fqkv[at, s * width : (s + 1) * width] = part

            keep_rows(here, write, value.astype(BF))

        for s in range(2):
            high, low = split(rotate(dot(first, w_qkv[s]), turn))
            table = dct[:, 0:width]
            spectrum = dot(high, table, NT) + dot(low, table, NT) + dot(high, dct[:, width:], NT)

            def keep_spectrum(at, part):
                spec[s, at, :] = part

            keep_rows(here, keep_spectrum, spectrum)
            keep_field(s, weight_row * jnp.exp(scale_row * spectrum))
        keep_field(2, dot(first, w_qkv[2]))
        return carry

    def project(j, carry):
        pl.when(j >= 4)(lambda: attend(j - 4, None))

        @pl.when(j == 0)
        def _():
            g_tok.local().wait()

            g_cot.local().wait()

        @pl.when(j == 2)
        def _():
            g_tok.to_mate(mate).wait_recv()
            g_cot.to_mate(mate).wait_recv()

        for piece in range(g_tok.pieces):

            @pl.when(j == 4 + piece)
            def _():
                g_tok.to_peer(peer, piece).wait_recv()
                g_tok.forward(peer, piece).start()
                g_cot.to_peer(me, piece).start()
                g_tok.forward(cross, piece).wait_recv()

        late, row_a, _, here = tile_rows(j)
        for at in here:
            pltpu.make_async_copy(tok.at[at], tok_kept.at[at], tok_sem.at[0]).start()
        unit, _ = unit_rows(wide([tok[at, :] for at in here], 0).astype(F32))
        first = (unit * gain_one + bias_one).astype(BF)
        second = (unit * gain_two + bias_two).astype(BF)
        for k, at in enumerate(here):
            n_one[at, :] = first[k * PIECE : (k + 1) * PIECE]
            n_two[at, :] = second[k * PIECE : (k + 1) * PIECE]
        parity = lax.rem(j, 2)
        pl.when(j >= 6)(lambda: slope_copy(j - 6).wait())
        for at in range(0, w_up.shape[1], TILE):
            up = dot(second, w_up[:, at : at + TILE])
            below = 0.5 * (1.0 + lax.erf(up * math.sqrt(0.5)))

            def keep_hidden(rows_at, part):
                hid[rows_at, at : at + TILE] = part

            keep_rows(here, keep_hidden, (up * below).astype(BF))
            temp[parity, :, at : at + TILE] = below + up * (
                jnp.exp(-0.5 * up * up) * (1.0 / math.sqrt(2.0 * math.pi))
            )

        @pl.when(late == 0)
        def _():
            turned = wide([cot[at, :] for at in here], 0)
            first_at = pl.multiple_of(row_a, TILE)
            for at in range(0, hid.shape[1], TILE):
                d_hidden = dot(turned, w_down[at : at + TILE, :], NT)
                d_up[pl.ds(first_at, TILE), at : at + TILE] = (d_hidden * temp[parity, :, at : at + TILE]).astype(BF)

        pl.when(late == 1)(lambda: slope_copy(j - 4).start())
        return carry

    for copy in weight_copies:
        copy.wait()
    with jax.named_scope("project"):
        lax.fori_loop(0, rows // TILE, project, 0)
    for p in (2, 3):
        slope_copy(p).wait()
    for p in range(2):
        slope_copy(p, True).start()

    grid_t = lax.broadcasted_iota(jnp.int32, (CHUNK, CHUNK), 0)
    grid_s = lax.broadcasted_iota(jnp.int32, (CHUNK, CHUNK), 1)
    together = (grid_t < BLOCK) == (grid_s < BLOCK)
    causal = wide([jnp.where((grid_t >= grid_s) & together, 1.0, 0.0).astype(F32)] * heads)
    causal_back = wide([jnp.where((grid_t <= grid_s) & together, 1.0, 0.0).astype(F32)] * heads)
    head_rows = jnp.where(
        lax.broadcasted_iota(jnp.int32, (8, width), 0) == lax.div(lax.broadcasted_iota(jnp.int32, (8, width), 1), HEAD_DIM),
        1.0,
        0.0,
    ).astype(BF)
    both_chunks = range(2)
    both_blocks = range(CHUNK // BLOCK)

    def joined(block):
        return jnp.where(segment(block) == segment(block - 1), jnp.float32(1.0), jnp.float32(0.0))

    def per_head(value):
        return wide([value * masks[h * CHUNK : (h + 1) * CHUNK, :] for h in range(heads)], 0)

    def halves(value):
        return [value[k * BLOCK : (k + 1) * BLOCK] for k in both_blocks]

    def chunk_rows(pair):
        return [pl.ds(pl.multiple_of((2 * pair + c) * CHUNK, CHUNK), CHUNK) for c in both_chunks]

    state[...] = jnp.zeros_like(state)
    krow[...] = jnp.zeros_like(krow)

    def mix(pair, carry):
        diag = diagonal[...].astype(F32)
        here = chunk_rows(pair)
        query, key, value = ([fqkv[at, s * width : (s + 1) * width] for at in here] for s in range(3))
        scores = [split(dot(query[c], per_head(key[c]), NT) * causal) for c in both_chunks]
        turned = [key[c].T for c in both_chunks]
        over = [dot(scores[c][0], per_head(value[c])) for c in both_chunks]
        under = [dot(scores[c][0], masks[...]) + dot(scores[c][1], masks[...]) for c in both_chunks]
        made = [
            dot(turned[c][:, k * BLOCK : (k + 1) * BLOCK], halves(value[c])[k]) * diag
            for c in both_chunks
            for k in both_blocks
        ]
        row_made = [jnp.sum(halves(key[c])[k].astype(F32), 0, keepdims=True) for c in both_chunks for k in both_blocks]
        now, row = state[...], krow[0:1, :]
        carried, rows_in = [], []
        for k in range(4):
            carried.append(now.astype(BF))
            rows_in.append(row)
            states[4 * pair + k] = sum(now[h * HEAD_DIM : (h + 1) * HEAD_DIM] for h in range(heads)).astype(BF)
            ksums[pl.ds(4 * pair + k, 1), :] = row
            keep = joined(4 * pair + k + 1)
            now = (now + made[k]) * keep
            row = (row + row_made[k]) * keep
        state[...] = now
        krow[0:1, :] = row
        for c in both_chunks:
            parts = halves(query[c])
            more = wide([dot(parts[k], carried[2 * c + k]) for k in both_blocks], 0)
            high, low = split(wide([parts[k].astype(F32) * rows_in[2 * c + k] for k in both_blocks], 0))
            inverse = 1.0 / (under[c] + dot(high, diagonal[...]) + dot(low, diagonal[...]))
            attended = (over[c] + more) * inverse
            att[here[c], :] = attended
            rden[here[c], :] = wide([inverse[:, h * HEAD_DIM : h * HEAD_DIM + HEAD_DIM // 2] for h in range(heads)])
            mixed[here[c], :] = attended.astype(BF)

        return carry

    def add_parts(base, first, count, sources):
        cut = min(SUB, count)
        for at in range(0, count, cut):
            total = base[pl.ds(first + at, cut), :].astype(F32)
            for source, place in sources:
                total = total + source[pl.ds(place + at, cut), :].astype(F32)
            base[pl.ds(first + at, cut), :] = total.astype(BF)

    def bring(base, first, box, place, count):
        base[pl.ds(first, count), :] = box[pl.ds(place, count), :]

    half, quarter = UNIT // 2, UNIT // 4

    def rows_of(index, size):
        return pl.multiple_of(index * size, size)

    def unit_of(n):
        return grads.at[pl.ds(pl.multiple_of(n * UNIT, UNIT), UNIT)]

    def hop(box, kind, source, target, device):
        return pltpu.make_async_remote_copy(
            src_ref=source,
            dst_ref=target,
            send_sem=ar_send.at[box, kind],
            recv_sem=ar_recv.at[box, kind],
            device_id={"dp": device},
            device_id_type=MESH,
        )

    plain = units - 3 * width // UNIT
    per_tile = TILE // UNIT

    class Copies:
        def __init__(self, n):
            self.n = n

        def whole(self):
            first = pl.multiple_of(self.n * UNIT, UNIT)
            return pltpu.make_async_copy(unit_of(self.n), grads_out.at[pl.ds(first, UNIT)], grad_sem.at[0])

        def piece(self, q):
            u = self.n - plain
            at = 4 * lax.div(u, per_tile) + q
            row = pl.multiple_of(lax.div(at, 3) * TILE + lax.rem(u, per_tile) * UNIT, UNIT)
            return pltpu.make_async_copy(
                unit_of(self.n).at[:, q * width : (q + 1) * width],
                qkv_out.at[lax.rem(at, 3), pl.ds(row, UNIT)],
                grad_sem.at[1],
            )

        def start(self):
            pl.when(self.n < plain)(lambda: self.whole().start())

            @pl.when(self.n >= plain)
            def _():
                for q in range(4):
                    self.piece(q).start()

    def kind_of(n):
        return lax.rem(n, 2)

    def box_of(n):
        return lax.rem(lax.div(n, 2), BOXES_X), lax.rem(lax.div(n, 2), BOXES_Z)

    def begin(n):
        place, place_b = box_of(n)
        code = 4 * kind_of(n) + middle

        @pl.when(code < 4)
        def _():
            theirs = unit_of(n).at[pl.ds(rows_of(1 - along_x, half), half)]
            hop(place, 0, theirs, recv_a.at[place, pl.ds(0, half)], across).start()

        @pl.when(code == 4)
        def _():
            hop(BOXES_X + place_b, 0, unit_of(n), recv_b.at[place_b, pl.ds(0, UNIT)], inward).start()

    def advance(n, stage):
        kind = jnp.where(n < 0, 2, jnp.where(n >= units, 2, kind_of(n)))
        n = jnp.where(kind == 2, 0, n)
        code = 4 * kind + middle
        place, place_b = box_of(n)

        def case(number):
            return pl.when(code == number)

        base, box = unit_of(n), recv_a.at[place]
        mine_at, theirs_at = rows_of(along_x, half), rows_of(1 - along_x, half)
        own_at = pl.multiple_of(along_x * half + side * quarter, quarter)
        other_at = pl.multiple_of(along_x * half + (1 - side) * quarter, quarter)
        own_in, other_in = rows_of(side, quarter), rows_of(1 - side, quarter)

        def rows(first, size):
            return base.at[pl.ds(first, size)]

        def x_one():
            return hop(place, 0, rows(theirs_at, half), box.at[pl.ds(0, half)], across)

        def z_one():
            return hop(place, 1, rows(mine_at, half), box.at[pl.ds(half, half)], inward)

        def z_two():
            return hop(place, 2, rows(other_at, quarter), box.at[pl.ds(2 * half, quarter)], inward)

        def z_swap():
            return hop(place, 3, rows(own_at, quarter), box.at[pl.ds(swap_at, quarter)], inward)

        def out(kind, first, place_in):
            return hop(place, kind, rows(first, quarter), box.at[pl.ds(half + place_in, quarter)], outward)

        def x_two():
            return hop(place, 6, rows(mine_at, half), box.at[pl.ds(last_at, half)], across)

        swap_at, last_at = 2 * half + quarter, 3 * half

        if stage == 1:

            @case(0)
            def _():
                x_one().wait_recv()
                add_parts(base, mine_at, half, [(box, 0)])
                z_one().start()

        if stage == 2:

            @case(2)
            def _():
                x_one().wait_recv()
                z_one().wait_recv()
                add_parts(base, other_at, quarter, [(box, other_in), (box, half + other_in)])
                z_two().start()

        if stage == 3:

            @case(2)
            def _():
                z_two().wait_recv()
                add_parts(base, own_at, quarter, [(box, own_in), (box, half + own_in), (box, 2 * half)])
                z_swap().start()
                out(4, own_at, own_in).start()

        if stage == 4:

            @case(2)
            def _():
                z_swap().wait_recv()
                z_two().wait_send()
                bring(base, other_at, box, swap_at, quarter)
                out(5, other_at, other_in).start()
                x_two().start()

        if stage == 5:

            @case(0)
            def _():
                z_one().wait_send()
                out(4, own_at, own_in).wait_recv()
                out(5, other_at, other_in).wait_recv()
                bring(base, mine_at, box, half, half)
                x_two().start()

        if stage == 6:

            @case(2)
            def _():
                z_swap().wait_send()
                out(4, own_at, own_in).wait_send()
                out(5, other_at, other_in).wait_send()

            @pl.when(kind == 0)
            def _():
                x_one().wait_send()
                x_two().wait()
                bring(base, theirs_at, box, last_at, half)

        box_b = recv_b.at[place_b]
        mine_z, theirs_z = rows_of(side, half), rows_of(1 - side, half)
        own_x = pl.multiple_of(side * half + along_x * quarter, quarter)
        other_x = pl.multiple_of(side * half + (1 - along_x) * quarter, quarter)
        own_part_at, other_part_at = rows_of(along_x, quarter), rows_of(1 - along_x, quarter)

        def z_in():
            return hop(BOXES_X + place_b, 0, base, box_b.at[pl.ds(0, UNIT)], inward)

        def z_mid():
            return hop(BOXES_X + place_b, 1, rows(theirs_z, half), box_b.at[pl.ds(UNIT, half)], inward)

        def x_mid():
            return hop(BOXES_X + place_b, 2, rows(other_x, quarter), box_b.at[pl.ds(UNIT + half, quarter)], across)

        def x_swap():
            return hop(BOXES_X + place_b, 3, rows(own_x, quarter), box_b.at[pl.ds(swap_at, quarter)], across)

        def z_share():
            return hop(BOXES_X + place_b, 4, rows(mine_z, half), box_b.at[pl.ds(last_at, half)], inward)

        def z_out(kind, first):
            return hop(BOXES_X + place_b, kind, rows(first, half), box_b.at[pl.ds(first, half)], outward)

        swap_at, last_at = UNIT + half + quarter, 2 * UNIT

        if stage == 1:

            @case(6)
            def _():
                z_in().wait_recv()
                add_parts(base, theirs_z, half, [(box_b, theirs_z)])
                z_mid().start()

        if stage == 2:

            @case(6)
            def _():
                z_mid().wait_recv()
                add_parts(base, other_x, quarter, [(box_b, other_x), (box_b, UNIT + other_part_at)])
                x_mid().start()

        if stage == 3:

            @case(6)
            def _():
                x_mid().wait_recv()
                add_parts(
                    base, own_x, quarter, [(box_b, own_x), (box_b, UNIT + own_part_at), (box_b, UNIT + half)]
                )
                x_swap().start()

        if stage == 4:

            @case(6)
            def _():
                x_swap().wait_recv()
                x_mid().wait_send()
                bring(base, other_x, box_b, swap_at, quarter)
                z_share().start()
                z_out(5, mine_z).start()

        if stage == 5:

            @case(6)
            def _():
                z_share().wait_recv()
                z_mid().wait_send()
                bring(base, theirs_z, box_b, last_at, half)
                z_out(6, theirs_z).start()

        if stage == 6:

            @case(6)
            def _():
                x_swap().wait_send()
                z_share().wait_send()
                z_out(5, mine_z).wait_send()
                z_out(6, theirs_z).wait_send()

            @case(4)
            def _():
                z_in().wait_send()
                z_out(5, mine_z).wait_recv()
                z_out(6, theirs_z).wait_recv()
                bring(base, 0, box_b, 0, UNIT)

            pl.when(kind < 2)(lambda: Copies(n).start())

    def at_ready(n):
        return jnp.where(n < LEAD, 1, jnp.where(n < plain, 0, jnp.where(n < plain + LEAD, 1, 0)))

    def ready(first, count):
        for n in (first + k for k in range(count)):
            if reduce_dp:
                pl.when(at_ready(n) == 1)(functools.partial(begin, n))
            else:
                Copies(n).start()

    def tick(t):
        if reduce_dp:
            with jax.named_scope("dp_tick"):
                move(t)

    def move(t):
        for stage in (6, 5, 4, 3, 2, 1):
            advance(t - LAG * (stage - 1), stage)
        later = t + LEAD

        @pl.when(jnp.where(later >= units, 1, at_ready(later)) == 0)
        def _():
            begin(later)

    def tick_at(j, every, first):
        @pl.when(lax.rem(j, every) == every - 1)
        def _():
            tick(first + lax.div(j, every))

    ticks = units + 5 * LAG

    def run_ticks(first, last):
        lax.fori_loop(first, last, pause, 0)

    def pause(t, carry):
        tick(t)
        return carry

    def landed(which, number):
        if which:
            return n_one.at[pl.ds(pl.multiple_of(number * TILE, TILE), TILE)]
        return rs_in.at[number]

    def late_landed(number):
        return n_one.at[pl.ds(pl.multiple_of((6 + number) * TILE, TILE), TILE)]

    def crossed(which, number):
        at = pl.multiple_of((4 + number) * TILE, TILE)
        return n_one.at[pl.ds(at, TILE)] if which else y_in.at[number]

    def to_mate(which, number, late=False):
        return pltpu.make_async_remote_copy(
            src_ref=rs_out.at[lax.rem(number, 2)],
            dst_ref=late_landed(number - 2) if late else landed(which, number),
            send_sem=rs_send.at[which, number],
            recv_sem=rs_recv.at[which, number],
            device_id={"tensor": mate},
            device_id_type=MESH,
        )

    def to_peer(which, number):
        return pltpu.make_async_remote_copy(
            src_ref=landed(which, number),
            dst_ref=crossed(which, number),
            send_sem=rs_send.at[which, 4 + number],
            recv_sem=rs_recv.at[which, 4 + number],
            device_id={"tensor": peer},
            device_id_type=MESH,
        )

    def scatter(j, which, compute):
        owner = jnp.where(j < 2, cross, jnp.where(j < 4, peer, mate))
        number = lax.rem(j, 2)
        row0 = pl.multiple_of(owner * rows_own + number * TILE, TILE)

        @pl.when(lax.div(j, 2) != 1)
        def _():
            at = jnp.where(j < 2, j, j - 2)
            pl.when(j >= 4)(lambda: to_mate(which, number).wait_send())

            def put(columns, part):
                rs_out[number, :, columns] = part.astype(BF)

            compute(row0, put)
            if which:
                to_mate(which, at).start()
            else:
                pl.when(j < 2)(lambda: to_mate(0, at).start())
                pl.when(j >= 4)(lambda: to_mate(0, at, True).start())

        @pl.when(lax.div(j, 2) == 1)
        def _():
            to_mate(which, number).wait_recv()

            here = landed(which, number)

            def put(columns, part):
                here[:, columns] = (here[:, columns].astype(F32) + part).astype(BF)

            compute(row0, put)
            to_peer(which, number).start()

    def gathered(which, number):
        to_mate(which, 2 + number, not which).wait_recv()
        to_peer(which, number).wait_recv()

    def stored(which, number):
        result = input_grad if which else mixed_out
        here = rs_out.at[number] if which else late_landed(number)
        target = result.at[pl.ds(pl.multiple_of(number * TILE, TILE), TILE)]
        return pltpu.make_async_copy(here, target, result_sem.at[which, number])

    pltpu.make_async_copy(tok.at[pl.ds(0, rows)], tok_kept, tok_sem.at[0]).wait()
    for piece in range(g_tok.pieces):
        g_tok.forward(peer, piece).wait_send()

    def keep_unit(n, value):
        grads[pl.ds(pl.multiple_of(n * UNIT, UNIT), value.shape[0]), :] = value
        ready(n, value.shape[0] // UNIT)

    first_out = hid.shape[1] // UNIT
    first_up = first_out + width // UNIT

    def arrive(piece):
        g_cot.to_peer(peer, piece).wait_recv()
        g_cot.forward(peer, piece).start()

    def down(piece):
        g_cot.forward(cross, piece).wait_recv()
        tile = dot(cot[:, piece * TILE : (piece + 1) * TILE], hid[...], TN)
        keep_unit(per_tile * piece, tile.astype(BF))

    def mix_some(first, last):
        with jax.named_scope("mixer"):
            lax.fori_loop(first, last, mix, 0)

    pairs = chunks // 2
    tiles = rows // TILE
    with jax.named_scope("grad_down"):
        lax.fori_loop(tiles - 4, tiles - 2, attend, 0)
        arrive(0)
        down(0)
        lax.fori_loop(tiles - 2, tiles, attend, 0)
        arrive(1)
        run_ticks(0, 2)
        down(1)
    mix_some(0, pairs // 4)
    run_ticks(2, 4)
    arrive(2)
    mix_some(pairs // 4, pairs // 2)
    run_ticks(4, 5)
    with jax.named_scope("grad_down"):
        down(2)
    run_ticks(5, 7)
    mix_some(pairs // 2, 3 * pairs // 4)
    run_ticks(7, 8)
    arrive(3)
    mix_some(3 * pairs // 4, pairs)
    run_ticks(8, 10)
    with jax.named_scope("grad_down"):
        down(3)
    run_ticks(10, 12)
    keep_unit(first_out, dot(mixed[...], cot[...], TN).astype(BF))
    run_ticks(12, 14)

    column_tiles = [slice(at, at + TILE) for at in range(0, cot.shape[1], TILE)]

    def branch(row0, put):
        here = pl.ds(row0, TILE)
        left, right = mixed[here, :], hid[here, :]
        for columns in column_tiles:
            put(columns, dot(left, w_out[:, columns]) + dot(right, w_down[:, columns]))

    def keep_temp(number):
        def put(columns, part):
            temp[number, :, columns] = part

        return put

    def produce(j, carry):
        scatter(j, 0, branch)
        run_ticks(14 + j, 15 + j)
        return carry

    with jax.named_scope("outputs"):
        lax.fori_loop(0, 4, produce, 0)

    def descend(p, carry):
        here = [pl.ds(pl.multiple_of(owner * rows_own + p * PIECE, PIECE), PIECE) for owner in (peer, cross)]
        parity = lax.rem(p, 2)
        slope_copy(p, True).wait()
        turned = wide([cot[at, :] for at in here], 0)
        for at in range(0, hid.shape[1], TILE):
            d_hidden = dot(turned, w_down[at : at + TILE, :], NT)
            value = (d_hidden * temp[parity, :, at : at + TILE]).astype(BF)
            for k, rows_at in enumerate(here):
                d_up[rows_at, at : at + TILE] = value[k * PIECE : (k + 1) * PIECE]
        pl.when(p < 2)(lambda: slope_copy(p + 2, True).start())
        return carry

    with jax.named_scope("grad_gelu"):
        lax.fori_loop(0, 4, descend, 0)
    def upward(j, carry):
        at = pl.ds(pl.multiple_of(j * TILE, TILE), TILE)
        keep_unit(first_up + per_tile * j, dot(n_two[:, at], d_up[...], TN).astype(BF))
        run_ticks(18 + j, 19 + j)
        return carry

    with jax.named_scope("grad_up"):
        lax.fori_loop(0, n_two.shape[1] // TILE, upward, 0)

    state[...] = jnp.zeros_like(state)
    krow[...] = jnp.zeros_like(krow)
    feat_sums[...] = jnp.zeros_like(feat_sums)

    def unmix(step, carry):
        pair = chunks // 2 - 1 - step
        diag = diagonal[...].astype(F32)
        row_pair = pl.multiple_of(pair * 2 * CHUNK, 2 * CHUNK)
        d_mixed = dot(cot[pl.ds(row_pair, 2 * CHUNK), :], w_out[...], NT)
        here = chunk_rows(pair)
        query, key, value = ([fqkv[at, s * width : (s + 1) * width] for at in here] for s in range(3))
        d_over, under_parts = [], []
        for c in both_chunks:
            packed = rden[here[c], :]
            inverse = wide(
                [packed[:, h // 2 * HEAD_DIM // 2 : (h // 2 + 1) * HEAD_DIM // 2] for h in range(2 * heads)]
            )
            d_over.append(d_mixed[c * CHUNK : (c + 1) * CHUNK] * inverse)
            under_parts.append(split(d_over[c] * att[here[c], :]))
        d_under = [-dot(part[0], diagonal[...]) - dot(part[1], diagonal[...]) for part in under_parts]
        under_row = [-dot(head_rows, under_parts[c][0], NT) - dot(head_rows, under_parts[c][1], NT) for c in both_chunks]
        over_split = [split(d_over[c]) for c in both_chunks]
        over_both = [wide(over_split[c]) for c in both_chunks]
        over_heads = [wide([per_head(part) for part in over_split[c]]) for c in both_chunks]
        query_heads, key_heads, value_heads = ([per_head(field[c]) for c in both_chunks] for field in (query, key, value))
        scores_back = [(dot(key[c], query_heads[c], NT) * causal_back).astype(BF) for c in both_chunks]
        d_scores = [dot(over_both[c], wide([value_heads[c]] * 2), NT) for c in both_chunks]
        d_back = [dot(wide([value[c]] * 2), over_heads[c], NT) for c in both_chunks]
        turned = [query[c].T for c in both_chunks]
        made = []
        for c in both_chunks:
            for k in both_blocks:
                left = turned[c][:, k * BLOCK : (k + 1) * BLOCK]
                made.append(dot(wide([left, left]), wide([halves(part)[k] for part in over_split[c]], 0)) * diag)
        d_scores = [
            wide(
                split(
                    (
                        d_scores[c]
                        + wide(
                            [
                                jnp.broadcast_to(d_under[c][:, h * HEAD_DIM : h * HEAD_DIM + 1], (CHUNK, CHUNK))
                                for h in range(heads)
                            ]
                        )
                    )
                    * causal
                )
            )
            for c in both_chunks
        ]
        d_back = [
            wide(split((d_back[c] + wide([under_row[c][h : h + 1, :] for h in range(heads)])) * causal_back))
            for c in both_chunks
        ]
        d_query = [dot(d_scores[c], wide([key_heads[c]] * 2, 0)) for c in both_chunks]
        d_key = [dot(d_back[c], wide([query_heads[c]] * 2, 0)) for c in both_chunks]
        d_value = [dot(scores_back[c], over_heads[c]) for c in both_chunks]
        later, later_row = state[...], krow[0:1, :]
        more = {}
        for at in reversed(range(4)):
            c, k = divmod(at, 2)
            block = 4 * pair + at
            query_k, key_k, value_k, both_k, under_k = (
                halves(field[c])[k] for field in (query, key, value, over_both, d_under)
            )
            carried = wide([states[block]] * heads, 0) * diagonal[...]
            keep = joined(block + 1)
            later, later_row = later * keep, later_row * keep
            high, low = split(later)
            more[at] = (
                dot(both_k, wide([carried, carried]), NT) + under_k * ksums[pl.ds(block, 1), :],
                dot(wide([value_k, value_k]), wide([high, low]), NT) + later_row,
                dot(wide([key_k, key_k]), wide([high, low], 0)),
            )
            later = later + made[at]
            later_row = later_row + jnp.sum(query_k.astype(F32) * under_k, 0, keepdims=True)
        state[...] = later
        krow[0:1, :] = later_row
        turn = rotation(row_pair, 2 * CHUNK // BLOCK)
        here = pl.ds(row_pair, 2 * CHUNK)
        for s, found in enumerate((d_query, d_key)):
            grad = wide(found, 0) + wide([more[at][s] for at in range(4)], 0)
            spectrum = spec[s, here, :]
            grad = grad * (weight_row * jnp.exp(scale_row * spectrum))
            feat_sums[0:1, :] += jnp.sum(grad * spectrum, 0, keepdims=True)
            feat_sums[1:2, :] += jnp.sum(grad, 0, keepdims=True)
            high, low = split(grad * scale_row)
            back = dot(high, dct[:, 0:width]) + dot(low, dct[:, 0:width]) + dot(high, dct[:, width:])
            fqkv[here, s * width : (s + 1) * width] = rotate(back, turn, True).astype(BF)
        d_value = wide([d_value[c][:, :width] + d_value[c][:, width:] for c in both_chunks], 0)
        fqkv[here, 2 * width : 3 * width] = (d_value + wide([more[at][2] for at in range(4)], 0)).astype(BF)
        run_ticks(22 + lax.div(14 * step, chunks // 2), 22 + lax.div(14 * (step + 1), chunks // 2))

        return carry

    with jax.named_scope("mixer_back"):
        lax.fori_loop(0, chunks // 2, unmix, 0)

    def projected(j, carry):
        tile = dot(n_one[:, pl.ds(pl.multiple_of(j * TILE, TILE), TILE)], fqkv[...], TN).astype(BF)
        for s in range(3):
            at = 3 * j + s
            first = pl.multiple_of(plain * UNIT + lax.div(at, 4) * TILE, TILE)
            columns = pl.ds(pl.multiple_of(lax.rem(at, 4) * width, width), width)
            grads[pl.ds(first, TILE), columns] = tile[:, s * width : (s + 1) * width]

        @pl.when(j >= 1)
        def _():
            ready(plain + (j - 1) * per_tile, per_tile)

        return carry

    with jax.named_scope("grad_qkv"):
        lax.fori_loop(0, n_one.shape[1] // TILE, projected, 0)
    pl.semaphore_signal(free_mate, inc=1, device_id={"tensor": mate}, device_id_type=MESH)
    pl.semaphore_signal(free_peer, inc=1, device_id={"tensor": peer}, device_id_type=MESH)
    run_ticks(36, 38)

    sums[...] = jnp.zeros_like(sums)

    def row_of(j):
        owner = jnp.where(j < 2, cross, jnp.where(j < 4, peer, jnp.where(j < 6, mate, me)))
        return pl.multiple_of(owner * rows_own + lax.rem(j, 2) * TILE, TILE)

    def tok_copy(j):
        which = lax.rem(j, 2)
        return pltpu.make_async_copy(
            tok_kept.at[pl.ds(row_of(j), TILE)], n_two.at[pl.ds(pl.multiple_of(which * TILE, TILE), TILE)], tok_sem.at[which]
        )

    def row_grads(j):
        def compute(row0, put):
            here = pl.ds(row0, TILE)
            unit, _ = unit_rows(n_two[pl.ds(pl.multiple_of(lax.rem(j, 2) * TILE, TILE), TILE), :].astype(F32))
            fields = [fqkv[here, s * width : (s + 1) * width] for s in range(3)]
            right = d_up[here, :]
            for columns in column_tiles:
                one = sum(dot(fields[s], w_qkv[s, columns, :], NT) for s in range(3))
                two = dot(right, w_up[columns, :], NT)
                part = unit[:, columns]
                for number, term in enumerate((one * part, one, two * part, two)):
                    sums[number, :, columns] += jnp.sum(term.reshape(TILE // 8, 8, TILE), 0)
                put(columns, one * gain_one[:, columns] + two * gain_two[:, columns])

        return compute

    tok_copy(0).start()

    def own_tok(number):
        here = n_two.at[pl.ds((2 + number) * TILE, TILE)]
        return pltpu.make_async_copy(tok_in.at[pl.ds(number * TILE, TILE)], here, local_sem.at[number])

    for number in range(2):
        own_tok(number).start()

    def finish(number):
        gathered(0, number)
        tokens, result = n_two.at[pl.ds((2 + number) * TILE, TILE)], late_landed(number)

        def put(columns, part):
            total = part + result[:, columns].astype(F32) + y_in[number, :, columns].astype(F32)
            result[:, columns] = (total + tokens[:, columns].astype(F32)).astype(BF)

        branch(pl.multiple_of(me * rows_own + number * TILE, TILE), put)
        stored(0, number).start()

    pl.semaphore_wait(free_mate, 1)
    pl.semaphore_wait(free_peer, 1)

    def produce_late(j, carry):
        scatter(j, 0, branch)
        return carry

    with jax.named_scope("outputs"):
        lax.fori_loop(4, 6, produce_late, 0)
    for number in range(2):
        to_mate(0, 2 + number, True).wait_send()

    def inputs(j, carry):
        tok_copy(j).wait()
        pl.when(j < 7)(lambda: tok_copy(j + 1).start())

        @pl.when(j < 6)
        def _():
            scatter(j, 1, row_grads(j))

        @pl.when(j >= 6)
        def _():
            row_grads(j)(row_of(j), keep_temp(lax.rem(j, 2)))

        run_ticks(38 + 2 * j, 40 + 2 * j)
        return carry

    with jax.named_scope("row_grads"):
        lax.fori_loop(0, 8, inputs, 0)
    def conclude(number):
        gathered(1, number)
        tokens = n_two.at[pl.ds((2 + number) * TILE, TILE)]
        from_mate, from_peer = landed(1, 2 + number), crossed(1, number)

        def step(i, inner):
            at = pl.ds(pl.multiple_of(i * PIECE, PIECE), PIECE)
            group_at = pl.multiple_of(me * rows_own + number * TILE + i * PIECE, PIECE)
            unit, deviation = unit_rows(tokens[at, :].astype(F32))
            total = temp[number, at, :] + from_mate[at, :].astype(F32) + from_peer[at, :].astype(F32)
            along = jnp.mean(total * unit, -1, keepdims=True)
            total = total - jnp.mean(total, -1, keepdims=True) - unit * along
            total = cot[pl.ds(group_at, PIECE), :].astype(F32) + deviation * total
            rs_out[number, at, :] = total.astype(BF)
            return inner

        lax.fori_loop(0, TILE // PIECE, step, 0)
        stored(1, number).start()

    small[...] = jnp.zeros_like(small)
    for number in range(4):
        small[number : number + 1, :] = jnp.sum(sums[number], 0, keepdims=True)
    small[4:5, 0:width] = feat_sums[0:1, :]
    small[5:6, 0:width] = feat_sums[1:2, :] / weight_row

    def small_hops(axis, own, count, boxes, first):
        hops = []
        for step in range(1, count):
            hops.append(
                pltpu.make_async_remote_copy(
                    src_ref=small,
                    dst_ref=boxes.at[own],
                    send_sem=small_send.at[first + step - 1],
                    recv_sem=small_recv.at[first + step - 1],
                    device_id={axis: lax.rem(own + step, count)},
                    device_id_type=MESH,
                )
            )
        return hops

    over_tensor = small_hops("tensor", me, 4, small_in, 0)
    over_dp = small_hops("dp", group, members, small_wide, 3)

    def small_step(k):
        if k == 0:
            for copy in over_tensor:
                copy.start()
            small_in[me] = small[...]
        if k == 1:
            for copy in over_tensor:
                copy.wait()
            total = small_in[0]
            for member in range(1, 4):
                total = total + small_in[member]
            small[0:4, :] = total[0:4, :]
        if k == 1 and reduce_dp:
            for copy in over_dp:
                copy.start()
            small_wide[group] = small[...]
        if k == 2 and reduce_dp:
            for copy in over_dp:
                copy.wait()
            total = small_wide[0]
            for member in range(1, members):
                total = total + small_wide[member]
            small[...] = total

    for number in range(2):
        to_mate(1, 2 + number).wait_send()
        own_tok(number).wait()
    small_step(0)
    run_ticks(54, 56)
    finish(0)
    small_step(1)
    run_ticks(56, 58)
    finish(1)
    conclude(0)
    run_ticks(58, 60)
    conclude(1)
    small_step(2)
    if reduce_dp:
        run_ticks(60, ticks)
    for h in range(heads):
        at = slice(h * HEAD_DIM, (h + 1) * HEAD_DIM)
        feat_out[0, h : h + 1, :] = small[4:5, at]
        feat_out[1, h : h + 1, :] = small[5:6, at]

    pltpu.make_async_copy(grads.at[pl.ds(0, plain * UNIT)], grads_out, grad_sem.at[0]).wait()
    pltpu.make_async_copy(w_qkv, qkv_out, grad_sem.at[1]).wait()
    for number in range(2):
        to_peer(0, number).wait_send()
        to_peer(1, number).wait_send()
        for which in range(2):
            stored(which, number).wait()

    for gather in (g_tok, g_cot):
        gather.to_mate(me).wait_send()
        for piece in range(gather.pieces):
            gather.to_peer(me, piece).wait_send()
    for piece in range(g_cot.pieces):
        g_cot.forward(peer, piece).wait_send()


def widen(down_in, out_in, up_in, qkv_in, small_in, feats_in, mixed_in, input_in, *outs):
    down, out, up, qkv, *norms, scale, weight, mixed, input_grad = outs
    down[...] = down_in[...].astype(F32).T
    out[...] = out_in[...].astype(F32)
    up[...] = up_in[...].astype(F32)
    qkv[...] = qkv_in[...].astype(F32)
    for number, norm in enumerate(norms):
        norm[...] = small_in[number : number + 1, :]
    scale[...] = feats_in[0]
    weight[...] = feats_in[1]
    mixed[...] = mixed_in[...]
    input_grad[...] = input_in[...]


def shards(
    reduce_dp,
    tokens,
    ln1_gain,
    ln1_bias,
    ln2_gain,
    ln2_bias,
    w_qkv,
    w_out,
    w_up,
    w_down,
    feature_scale,
    feature_weight,
    lengths,
    cotangent,
):
    rows_own, model = tokens.shape
    rows = 4 * rows_own
    heads = feature_scale.shape[0]
    width = heads * HEAD_DIM
    hidden = w_up.shape[1]
    consts = tables(rows // BLOCK, heads)
    norms = [value.reshape(1, model) for value in (ln1_gain, ln1_bias, ln2_gain, ln2_bias)]
    anywhere = pl.BlockSpec(memory_space=pl.ANY)
    vmem = pl.BlockSpec(memory_space=pltpu.VMEM)
    smem = pl.BlockSpec(memory_space=pltpu.SMEM)
    shape = jax.ShapeDtypeStruct
    plain = 2 * hidden + width
    units = (plain + 3 * width) // UNIT
    mixed_out, input_grad, grads, g_qkv, _, _, small, feats = pl.pallas_call(
        functools.partial(kernel, reduce_dp),
        out_shape=(
            shape((rows_own, model), BF),
            shape((rows_own, model), BF),
            shape((plain, model), BF),
            shape((3, model, width), BF),
            shape((rows // 2, hidden), F32),
            shape((rows, model), BF),
            shape((8, model), F32),
            shape((2, heads, HEAD_DIM), F32),
        ),
        in_specs=[smem, anywhere, anywhere] + [vmem] * 4 + [anywhere] * 4 + [vmem] * 6,
        out_specs=(anywhere,) * 6 + (vmem, vmem),
        scratch_shapes=[
            pltpu.VMEM((rows, model), BF),
            pltpu.VMEM((rows, model), BF),
            pltpu.VMEM((rows, model), BF),
            pltpu.VMEM((rows, hidden), BF),
            pltpu.VMEM((rows, hidden), BF),
            pltpu.VMEM((rows, 3 * width), BF),
            pltpu.VMEM((2, rows, width), F32),
            pltpu.VMEM((rows, width), BF),
            pltpu.VMEM((rows, width), F32),
            pltpu.VMEM((rows, width // 2), F32),
            pltpu.VMEM((rows // BLOCK, HEAD_DIM, width), BF),
            pltpu.VMEM((rows // BLOCK, width), F32),
            pltpu.VMEM((width, width), F32),
            pltpu.VMEM((8, width), F32),
            pltpu.VMEM((units * UNIT, model), BF),
            pltpu.VMEM((BOXES_X, 2 * UNIT, model), BF),
            pltpu.VMEM((BOXES_Z, 5 * UNIT // 2, model), BF),
            pltpu.VMEM((2, TILE, model), BF),
            pltpu.VMEM((2, TILE, model), BF),
            pltpu.VMEM((2, TILE, model), BF),
            pltpu.VMEM((2, TILE, model), F32),
            pltpu.VMEM((4, 8, model), F32),
            pltpu.VMEM((8, width), F32),
            pltpu.VMEM((4, 8, model), F32),
            pltpu.VMEM((8, 8, model), F32),
            pltpu.VMEM(w_qkv.shape, BF),
            pltpu.VMEM(w_out.shape, BF),
            pltpu.VMEM(w_up.shape, BF),
            pltpu.VMEM(w_down.shape, BF),
            pltpu.SemaphoreType.DMA((2 + 2 * rows_own // PIECE,)),
            pltpu.SemaphoreType.DMA((2 + 2 * rows_own // PIECE + 2 * model // TILE,)),
            pltpu.SemaphoreType.DMA((2 + 2 * rows_own // PIECE + 2 * model // TILE,)),
            pltpu.SemaphoreType.DMA((4,)),
            pltpu.SemaphoreType.DMA((BOXES_X + BOXES_Z, 7)),
            pltpu.SemaphoreType.DMA((BOXES_X + BOXES_Z, 7)),
            pltpu.SemaphoreType.DMA((2, 6)),
            pltpu.SemaphoreType.DMA((2, 6)),
            pltpu.SemaphoreType.DMA((10,)),
            pltpu.SemaphoreType.DMA((10,)),
            pltpu.SemaphoreType.DMA((2,)),
            pltpu.SemaphoreType.DMA((2,)),
            pltpu.SemaphoreType.DMA((2,)),
            pltpu.SemaphoreType.DMA((2, 2)),
            pltpu.SemaphoreType.REGULAR,
            pltpu.SemaphoreType.REGULAR,
        ],
        compiler_params=pltpu.CompilerParams(
            collective_id=0, has_side_effects=True, vmem_limit_bytes=62 * 2**20
        ),
    )(lengths, tokens, cotangent, *norms, w_qkv, w_out, w_up, w_down, feature_scale, feature_weight, *consts)
    if not reduce_dp:
        grads, g_qkv, small, feats = lax.psum(
            (*lax.optimization_barrier((grads.astype(F32), g_qkv.astype(F32))), small, feats), "dp"
        )
    steps = 4
    down_cut, out_cut, up_cut, row_cut, own_cut = (
        size // steps for size in (hidden, width, model, model, rows_own)
    )
    rows_spec = pl.BlockSpec((own_cut, model), lambda i: (i, 0))
    row_spec = pl.BlockSpec((1, model), lambda i: (0, 0))
    feat_spec = pl.BlockSpec((heads, HEAD_DIM), lambda i: (0, 0))
    g_down, g_out, g_up, g_qkv, *norm_sums, g_scale, g_weight, mixed_out, input_grad = pl.pallas_call(
        widen,
        grid=(steps,),
        out_shape=(
            shape((hidden, model), F32),
            shape((width, model), F32),
            shape((model, hidden), F32),
            shape((3, model, width), F32),
            *[shape((1, model), F32)] * 4,
            *[shape((heads, HEAD_DIM), F32)] * 2,
            *[shape((rows_own, model), BF)] * 2,
        ),
        in_specs=[
            pl.BlockSpec((model, down_cut), lambda i: (0, i)),
            pl.BlockSpec((out_cut, model), lambda i: (hidden // out_cut + i, 0)),
            pl.BlockSpec((up_cut, hidden), lambda i: ((hidden + width) // up_cut + i, 0)),
            pl.BlockSpec((3, row_cut, width), lambda i: (0, i, 0)),
            pl.BlockSpec((8, model), lambda i: (0, 0)),
            pl.BlockSpec((2, heads, HEAD_DIM), lambda i: (0, 0, 0)),
            rows_spec,
            rows_spec,
        ],
        out_specs=(
            pl.BlockSpec((down_cut, model), lambda i: (i, 0)),
            pl.BlockSpec((out_cut, model), lambda i: (i, 0)),
            pl.BlockSpec((up_cut, hidden), lambda i: (i, 0)),
            pl.BlockSpec((3, row_cut, width), lambda i: (0, i, 0)),
            *[row_spec] * 4,
            *[feat_spec] * 2,
            *[rows_spec] * 2,
        ),
        compiler_params=pltpu.CompilerParams(vmem_limit_bytes=60 * 2**20),
    )(grads, grads, grads, g_qkv, small, feats, mixed_out, input_grad)
    return (
        mixed_out,
        input_grad,
        *[value.reshape(model) for value in norm_sums],
        g_qkv,
        g_out,
        g_up,
        g_down,
        g_scale,
        g_weight,
    )


def solution(mesh):
    placed = (
        P(("dp", "tensor"), None),
        P(),
        P(),
        P(),
        P(),
        P(None, None, "tensor"),
        P("tensor", None),
        P(None, "tensor"),
        P("tensor", None),
        P("tensor", None),
        P("tensor", None),
        P("dp", None),
        P(("dp", "tensor"), None),
    )
    return jax.shard_map(
        functools.partial(shards, mesh.shape["dp"] == 8),
        mesh=mesh,
        in_specs=placed,
        out_specs=(
            P(("dp", "tensor"), None),
            P(("dp", "tensor"), None),
            P(),
            P(),
            P(),
            P(),
            P(None, None, "tensor"),
            P("tensor", None),
            P(None, "tensor"),
            P("tensor", None),
            P("tensor", None),
            P("tensor", None),
        ),
        check_vma=False,
    )
```
